32 devices in a mesh: role: 2 (over x), batch: 16 (over z, y, core).
Axes of the slice: x: 2, y: 2, z: 4, core: 2. Of those that a mesh axis runs over, the one named last changes fastest.
Arguments:
- frames: float32 [2, 3584, 4, 7056], P('role', 'batch'), may hold values from 0 to 1
- conv1_weight: bfloat16 [2, 256, 32], P('role'), may hold values from -0.375 to 0.375
- conv1_bias: float32 [2, 32], P('role'), may hold values from -1.5 to 1.5
- conv2_weight: bfloat16 [2, 512, 64], P('role'), may hold values from -0.25 to 0.25
- conv2_bias: float32 [2, 64], P('role'), may hold values from -1.5 to 1.5
- conv3_weight: bfloat16 [2, 576, 64], P('role'), may hold values from -0.25 to 0.25
- conv3_bias: float32 [2, 64], P('role'), may hold values from -1.5 to 1.5
- dense_weight: bfloat16 [2, 3136, 512], P('role'), may hold values from -0.109375 to 0.109375
- dense_bias: float32 [2, 512], P('role'), may hold values from -1.5 to 1.5
- head_weight: bfloat16 [2, 512, 918], P('role'), may hold values from -0.5 to 0.5
- head_bias: float32 [2, 918], P('role'), may hold values from -2.5 to 2.5
- taken_actions: int32 [3584], P('batch'), may hold values from 0 to 17
- next_actions: int32 [3584], P('batch'), may hold values from 0 to 17
- rewards: float32 [3584], P('batch'), may hold values from -12 to 12
- discounts: float32 [3584], P('batch'), may hold values from 0 to 0.99
- importance: float32 [3584], P('batch'), may hold values from 0.1 to 3, as said below
- buffer_slots: int32 [3584], P('batch'), may hold values from 0 to 3583, each once
Outputs:
- frame_grad: float32 [3584, 4, 7056], P('batch', 'role')
- conv1_weight_grad: float32 [256, 32], replicated
- conv1_bias_grad: float32 [32], replicated
- conv2_weight_grad: float32 [512, 64], replicated
- conv2_bias_grad: float32 [64], replicated
- conv3_weight_grad: float32 [576, 64], replicated
- conv3_bias_grad: float32 [64], replicated
- dense_weight_grad: float32 [3136, 512], replicated
- dense_bias_grad: float32 [512], replicated
- head_weight_grad: float32 [512, 918], replicated
- head_bias_grad: float32 [918], replicated
- priorities: float32 [3584], P(('role', 'batch'))
The draws below stay inside these ranges and needn't reach their ends.
Inputs may be any that keep to these rules, and one draw needn't show every extreme that they name: importance weights are positive.
All inputs are finite; a program needn't handle non-finite values.
Results may differ from the reference program's by a relative error of at most 0.0085.
Values may be sent and summed in bfloat16 or wider, within the bound.
A program may use at most 192 MiB of HBM per device.

```python
import jax
import jax.numpy as jnp
from jax import lax

STACK = 4
SIDE = 84
CH1 = 32
CH2 = 64
CH3 = 64
UNITS = 512
ACTIONS = 18
ATOMS = 51
TRANS = 3584
PIX = 7056
FLAT = 3136
LOGITS = 918


def draw_importance(key, part):
    key = jax.random.fold_in(key, 11)
    place = jnp.arange(TRANS).astype(jnp.float32) / max(TRANS - 1, 1)
    base = jnp.exp(jax.random.uniform(key, (TRANS,), jnp.float32, -2.302585, 0.0))
    ramp = 1.0 + 2.0 * place
    return jnp.clip(base * ramp, 0.1, 3.0)


def set_ends(array, own_key, low, largest):
    spot = [jax.random.randint(jax.random.fold_in(own_key, axis), (), 0, length) for axis, length in enumerate(array.shape)]
    longest = array.shape.index(max(array.shape))
    next_to = spot[:longest] + [(spot[longest] + 1) % array.shape[longest]] + spot[longest + 1:]
    return array.at[tuple(spot)].set(low).at[tuple(next_to)].set(largest)


def block_levels(own_key, extent, cuts, smallest, high):
    def one(axis_at, shards_of):
        steps = jax.random.uniform(jax.random.fold_in(jax.random.fold_in(own_key, 6), axis_at), (shards_of,), jnp.float32, smallest / len(cuts), high / len(cuts))
        return jnp.repeat(jnp.exp(steps), extent[axis_at] // shards_of).reshape((-1,) + (1,) * (len(extent) - axis_at - 1))

    gain = one(*cuts[0])
    for cut in cuts[1:]:
        gain = gain * one(*cut)
    return gain


def scatter_about(rng, extent, width, most, shards=(), held_as=jnp.bfloat16):
    result = width * jax.random.normal(rng, extent, jnp.float32)
    if shards:
        result = result * block_levels(rng, extent, shards, -0.22, 0.18)
    return jnp.clip(result, -most, most).astype(held_as)


def setup_inputs(seed: int = 0) -> dict:
    streams_of = jax.random.split(jax.random.key(seed), 18)
    frames = jnp.clip(1.0 * jax.random.uniform(streams_of[0], (2, TRANS, STACK, PIX), jnp.float32) ** block_levels(streams_of[0], (2, TRANS, STACK, PIX), ((0, 2), (1, 16)), -0.2, 0.2), 0.0, 1.0)
    conv1_weight = scatter_about(streams_of[1], (2, 64 * STACK, CH1), (64 * STACK) ** -0.5, 0.375, ((0, 2),))
    conv1_bias = scatter_about(streams_of[2], (2, CH1), 0.3, 1.5, ((0, 2),), jnp.float32)
    conv2_weight = scatter_about(streams_of[3], (2, 16 * CH1, CH2), (16 * CH1) ** -0.5, 0.25, ((0, 2),))
    conv2_bias = scatter_about(streams_of[4], (2, CH2), 0.3, 1.5, ((0, 2),), jnp.float32)
    conv3_weight = scatter_about(streams_of[5], (2, 9 * CH2, CH3), (9 * CH2) ** -0.5, 0.25, ((0, 2),))
    conv3_bias = scatter_about(streams_of[6], (2, CH3), 0.3, 1.5, ((0, 2),), jnp.float32)
    dense_weight = scatter_about(streams_of[7], (2, FLAT, UNITS), FLAT ** -0.5, 0.109375, ((0, 2),))
    dense_bias = scatter_about(streams_of[8], (2, UNITS), 0.3, 1.5, ((0, 2),), jnp.float32)
    head_weight = scatter_about(streams_of[9], (2, UNITS, LOGITS), (UNITS // 4) ** -0.5, 0.5, ((0, 2),))
    head_bias = scatter_about(streams_of[10], (2, LOGITS), 0.5, 2.5, ((0, 2),), jnp.float32)
    taken_actions = set_ends(jax.random.randint(streams_of[11], (TRANS,), 0, ACTIONS), jax.random.fold_in(streams_of[11], 1), 0, ACTIONS - 1).astype(jnp.int32)
    next_actions = set_ends(jax.random.randint(streams_of[12], (TRANS,), 0, ACTIONS), jax.random.fold_in(streams_of[12], 1), 0, ACTIONS - 1).astype(jnp.int32)
    rewards = scatter_about(streams_of[13], (TRANS,), 3.0, 12.0, ((0, 16),), jnp.float32)
    discounts = jnp.clip(0.99 * jax.random.uniform(streams_of[14], (TRANS,), jnp.float32) ** block_levels(streams_of[14], (TRANS,), ((0, 16),), -0.2, 0.2), 0.0, 0.99)
    importance = draw_importance(jax.random.fold_in(streams_of[17], 71), 0)
    buffer_slots = jax.random.permutation(streams_of[16], TRANS).astype(jnp.int32)
    return dict(frames=frames, conv1_weight=conv1_weight, conv1_bias=conv1_bias, conv2_weight=conv2_weight, conv2_bias=conv2_bias, conv3_weight=conv3_weight, conv3_bias=conv3_bias, dense_weight=dense_weight, dense_bias=dense_bias, head_weight=head_weight, head_bias=head_bias, taken_actions=taken_actions, next_actions=next_actions, rewards=rewards, discounts=discounts, importance=importance, buffer_slots=buffer_slots)


@jax.custom_vjp
def low(v):
    return lax.optimization_barrier(v.astype(jnp.bfloat16)).astype(jnp.float32)

@jax.custom_vjp
def low_back(v):
    return v

def low_keep(v):
    return (low(v), None)

def low_pass(kept, grad):
    return (grad,)

def back_keep(v):
    return (v, None)

def back_low(kept, grad):
    return (low(grad),)
low.defvjp(low_keep, low_pass)
low_back.defvjp(back_keep, back_low)

def convolve(inputs, kernel, size, stride):
    channels = kernel.shape[0] // (size * size)
    shaped = kernel.reshape(channels, size, size, kernel.shape[1])
    return lax.conv_general_dilated(inputs, shaped, (stride, stride), 'VALID', dimension_numbers=('NCHW', 'IHWO', 'NCHW'), precision=lax.Precision.HIGHEST)

def network(observed, weights):
    kernel_one, bias_one, kernel_two, bias_two, kernel_three, bias_three, dense_w, dense_b, head_w, head_b = weights
    count = observed.shape[0]
    pixels = low(observed).reshape(count, STACK, SIDE, SIDE)
    pre_one = low_back(convolve(pixels, kernel_one, 8, 4) + bias_one[None, :, None, None])
    act_one = low(jax.nn.silu(pre_one))
    pre_two = low_back(convolve(act_one, kernel_two, 4, 2) + bias_two[None, :, None, None])
    act_two = low(jax.nn.silu(pre_two))
    pre_three = low_back(convolve(act_two, kernel_three, 3, 1) + bias_three[None, :, None, None])
    act_three = low(jax.nn.silu(pre_three)).reshape(count, FLAT)
    pre_four = low_back(jnp.dot(act_three, dense_w, precision=lax.Precision.HIGHEST, preferred_element_type=jnp.float32) + dense_b)
    act_four = low(jax.nn.silu(pre_four))
    logits = low_back(jnp.dot(act_four, head_w, precision=lax.Precision.HIGHEST, preferred_element_type=jnp.float32) + head_b)
    return logits.reshape(count, ACTIONS, ATOMS)

def project_target(next_probs, rewards, discounts):
    support = -10.0 + 20.0 / (ATOMS - 1) * jnp.arange(ATOMS).astype(jnp.float32)
    moved = jnp.clip(rewards[:, None] + discounts[:, None] * support[None, :], -10.0, 10.0)
    place = (moved + 10.0) * ((ATOMS - 1) / 20.0)
    nodes = jnp.arange(ATOMS).astype(jnp.float32)
    spread = jnp.maximum(0.0, 1.0 - jnp.abs(place[:, :, None] - nodes[None, None, :]))
    return lax.optimization_barrier(jnp.sum(next_probs[:, :, None] * spread, axis=1))

def reference(frames, conv1_weight, conv1_bias, conv2_weight, conv2_bias, conv3_weight, conv3_bias, dense_weight, dense_bias, head_weight, head_bias, taken_actions, next_actions, rewards, discounts, importance, buffer_slots):
    stacked = (conv1_weight, conv1_bias, conv2_weight, conv2_bias, conv3_weight, conv3_bias, dense_weight, dense_bias, head_weight, head_bias)
    online = tuple((item[0].astype(jnp.float32) for item in stacked))
    target_net = tuple((item[1].astype(jnp.float32) for item in stacked))
    next_logits = network(frames[1], target_net)
    next_pick = jnp.take_along_axis(next_logits, next_actions.astype(jnp.int32)[:, None, None], axis=1)[:, 0, :]
    next_probs = jax.nn.softmax(next_pick, axis=1)
    projected = project_target(next_probs, rewards, discounts)
    total = jnp.sum(importance)

    def loss_fn(states, weights):
        logits = network(states, weights)
        chosen = jnp.take_along_axis(logits, taken_actions.astype(jnp.int32)[:, None, None], axis=1)[:, 0, :]
        log_probs = jax.nn.log_softmax(chosen, axis=1)
        row_loss = -lax.optimization_barrier(jnp.sum(projected * log_probs, axis=1))
        return (jnp.sum(importance * row_loss) / total, row_loss)
    loss, pullback, row_loss = jax.vjp(loss_fn, frames[0], online, has_aux=True)
    state_grad, grads = pullback(jnp.ones((), loss.dtype))
    priorities = jnp.zeros((TRANS,), row_loss.dtype).at[buffer_slots.astype(jnp.int32)].set(row_loss)
    return (state_grad, grads[0], grads[1], grads[2], grads[3], grads[4], grads[5], grads[6], grads[7], grads[8], grads[9], priorities)
```

```python
import functools

import jax
import jax.numpy as jnp
import numpy as np
from jax import lax
from jax.experimental import pallas as pl
from jax.experimental.pallas import tpu as pltpu
from jax.sharding import PartitionSpec as P

STACK = 4
SIDE = 84
ACTIONS = 18
ATOMS = 51
LOGITS = ACTIONS * ATOMS
PIX = SIDE * SIDE
BAND = 4 * SIDE
WIDE = 384
TILES = 56
SUB = 32
F32 = jnp.float32
BF16 = jnp.bfloat16
HIGHEST = lax.Precision.HIGHEST
MESH = pl.DeviceIdType.MESH

NN = (((1,), (0,)), ((), ()))
NT = (((1,), (1,)), ((), ()))
TN = (((0,), (0,)), ((), ()))

ROW_HEAD = 3136
ROW_TWO = ROW_HEAD + 928
ROW_THREE = ROW_TWO + 64
ROW_THREE_REST = ROW_THREE + 64
ROW_ONE = ROW_THREE_REST + 64
ROW_BIAS = ROW_ONE + 32
ROW_LOSS = ROW_BIAS + 16


def dot(left, right, dims=NN, precision=None):
    return lax.dot_general(left, right, dims, precision=precision, preferred_element_type=F32)


def iota(shape, dim):
    return lax.broadcasted_iota(jnp.int32, shape, dim)


def onehot(condition, dtype):
    return jnp.where(condition, 1.0, 0.0).astype(dtype)


def silu_and_slope(pre):
    gate = 0.5 * jnp.tanh(0.5 * pre) + 0.5
    act = pre * gate
    return act.astype(BF16), gate + act * (1.0 - gate)


def tall(value):
    return value.reshape(value.shape[0] * value.shape[1], value.shape[2])


class Plan:
    def __init__(self, batch, slots):
        self.batch = batch
        self.bits = batch.bit_length() - 1
        if 1 << self.bits != batch:
            raise ValueError("batch axis")
        self.loss_rows = -(-slots // (512 * 16)) * 16
        unit = 16 * batch
        units = -(-(ROW_LOSS + self.loss_rows) // unit)
        self.rows = units * unit
        count = min(4, units)
        up = list(range(self.bits))
        round_way = up[:1] + up[2:] + up[1:2]
        self.streams, at = [], 0
        for s in range(count):
            size = (units // count + (1 if s < units % count else 0)) * unit
            self.streams.append((at, size, up if s % 2 == 0 else round_way))
            at += size


def banded_first(kernel_t, channel, line, column, real, channels, lanes):
    rows = channel.shape[0]
    spread = onehot((iota((lanes, 32), 0) & 31) == iota((lanes, 32), 1), BF16)
    tiled = dot(spread, kernel_t).astype(BF16)
    block, rest = column >> 2, column & 3
    lane_x = iota((rows, lanes), 1) >> 5
    found = []
    for half in range(2):
        parts = []
        for step in range(2):
            goal = jnp.where(real, channel * 64 + (4 * half + line) * 8 + 4 * step + rest, -1)
            pick = onehot(iota((rows, channels * 64), 1) == goal, BF16)
            parts.append(dot(pick, tiled, NT))
        found.append(jnp.where(lane_x == block, parts[0], jnp.where(lane_x == block - 1, parts[1], 0.0)).astype(BF16))
    return found


def build_first(kernel_t, out):
    row = iota((512, 1), 0)
    found = banded_first(kernel_t, row >> 7, (row >> 5) & 3, row & 31, row >= 0, STACK, 224)
    for half in range(2):
        out[half] = found[half]


def build_frame(kernel_t, out):
    row = iota((2 * WIDE, 1), 0)
    channel = (row >= WIDE).astype(jnp.int32)
    inner = row - channel * WIDE
    line = sum((inner >= SIDE * i).astype(jnp.int32) for i in range(1, 5))
    found = banded_first(kernel_t, channel, line, inner - line * SIDE, line < 4, 2, 640)
    for half in range(2):
        out[half] = found[half]


def build_second(kernel_t, out):
    goal = (iota((512, 512), 0) & 31) * 16 + (iota((512, 512), 0) >> 5)
    by_place = dot(onehot(iota((512, 512), 1) == goal, BF16), kernel_t, NT).astype(BF16)
    out[...] = jnp.zeros_like(out)
    for ky in range(4):
        for kx in range(4):
            piece = by_place[(ky * 4 + kx) * 32 : (ky * 4 + kx + 1) * 32]
            for x in range(3):
                low = 256 * ky + (2 * x + kx) * 32
                out[low : low + 32, 64 * x : 64 * x + 64] = piece


def build_third(kernel_t, tall_out, wide_out):
    goal = (iota((576, 576), 0) & 63) * 9 + (iota((576, 576), 0) >> 6)
    by_place = dot(onehot(iota((576, 576), 1) == goal, BF16), kernel_t, NT).astype(BF16)
    tall_out[...] = jnp.zeros_like(tall_out)
    wide_out[...] = jnp.zeros_like(wide_out)
    for ky in range(3):
        for kx in range(3):
            piece = by_place[(ky * 3 + kx) * 64 : (ky * 3 + kx + 1) * 64]
            for x in range(2):
                low = (x + kx) * 64
                tall_out[256 * ky + low : 256 * ky + low + 64, 64 * x : 64 * x + 64] = piece
                wide_out[low : low + 64, 128 * ky + 64 * x : 128 * ky + 64 * x + 64] = piece


def build_picks(out):
    lane = iota((1, WIDE), 1)
    group, line, column = lane >> 7, (lane >> 5) & 3, lane & 31
    goal = jnp.where(28 * group + column < SIDE, SIDE * line + 28 * group + column, -1000)
    row = iota((512, WIDE), 0)
    for kind in range(8):
        out[512 * kind : 512 * kind + 512, :WIDE] = onehot(row == goal + (BAND * kind) % 128, BF16)


def core_kernel(plan, steps, *refs):
    (x_hbm, edge, k1_ref, k2_ref, k3_ref, w4_hbm, b1_ref, b2_ref, b3_ref, b4, w5, b5, cols, lane_action, compact) = refs[:15]
    frame_out, dense_out, sums_out = refs[15:18]
    (
        raw, lines, x, a1, s1, a2, s2, a3, s3, a4, g4, delta_all, g1, pad2, pad3, acc, band_k,
        k1, k2, k3, k3_wide, w4, bias, acc1, acc2, acc3, bias_sums, loss_sums, send, landed, final, probs_all, logp, nexts,
        totals, totals_in, k1_online,
        raw_sem, w4_sem, tile_sem, probs_send, probs_recv, g1_send, g1_recv, tot_send, tot_recv, k1_send, k1_recv,
        rs_send, rs_recv, ag_send, ag_recv, x_send, x_recv, out_sem,
    ) = refs[18:]
    role, place = lax.axis_index("role"), lax.axis_index("batch")
    online = role == 0

    def bit_of(bit):
        return (place // (1 << bit)) % 2

    def across(bit):
        return {"batch": place + (1 - 2 * bit_of(bit)) * (1 << bit)}

    other_role = {"role": 1 - role}

    def remote(src, dst, send_sem, recv_sem, device):
        return pltpu.make_async_remote_copy(
            src_ref=src, dst_ref=dst, send_sem=send_sem, recv_sem=recv_sem, device_id=device, device_id_type=MESH
        )

    def raw_copies(step, slot):
        return [
            pltpu.make_async_copy(
                x_hbm.at[0, pl.ds(step * SUB, SUB), :, pl.ds(128 * t, 128)], raw.at[slot, t], raw_sem.at[slot]
            )
            for t in range(TILES - 1)
        ]

    weight_copy = pltpu.make_async_copy(w4_hbm, send.at[pl.ds(0, 3136)], w4_sem)
    weight_copy.start()
    for c in raw_copies(0, 0):
        c.start()

    barrier = pltpu.get_barrier_semaphore()
    for bit in range(plan.bits):
        pl.semaphore_signal(barrier, inc=1, device_id=across(bit), device_id_type=MESH)
    pl.semaphore_signal(barrier, inc=1, device_id=other_role, device_id_type=MESH)
    pl.semaphore_wait(barrier, plan.bits + 1)

    kernel_copy = remote(k1_ref, k1_online, k1_send, k1_recv, other_role)

    @pl.when(online)
    def _():
        kernel_copy.start()

    totals[0] = jnp.broadcast_to(jnp.sum(cols[:, 2:3], axis=0, keepdims=True), (8, 128))

    def total_copy(stage):
        return remote(totals.at[stage], totals_in.at[stage], tot_send.at[stage], tot_recv.at[stage], across(stage))

    def total_step(stage):
        if stage > 0:
            total_copy(stage - 1).wait_recv()
            totals[stage] = totals[stage - 1] + totals_in[stage - 1]
        if stage < plan.bits:
            total_copy(stage).start()

    todo = list(range(plan.bits + 1))
    total_step(todo.pop(0))
    build_first(k1_ref[...], k1)
    total_step(todo.pop(0))
    build_second(k2_ref[...], k2)
    if len(todo) > 1:
        total_step(todo.pop(0))
    build_third(k3_ref[...], k3, k3_wide)
    if len(todo) > 1:
        total_step(todo.pop(0))
    bias[...] = jnp.zeros_like(bias)
    for at, (ref, size, copies) in enumerate(((b1_ref, 32, 20), (b2_ref, 64, 9), (b3_ref, 64, 7))):
        repeat = onehot((iota((size, size * copies), 1) & (size - 1)) == iota((size, size * copies), 0), F32)
        bias[at : at + 1, : size * copies] = dot(ref[...], repeat, precision=HIGHEST)
    acc1[...] = jnp.zeros_like(acc1)
    acc2[...] = jnp.zeros_like(acc2)
    acc3[...] = jnp.zeros_like(acc3)
    bias_sums[...] = jnp.zeros_like(bias_sums)
    loss_sums[...] = jnp.zeros_like(loss_sums)
    pad3[...] = jnp.zeros_like(pad3)
    pad2[...] = jnp.zeros_like(pad2)
    a2[...] = jnp.zeros_like(a2)
    for step in range(steps):
        g1[step, 0] = jnp.zeros((SUB, 640), BF16)
        g1[step, 21] = jnp.zeros((SUB, 640), BF16)
    weight_copy.wait()
    spare = raw.reshape(2, (TILES - 1) * SUB * STACK, 128)
    for pair in range(2):
        for q in range(2):
            low = 128 * (2 * pair + q)
            spare[1, 3136 * q : 3136 * q + 3136] = send[:3136, low : low + 128].astype(F32)
        for spot in range(49):
            for q in range(2):
                low = 128 * (2 * pair + q)
                w4[64 * spot : 64 * spot + 64, low : low + 128] = spare[
                    1, pl.ds(3136 * q + spot, 64, stride=49), :
                ].astype(BF16)
    build_picks(send)
    while todo:
        total_step(todo.pop(0))
    for stage in range(plan.bits):
        total_copy(stage).wait_send()

    raw_flat = raw.reshape(2, TILES - 1, SUB * STACK, 128)

    def forward(step, slot):
        rows = pl.ds(pl.multiple_of(step * SUB, SUB), SUB)
        own = cols[rows, :]
        for kind in range(8):
            bands = list(range(kind, 21, 8))
            for at, band in enumerate(bands):
                low = BAND * band // 128
                for c in range(STACK):
                    place_at = (at * STACK + c) * SUB
                    for t in range(4):
                        if low + t < TILES - 1:
                            piece = raw_flat[slot, low + t, pl.ds(c, SUB, stride=STACK), :]
                        else:
                            piece = edge[pl.ds(step * (SUB * STACK) + c, SUB, stride=STACK), :]
                        lines[place_at : place_at + SUB, 128 * t : 128 * t + 128] = piece.astype(BF16)
            count = len(bands) * STACK * SUB
            sorted_lines = dot(lines[:count], send[512 * kind : 512 * kind + 512, :WIDE]).astype(BF16)
            for at, band in enumerate(bands):
                for c in range(STACK):
                    place_at = (at * STACK + c) * SUB
                    for group in range(3):
                        x[band, :, 512 * group + 128 * c : 512 * group + 128 * c + 128] = sorted_lines[
                            place_at : place_at + SUB, 128 * group : 128 * group + 128
                        ]
        for group, lanes in enumerate((224, 224, 192)):
            part = tall(x[:, :, 512 * group : 512 * group + 512])
            acc[: 20 * SUB, 224 * group : 224 * group + lanes] = dot(part[: 20 * SUB], k1[0, :, :lanes]) + dot(
                part[SUB:], k1[1, :, :lanes]
            )
        for y in range(20):
            act, slope = silu_and_slope(acc[y * SUB : (y + 1) * SUB, :640] + bias[0:1, :640])
            a1[y % 2, y // 2] = act
            s1[y % 2, y // 2] = slope
        for group in range(3):
            even, odd = (tall(a1[p, :, :, 192 * group : 192 * group + 256]) for p in range(2))
            joined = jnp.concatenate([even[: 9 * SUB], odd[: 9 * SUB], even[SUB:], odd[SUB:]], axis=1)
            acc[: 9 * SUB, 192 * group : 192 * group + 192] = dot(joined, k2[...])
        for y in range(9):
            act, slope = silu_and_slope(acc[y * SUB : (y + 1) * SUB, :576] + bias[1:2, :576])
            a2[y, :, :576] = act
            s2[y] = slope
        for pair in range(4):
            low = 128 * pair
            joined = jnp.concatenate([tall(a2[ky : ky + 7, :, low : low + 256]) for ky in range(3)], axis=1)
            acc[: 7 * SUB, low : low + 128] = dot(joined, k3[...])
        pre4 = b4[...]
        for y in range(7):
            act, slope = silu_and_slope(acc[y * SUB : (y + 1) * SUB, :448] + bias[2:3, :448])
            a3[y, rows, :] = act
            s3[y] = slope
            pre4 = pre4 + dot(act, w4[448 * y : 448 * y + 448])
        act, slope4 = silu_and_slope(pre4)
        a4[rows, :] = act
        logits = dot(act, w5[...], NT) + b5[...]
        picked = jnp.where(lane_action[...] == own[:, 3:4], logits, 0.0)
        high = picked.astype(BF16)
        rest = picked - high.astype(F32)
        middle = rest.astype(BF16)
        low_part = (rest - middle.astype(F32)).astype(BF16)
        thrice = dot(jnp.concatenate([high, middle, low_part], axis=0), compact[...], NT)
        chosen = thrice[:SUB] + thrice[SUB : 2 * SUB] + thrice[2 * SUB :]
        real = iota((SUB, 128), 1) < ATOMS
        shifted = chosen - jnp.max(jnp.where(real, chosen, -jnp.inf), axis=1, keepdims=True)
        exps = jnp.where(real, jnp.exp(shifted), 0.0)
        sums = jnp.sum(exps, axis=1, keepdims=True)
        probs_all[step] = exps / sums
        logp[...] = jnp.where(real, shifted - jnp.log(sums), 0.0)
        return slope4

    def probs_copy(step):
        return remote(probs_all.at[step], nexts.at[step], probs_send.at[step], probs_recv.at[step], other_role)

    def grad_copy(step):
        return remote(g1.at[step, pl.ds(1, 20)], g1.at[step, pl.ds(1, 20)], g1_send.at[step], g1_recv.at[step], other_role)

    def backward(step, slope4):
        rows = pl.ds(pl.multiple_of(step * SUB, SUB), SUB)
        own = cols[rows, :]
        nodes = iota((SUB, 128), 1).astype(F32)
        reward, discount, importance = own[:, 0:1], own[:, 1:2], own[:, 2:3]
        support = -10.0 + 20.0 / (ATOMS - 1) * nodes
        spot = (jnp.clip(reward + discount * support, -10.0, 10.0) + 10.0) * ((ATOMS - 1) / 20.0)
        next_probs = nexts[step]
        projected = jnp.zeros((SUB, 128), F32)
        for j in range(ATOMS):
            projected += next_probs[:, j : j + 1] * jnp.maximum(0.0, 1.0 - jnp.abs(spot[:, j : j + 1] - nodes))
        projected = jnp.where(nodes < ATOMS, projected, 0.0)
        mass = jnp.sum(projected, axis=1, keepdims=True)
        row_loss = -jnp.sum(projected * logp[...], axis=1, keepdims=True)
        high = (row_loss * onehot(own[:, 5:6] == iota((SUB, plan.loss_rows), 1).astype(F32), F32)).astype(BF16)
        low = onehot(own[:, 6:7] == iota((SUB, 512), 1).astype(F32), BF16)
        loss_sums[...] += dot(high, low, TN)
        scaled = importance / totals[plan.bits, 0:1, 0:1]
        delta = (scaled * (probs_all[step] * mass - projected)).astype(BF16)
        spread = dot(delta, compact[...])
        delta_full = jnp.where(lane_action[...] == own[:, 4:5], spread, 0.0).astype(BF16)
        delta_all[rows, :] = delta_full
        grad4 = (dot(delta_full, w5[...]) * slope4).astype(BF16)
        g4[rows, :] = grad4
        for y in range(7):
            pad3[y + 2, :, :448] = (dot(grad4, w4[448 * y : 448 * y + 448], NT) * s3[y]).astype(BF16)
        for pair in range(4):
            low = 128 * pair
            joined = jnp.concatenate([tall(pad3[2 - ky : 11 - ky, :, low : low + 128]) for ky in range(3)], axis=1)
            total = dot(joined, k3_wide[...], NT)
            if pair == 0:
                acc[: 9 * SUB, :256] = total
            else:
                acc[: 9 * SUB, low : low + 128] += total[:, :128]
                acc[: 9 * SUB, low + 128 : low + 256] = total[:, 128:]
        for y in range(9):
            pad2[y + 1] = (acc[y * SUB : (y + 1) * SUB, :576] * s2[y]).astype(BF16)
        for parity in range(2):
            for group in range(3):
                low = 192 * group
                part = tall(pad2[:, :, low : low + 192])
                total = dot(part[SUB:], k2[256 * parity : 256 * parity + 256], NT) + dot(
                    part[: 10 * SUB], k2[256 * parity + 512 : 256 * parity + 768], NT
                )
                if group == 0:
                    acc[: 10 * SUB, :256] = total
                else:
                    acc[: 10 * SUB, low : low + 64] += total[:, :64]
                    acc[: 10 * SUB, low + 64 : low + 256] = total[:, 64:]
            for m in range(10):
                g1[step, 2 * m + parity + 1] = (acc[m * SUB : (m + 1) * SUB, :640] * s1[parity, m]).astype(BF16)

    def weight_step(step):
        for half in range(2):
            for group in range(3):
                lanes = 192 if group == 2 else 224
                part = tall(g1[step, 1:21, :, 224 * group : 224 * group + lanes])
                pixels = tall(x[half : half + 20, :, 512 * group : 512 * group + 512])
                acc1[half, :lanes] += dot(part, pixels, TN)
        for ky in range(4):
            total = None
            for group in range(3):
                part = tall(a1[ky % 2, ky // 2 : ky // 2 + 9, :, 192 * group : 192 * group + 256])
                term = dot(part, tall(pad2[1:10, :, 192 * group : 192 * group + 192]), TN)
                total = term if total is None else total + term
            acc2[ky] += total
        for ky in range(3):
            acc3[ky] += sum(
                dot(tall(a2[ky : ky + 7, :, 128 * pair : 128 * pair + 256]), tall(pad3[2:9, :, 128 * pair : 128 * pair + 128]), TN)
                for pair in range(4)
            )
        for at, (count, lanes) in enumerate(((20, 640), (9, 576), (7, 448))):
            part = jnp.zeros((8, lanes), F32)
            for y in range(count):
                piece = (g1[step, y + 1] if at == 0 else pad2[y + 1] if at == 1 else pad3[y + 2, :, :448]).astype(F32)
                for q in range(SUB // 8):
                    part += piece[8 * q : 8 * q + 8]
            bias_sums[at, :, :lanes] += part

    def one_step(step, _):
        slot = step % 2
        for c in raw_copies(step, slot):
            c.wait()

        @pl.when(step + 1 < steps)
        def _():
            for c in raw_copies(step + 1, 1 - slot):
                c.start()

        slope4 = forward(step, slot)

        @pl.when(role == 1)
        def _():
            probs_copy(step).start()

        @pl.when(online)
        def _():
            probs_copy(step).wait_recv()
            backward(step, slope4)
            @pl.when(step + 1 < steps)
            def _():
                grad_copy(step).start()

            weight_step(step)

        return 0

    lax.fori_loop(0, steps, one_step, 0)

    @pl.when(online)
    def _():
        flat = raw.reshape(2 * (TILES - 1) * SUB * STACK, 128)
        for y in range(7):
            block = dot(a3[y], g4[...], TN)
            for px in range(7):
                for q in range(4):
                    flat[pl.ds(3136 * q + 7 * y + px, 64, stride=49), :] = block[
                        64 * px : 64 * px + 64, 128 * q : 128 * q + 128
                    ]
        for q in range(4):
            send[:3136, 128 * q : 128 * q + 128] = flat[3136 * q : 3136 * q + 3136].astype(BF16)
        send[ROW_HEAD + 912 : ROW_TWO] = jnp.zeros((16, 512), BF16)
        head = dot(delta_all[...], a4[...], TN)
        send[ROW_HEAD : ROW_HEAD + 912] = head[:912].astype(BF16)
        send[ROW_HEAD + 912 : ROW_TWO] = jnp.concatenate([head[912:LOGITS], jnp.zeros((16 + 912 - LOGITS, 512), F32)], axis=0).astype(BF16)
        total = jnp.zeros((32, 256), F32)
        for half in range(2):
            folded = acc1[half, 0:32]
            for px in range(1, 7):
                folded += pltpu.roll(acc1[half, 32 * px : 32 * px + 32], 512 - 4 * px, 1)
            column = iota((512, 256), 1)
            goal = (column >> 6) * 128 + ((column >> 3) & 3) * 32 + (column & 7)
            mine = ((column >> 5) & 1) == half
            pick = onehot(mine & (iota((512, 256), 0) == goal), F32)
            total += dot(folded, pick, precision=HIGHEST)
        send[ROW_ONE:ROW_BIAS] = jnp.concatenate([total, jnp.zeros((32, 256), F32)], axis=1).astype(BF16)
        pieces = []
        for ky in range(4):
            for kx in range(4):
                pieces.append(
                    sum(acc2[ky, (2 * px + kx) * 32 : (2 * px + kx + 1) * 32, 64 * px : 64 * px + 64] for px in range(3))
                )
        pick = onehot(iota((512, 512), 1) == (iota((512, 512), 0) & 31) * 16 + (iota((512, 512), 0) >> 5), F32)
        send[ROW_TWO:ROW_THREE] = dot(jnp.concatenate(pieces, axis=0), pick, TN, HIGHEST).astype(BF16)
        pieces = []
        for ky in range(3):
            for kx in range(3):
                pieces.append(
                    sum(acc3[ky, (px + kx) * 64 : (px + kx + 1) * 64, 64 * px : 64 * px + 64] for px in range(2))
                )
        pick = onehot(iota((576, 576), 1) == (iota((576, 576), 0) & 63) * 9 + (iota((576, 576), 0) >> 6), F32)
        third = dot(jnp.concatenate(pieces, axis=0), pick, TN, HIGHEST)
        send[ROW_THREE:ROW_THREE_REST] = third[:, :512].astype(BF16)
        send[ROW_THREE_REST:ROW_ONE] = jnp.concatenate([third[:, 512:], jnp.zeros((64, 448), F32)], axis=1).astype(BF16)
        bias_rows = []
        for at, (size, copies) in enumerate(((32, 20), (64, 9), (64, 7))):
            fold = onehot((iota((size * copies, 512), 0) & (size - 1)) == iota((size * copies, 512), 1), F32)
            line = jnp.sum(bias_sums[at, :, : size * copies], axis=0, keepdims=True)
            bias_rows.append(dot(line, fold, precision=HIGHEST))
        bias_rows.append(jnp.sum(g4[...].astype(F32), axis=0, keepdims=True))
        head_bias = jnp.sum(delta_all[...].astype(F32), axis=0, keepdims=True)
        bias_rows.append(head_bias[:, :512])
        bias_rows.append(jnp.concatenate([head_bias[:, 512:], jnp.zeros((1, 1024 - LOGITS), F32)], axis=1))
        bias_rows.append(jnp.zeros((10, 512), F32))
        send[ROW_BIAS:ROW_LOSS] = jnp.concatenate(bias_rows, axis=0).astype(BF16)
        send[ROW_LOSS : ROW_LOSS + plan.loss_rows] = loss_sums[...].astype(BF16)
        if plan.rows > ROW_LOSS + plan.loss_rows:
            left = plan.rows - ROW_LOSS - plan.loss_rows
            send[ROW_LOSS + plan.loss_rows :] = jnp.zeros((left, 512), BF16)

    def stage_rows(stream, stage):
        base, size, order = plan.streams[stream]
        low = base
        for bit in order[:stage]:
            size //= 2
            low = low + bit_of(bit) * size
        return low, size

    def aligned(at):
        return pl.multiple_of(at, 16)

    def scatter_copy(stream, stage):
        base, size, order = plan.streams[stream]
        low, count = stage_rows(stream, stage)
        half = count // 2
        away = aligned(low + (1 - bit_of(order[stage])) * half)
        into = base + size - count
        index = stream * plan.bits + stage
        return remote(
            send.at[pl.ds(away, half)], landed.at[pl.ds(into, half)], rs_send.at[index], rs_recv.at[index],
            across(order[stage]),
        )

    def scatter_start(stage):
        for stream in range(len(plan.streams)):
            scatter_copy(stream, stage).start()

    def scatter_finish(stage):
        for stream, (base, size, order) in enumerate(plan.streams):
            scatter_copy(stream, stage).wait_recv()
            low, count = stage_rows(stream, stage)
            half = count // 2
            keep = aligned(low + bit_of(order[stage]) * half)
            into = base + size - count
            target = final if stage == plan.bits - 1 else send
            block = 64 if half % 64 == 0 else 16

            def add(i, _, keep=keep, into=into, target=target, block=block):
                at = aligned(keep + i * block)
                new = landed[pl.ds(aligned(into + i * block), block)].astype(F32)
                target[pl.ds(at, block)] = (send[pl.ds(at, block)].astype(F32) + new).astype(BF16)
                return 0

            lax.fori_loop(0, half // block, add, 0)
            if stage + 1 < plan.bits:
                scatter_copy(stream, stage + 1).start()
            else:
                over_copy(stream).start()
                gather_copy(stream, 0).start()
        if stage == plan.bits - 1:
            grad_copy(steps - 1).start()

    def over_copy(stream):
        low, count = stage_rows(stream, plan.bits)
        spot = pl.ds(aligned(low), count)
        return remote(final.at[spot], final.at[spot], x_send.at[stream], x_recv.at[stream], other_role)

    def gather_copy(stream, stage):
        order = plan.streams[stream][2]
        low, count = stage_rows(stream, plan.bits - stage)
        spot = pl.ds(aligned(low), count)
        index = stream * plan.bits + stage
        return remote(
            final.at[spot], final.at[spot], ag_send.at[index], ag_recv.at[index], across(order[plan.bits - 1 - stage])
        )

    def over_finish():
        for stream in range(len(plan.streams)):
            over_copy(stream).wait_recv()
            gather_copy(stream, 0).start()

    def gather_finish(stage):
        for stream in range(len(plan.streams)):
            gather_copy(stream, stage).wait_recv()
            if stage + 1 < plan.bits:
                gather_copy(stream, stage + 1).start()

    tile_rows = raw.reshape(2 * (TILES - 1) * SUB * STACK, 128)

    tile_pairs = raw.reshape((TILES - 1) * SUB * STACK, 2, 128)

    def tile_copies(step):
        return [
            pltpu.make_async_copy(
                tile_pairs.at[pl.ds(t * SUB, SUB)],
                frame_out.at[pl.ds(step * SUB, SUB), :, pl.ds(128 * t, 128)],
                tile_sem,
            )
            for t in range(TILES)
        ]

    def frame_step(step):
        acc[...] = dot(tall(g1[step, 1:22]), band_k[0], NT) + dot(tall(g1[step, 0:21]), band_k[1], NT)

        @pl.when(step > 0)
        def _():
            for c in tile_copies(step - 1):
                c.wait()

        for c in range(2):
            for t in range(TILES):
                pieces, at, end = [], 128 * t, min(128 * t + 128, PIX)
                while at < end:
                    band, inner = divmod(at, BAND)
                    size = min(end - at, BAND - inner)
                    pieces.append(acc[band * SUB : (band + 1) * SUB, WIDE * c + inner : WIDE * c + inner + size])
                    at += size
                if end < 128 * t + 128:
                    pieces.append(jnp.zeros((SUB, 128 * t + 128 - end), F32))
                tile_rows[pl.ds(t * SUB * 2 + c, SUB, stride=2), :] = (
                    pieces[0] if len(pieces) == 1 else jnp.concatenate(pieces, axis=1)
                )
        for c in tile_copies(step):
            c.start()

    @pl.when(online)
    def _():
        scatter_start(0)
        build_frame(k1_ref[:, 0:128], band_k)
        scatter_finish(0)

    @pl.when(role == 1)
    def _():
        kernel_copy.wait_recv()
        build_frame(k1_online[:, 128:256], band_k)

    def frame_and_more(step, _):
        @pl.when(role == 1)
        def _():
            grad_copy(step).wait_recv()

        frame_step(step)

        for stage in range(1, plan.bits):

            @pl.when(online & (step == min(3 * stage, steps - 1)))
            def _(stage=stage):
                scatter_finish(stage)

        @pl.when((role == 1) & (step == max(steps - 2, 0)))
        def _():
            over_finish()
            for stage in range(plan.bits - 1):
                gather_finish(stage)

        return 0

    lax.fori_loop(0, steps, frame_and_more, 0)

    @pl.when(online)
    def _():
        for stage in range(plan.bits - 1):
            gather_finish(stage)

    gather_finish(plan.bits - 1)
    out_copies = [
        pltpu.make_async_copy(final.at[pl.ds(0, ROW_HEAD)], dense_out, out_sem.at[0]),
        pltpu.make_async_copy(final.at[pl.ds(ROW_HEAD, plan.rows - ROW_HEAD)], sums_out, out_sem.at[1]),
    ]
    for c in out_copies:
        c.start()

    for c in tile_copies(steps - 1):
        c.wait()
    for stream in range(len(plan.streams)):
        for stage in range(plan.bits):
            gather_copy(stream, stage).wait_send()

    @pl.when(online)
    def _():
        kernel_copy.wait_send()
        for stream in range(len(plan.streams)):
            over_copy(stream).wait_send()
            for stage in range(plan.bits):
                scatter_copy(stream, stage).wait_send()

        def sent(step, _):
            grad_copy(step).wait_send()
            return 0

        lax.fori_loop(0, steps, sent, 0)

    @pl.when(role == 1)
    def _():
        def sent(step, _):
            probs_copy(step).wait_send()
            return 0

        lax.fori_loop(0, steps, sent, 0)

    for c in out_copies:
        c.wait()


def core(plan, frames, edge, weights, cols, tables):
    rows = frames.shape[1]
    steps = rows // SUB
    k1, k2, k3, w4, b1, b2, b3, b4, w5, b5 = weights
    vmem, hbm = pl.BlockSpec(memory_space=pltpu.VMEM), pl.BlockSpec(memory_space=pl.ANY)
    dma = pltpu.SemaphoreType.DMA
    streams = len(plan.streams)
    scratch = [
        pltpu.VMEM((2, TILES - 1, SUB, STACK, 128), F32),
        pltpu.VMEM((3 * STACK * SUB, 512), BF16),
        pltpu.VMEM((21, SUB, 1536), BF16),
        pltpu.VMEM((2, 10, SUB, 640), BF16),
        pltpu.VMEM((2, 10, SUB, 640), F32),
        pltpu.VMEM((9, SUB, 640), BF16),
        pltpu.VMEM((9, SUB, 576), F32),
        pltpu.VMEM((7, rows, 448), BF16),
        pltpu.VMEM((7, SUB, 448), F32),
        pltpu.VMEM((rows, 512), BF16),
        pltpu.VMEM((rows, 512), BF16),
        pltpu.VMEM((rows, LOGITS), BF16),
        pltpu.VMEM((steps, 22, SUB, 640), BF16),
        pltpu.VMEM((11, SUB, 576), BF16),
        pltpu.VMEM((11, SUB, 512), BF16),
        pltpu.VMEM((21 * SUB, 2 * WIDE), F32),
        pltpu.VMEM((2, 2 * WIDE, 640), BF16),
        pltpu.VMEM((2, 512, 224), BF16),
        pltpu.VMEM((1024, 192), BF16),
        pltpu.VMEM((768, 128), BF16),
        pltpu.VMEM((256, 384), BF16),
        pltpu.VMEM((3136, 512), BF16),
        pltpu.VMEM((8, 640), F32),
        pltpu.VMEM((2, 224, 512), F32),
        pltpu.VMEM((4, 256, 192), F32),
        pltpu.VMEM((3, 256, 128), F32),
        pltpu.VMEM((3, 8, 640), F32),
        pltpu.VMEM((plan.loss_rows, 512), F32),
        pltpu.VMEM((plan.rows, 512), BF16),
        pltpu.VMEM((plan.rows, 512), BF16),
        pltpu.VMEM((plan.rows, 512), BF16),
        pltpu.VMEM((steps, SUB, 128), F32),
        pltpu.VMEM((SUB, 128), F32),
        pltpu.VMEM((steps, SUB, 128), F32),
        pltpu.VMEM((plan.bits + 1, 8, 128), F32),
        pltpu.VMEM((plan.bits, 8, 128), F32),
        pltpu.VMEM((32, 256), BF16),
        dma((2,)), dma, dma, dma((steps,)), dma((steps,)), dma((steps,)), dma((steps,)),
        dma((plan.bits,)), dma((plan.bits,)), dma, dma,
        dma((streams * plan.bits,)), dma((streams * plan.bits,)), dma((streams * plan.bits,)), dma((streams * plan.bits,)),
        dma((streams,)), dma((streams,)), dma((2,)),
    ]
    return pl.pallas_call(
        functools.partial(core_kernel, plan, steps),
        in_specs=[hbm, vmem, vmem, vmem, vmem, hbm] + [vmem] * 9,
        out_specs=[hbm, hbm, hbm],
        out_shape=[
            jax.ShapeDtypeStruct((rows, 2, TILES * 128), F32),
            jax.ShapeDtypeStruct((ROW_HEAD, 512), BF16),
            jax.ShapeDtypeStruct((plan.rows - ROW_HEAD, 512), BF16),
        ],
        scratch_shapes=scratch,
        compiler_params=pltpu.CompilerParams(vmem_limit_bytes=63 << 20, collective_id=0, has_side_effects=True),
        name="core",
    )(frames, edge, k1, k2, k3, w4, b1, b2, b3, b4, w5, b5, cols, *tables)


def finish_kernel(frames, dense, sums, frame_out, w4, k1, b1, k2, b2, k3, b3, b4, w5, b5, losses):
    frame_out[...] = frames[:, :, :PIX]
    w4[...] = dense[...].astype(F32)

    def part(low, high):
        return sums[low - ROW_HEAD : high - ROW_HEAD]

    @pl.when(pl.program_id(0) == 0)
    def _():
        w5[:912] = part(ROW_HEAD, ROW_HEAD + 912).astype(F32)
        w5[912:] = part(ROW_HEAD + 912, ROW_TWO).astype(F32)[: LOGITS - 912]
        k2[...] = part(ROW_TWO, ROW_THREE).astype(F32)
        k3[:, :512] = part(ROW_THREE, ROW_THREE_REST).astype(F32)
        k3[:, 512:] = part(ROW_THREE_REST, ROW_ONE)[:, :64].astype(F32)
        k1[...] = part(ROW_ONE, ROW_BIAS)[:, :256].astype(F32)
        rows = part(ROW_BIAS, ROW_LOSS).astype(F32)
        b1[...] = rows[0:1, :32]
        b2[...] = rows[1:2, :64]
        b3[...] = rows[2:3, :64]
        b4[...] = rows[3:4]
        b5[:, :512] = rows[4:5]
        b5[:, 512:] = rows[5:6, : LOGITS - 512]
        losses[...] = part(ROW_LOSS, ROW_LOSS + losses.shape[0]).astype(F32)


def finish(plan, frames, dense, sums):
    rows = frames.shape[0]
    steps = rows // SUB
    small = ((32, 256), (1, 32), (64, 512), (1, 64), (64, 576), (1, 64), (1, 512), (LOGITS, 512), (1, LOGITS), (plan.loss_rows, 512))
    fixed = [pl.BlockSpec(s, lambda i: (0, 0)) for s in small]
    return pl.pallas_call(
        finish_kernel,
        grid=(steps,),
        in_specs=[
            pl.BlockSpec((SUB, 2, TILES * 128), lambda i: (i, 0, 0)),
            pl.BlockSpec((ROW_HEAD // 7, 512), lambda i: (jnp.minimum(i, 6), 0)),
            pl.BlockSpec(sums.shape, lambda i: (0, 0)),
        ],
        out_specs=[
            pl.BlockSpec((SUB, 2, PIX), lambda i: (i, 0, 0)),
            pl.BlockSpec((ROW_HEAD // 7, 512), lambda i: (jnp.minimum(i, 6), 0)),
            *fixed,
        ],
        out_shape=[jax.ShapeDtypeStruct(s, F32) for s in ((rows, 2, PIX), (ROW_HEAD, 512), *small)],
        compiler_params=pltpu.CompilerParams(vmem_limit_bytes=48 << 20),
        name="finish",
    )(frames, dense, sums)


def on_device(
    frames,
    conv1_weight,
    conv1_bias,
    conv2_weight,
    conv2_bias,
    conv3_weight,
    conv3_bias,
    dense_weight,
    dense_bias,
    head_weight,
    head_bias,
    taken_actions,
    next_actions,
    rewards,
    discounts,
    importance,
    buffer_slots,
):
    role, place = lax.axis_index("role"), lax.axis_index("batch")
    roles, batch = lax.axis_size("role"), lax.axis_size("batch")
    rows = frames.shape[1]
    slots = rows * batch
    plan = Plan(batch, slots)

    lane_action = jnp.asarray(np.arange(LOGITS)[None] // ATOMS, F32)
    compact = jnp.asarray(np.arange(128)[:, None] == np.arange(LOGITS)[None] % ATOMS, BF16)
    selected = jnp.where(role == 0, taken_actions, next_actions)
    columns = [rewards, discounts, importance, selected, taken_actions, buffer_slots // 512, buffer_slots % 512, rewards]
    cols = jnp.stack([c.astype(F32) for c in columns], axis=1)
    last = PIX - 128 * (TILES - 1)
    edge = jnp.pad(frames[0, :, :, PIX - last :].reshape(rows * STACK, last), ((0, 0), (0, 128 - last)))
    weights = (
        conv1_weight[0].T, conv2_weight[0].T, conv3_weight[0].T, dense_weight[0],
        conv1_bias, conv2_bias, conv3_bias, dense_bias, head_weight[0].T, head_bias,
    )
    wide_frames, dense, sums = core(plan, frames, edge, weights, cols, (lane_action, compact))
    frame_part, w4, k1, b1, k2, b2, k3, b3, b4, w5, b5, losses = finish(plan, wide_frames, dense, sums)
    own = slots // (roles * batch)
    priorities = lax.dynamic_slice_in_dim(losses.reshape(-1), (role * batch + place) * own, own, 0)
    return (frame_part, k1.T, b1[0], k2.T, b2[0], k3.T, b3[0], w4, b4[0], w5.T, b5[0], priorities)


def solution(mesh):
    in_specs = (
        P("role", "batch", None, None),
        P("role", None, None),
        P("role", None),
        P("role", None, None),
        P("role", None),
        P("role", None, None),
        P("role", None),
        P("role", None, None),
        P("role", None),
        P("role", None, None),
        P("role", None),
        P("batch"),
        P("batch"),
        P("batch"),
        P("batch"),
        P("batch"),
        P("batch"),
    )
    out_specs = (
        P("batch", "role", None),
        P(),
        P(),
        P(),
        P(),
        P(),
        P(),
        P(),
        P(),
        P(),
        P(),
        P(("role", "batch")),
    )
    return jax.shard_map(on_device, mesh=mesh, in_specs=in_specs, out_specs=out_specs, check_vma=False)
```

```python
import functools

import jax
import jax.numpy as jnp
import numpy as np
from jax import lax
from jax.experimental import pallas as pl
from jax.experimental.pallas import tpu as pltpu
from jax.sharding import PartitionSpec as P

STACK = 4
SIDE = 84
ACTIONS = 18
ATOMS = 51
LOGITS = ACTIONS * ATOMS
PIX = SIDE * SIDE
BAND = 4 * SIDE
WIDE = 384
TILES = 56
SUB = 32
F32 = jnp.float32
BF16 = jnp.bfloat16
HIGHEST = lax.Precision.HIGHEST
MESH = pl.DeviceIdType.MESH

NN = (((1,), (0,)), ((), ()))
NT = (((1,), (1,)), ((), ()))
TN = (((0,), (0,)), ((), ()))

ROW_HEAD = 3136
ROW_REST = 4096
ROW_TWO = 0
ROW_THREE = ROW_TWO + 64
ROW_THREE_REST = ROW_THREE + 64
ROW_ONE = ROW_THREE_REST + 64
ROW_BIAS = ROW_ONE + 32
ROW_LOSS = ROW_BIAS + 16


def dot(left, right, dims=NN, precision=None):
    return lax.dot_general(left, right, dims, precision=precision, preferred_element_type=F32)


def iota(shape, dim):
    return lax.broadcasted_iota(jnp.int32, shape, dim)


def onehot(condition, dtype):
    return jnp.where(condition, 1.0, 0.0).astype(dtype)


def silu_and_slope(pre):
    gate = 0.5 * jnp.tanh(0.5 * pre) + 0.5
    act = pre * gate
    return act.astype(BF16), gate + act * (1.0 - gate)


def tall(value):
    return value.reshape(value.shape[0] * value.shape[1], value.shape[2])


class Plan:
    def __init__(self, batch, slots):
        self.batch = batch
        self.bits = batch.bit_length() - 1
        if 1 << self.bits != batch:
            raise ValueError("batch axis")
        self.loss_rows = -(-slots // (512 * 16)) * 16
        unit = 16 * batch
        units = -(-ROW_REST // unit)
        self.rest = units * unit
        rest_units = -(-(ROW_LOSS + self.loss_rows) // unit)
        self.rows = (units + rest_units) * unit
        count = min(4, units)
        up = list(range(self.bits))
        round_way = up[:1] + up[2:] + up[1:2]
        self.streams, at = [], 0
        for s in range(count):
            size = (units // count + (1 if s < units % count else 0)) * unit
            self.streams.append((at, size, up if s % 2 == 0 else round_way))
            at += size
        self.first = list(range(count))
        self.second = [count]
        self.streams.append((at, rest_units * unit, up))


def banded_first(kernel_t, channel, line, column, real, channels, lanes):
    rows = channel.shape[0]
    spread = onehot((iota((lanes, 32), 0) & 31) == iota((lanes, 32), 1), BF16)
    tiled = dot(spread, kernel_t).astype(BF16)
    block, rest = column >> 2, column & 3
    lane_x = iota((rows, lanes), 1) >> 5
    found = []
    for half in range(2):
        parts = []
        for step in range(2):
            goal = jnp.where(real, channel * 64 + (4 * half + line) * 8 + 4 * step + rest, -1)
            pick = onehot(iota((rows, channels * 64), 1) == goal, BF16)
            parts.append(dot(pick, tiled, NT))
        found.append(jnp.where(lane_x == block, parts[0], jnp.where(lane_x == block - 1, parts[1], 0.0)).astype(BF16))
    return found


def build_first(kernel_t, out):
    row = iota((512, 1), 0)
    found = banded_first(kernel_t, row >> 7, (row >> 5) & 3, row & 31, row >= 0, STACK, 224)
    for half in range(2):
        out[512 * half : 512 * half + 512] = found[half]


def build_frame(kernel_t, out):
    row = iota((2 * WIDE, 1), 0)
    channel = (row >= WIDE).astype(jnp.int32)
    inner = row - channel * WIDE
    line = sum((inner >= SIDE * i).astype(jnp.int32) for i in range(1, 5))
    found = banded_first(kernel_t, channel, line, inner - line * SIDE, line < 4, 2, 640)
    for half in range(2):
        out[half] = found[half]


def build_second(kernel_t, out):
    goal = (iota((512, 512), 0) & 31) * 16 + (iota((512, 512), 0) >> 5)
    by_place = dot(onehot(iota((512, 512), 1) == goal, BF16), kernel_t, NT).astype(BF16)
    out[...] = jnp.zeros_like(out)
    for ky in range(4):
        for kx in range(4):
            piece = by_place[(ky * 4 + kx) * 32 : (ky * 4 + kx + 1) * 32]
            for x in range(3):
                low = 256 * ky + (2 * x + kx) * 32
                out[low : low + 32, 64 * x : 64 * x + 64] = piece


def build_third(kernel_t, tall_out, wide_out):
    goal = (iota((576, 576), 0) & 63) * 9 + (iota((576, 576), 0) >> 6)
    by_place = dot(onehot(iota((576, 576), 1) == goal, BF16), kernel_t, NT).astype(BF16)
    tall_out[...] = jnp.zeros_like(tall_out)
    wide_out[...] = jnp.zeros_like(wide_out)
    for ky in range(3):
        for kx in range(3):
            piece = by_place[(ky * 3 + kx) * 64 : (ky * 3 + kx + 1) * 64]
            for x in range(2):
                low = (x + kx) * 64
                tall_out[256 * ky + low : 256 * ky + low + 64, 64 * x : 64 * x + 64] = piece
                wide_out[low : low + 64, 128 * ky + 64 * x : 128 * ky + 64 * x + 64] = piece


def build_picks(out):
    lane = iota((1, WIDE), 1)
    group, line, column = lane >> 7, (lane >> 5) & 3, lane & 31
    goal = jnp.where(28 * group + column < SIDE, SIDE * line + 28 * group + column, -1000)
    row = iota((512, WIDE), 0)
    for kind in range(8):
        out[512 * kind : 512 * kind + 512, :WIDE] = onehot(row == goal + (BAND * kind) % 128, BF16)


def frame_products(grads, band_k, acc):
    acc[...] = dot(tall(grads[1:22]), band_k[0], NT) + dot(tall(grads[0:21]), band_k[1], NT)


def frame_tile(acc, c, t):
    pieces, at, end = [], 128 * t, min(128 * t + 128, PIX)
    while at < end:
        band, inner = divmod(at, BAND)
        size = min(end - at, BAND - inner)
        pieces.append(acc[band * SUB : (band + 1) * SUB, WIDE * c + inner : WIDE * c + inner + size])
        at += size
    if end < 128 * t + 128:
        pieces.append(jnp.zeros((SUB, 128 * t + 128 - end), F32))
    return pieces[0] if len(pieces) == 1 else jnp.concatenate(pieces, axis=1)


def core_kernel(plan, steps, *refs):
    (
        x_hbm, edge, k1_ref, k2_ref, k3_ref, w4_hbm, b1_ref, b2_ref, b3_ref, b4, w5, b5, taken, following, rewards, discounts,
        weighting, buffer_slots, lane_action, compact,
    ) = refs[:20]
    frame_out, dense_out, sums_out, x_kept, a1_kept, a2_kept, pad2_kept, pad3_kept = refs[20:28]
    (
        raw, lines, x, a1, s1, a2, s2, a3, s3, a4, g4, delta_all, g1, pad2, pad3, acc, band_k,
        k1, k2, k3, k3_wide, w4, bias, acc1, acc2, acc3, bias_sums, loss_sums, send, landed, final, probs_all, logp, nexts,
        totals, totals_in, k1_online, cols, slope4,
        keep_sem, back_sem, raw_sem, w4_sem, tile_sem, probs_send, probs_recv, g1_send, g1_recv, tot_send, tot_recv, k1_send, k1_recv,
        rs_send, rs_recv, ag_send, ag_recv, x_send, x_recv, out_sem,
    ) = refs[28:]
    role, place = lax.axis_index("role"), lax.axis_index("batch")
    online = role == 0

    def bit_of(bit):
        return (place // (1 << bit)) % 2

    def across(bit):
        return {"batch": place + (1 - 2 * bit_of(bit)) * (1 << bit)}

    other_role = {"role": 1 - role}

    def remote(src, dst, send_sem, recv_sem, device):
        return pltpu.make_async_remote_copy(
            src_ref=src, dst_ref=dst, send_sem=send_sem, recv_sem=recv_sem, device_id=device, device_id_type=MESH
        )

    def raw_copies(step, slot):
        return [
            pltpu.make_async_copy(
                x_hbm.at[0, pl.ds(step * SUB, SUB), :, pl.ds(128 * t, 128)], raw.at[slot, t], raw_sem.at[slot]
            )
            for t in range(TILES - 1)
        ]

    weight_copy = pltpu.make_async_copy(w4_hbm, send.at[pl.ds(0, 3136)], w4_sem)
    weight_copy.start()
    for c in raw_copies(0, 0):
        c.start()

    barrier = pltpu.get_barrier_semaphore()
    for bit in range(plan.bits):
        pl.semaphore_signal(barrier, inc=1, device_id=across(bit), device_id_type=MESH)
    pl.semaphore_signal(barrier, inc=1, device_id=other_role, device_id_type=MESH)

    slot_number = buffer_slots[...].astype(F32)
    slot_row = jnp.floor(slot_number * (1.0 / 512))
    taken_number = taken[...].astype(F32)
    facts = [
        rewards[...], discounts[...], weighting[...], jnp.where(online, taken_number, following[...].astype(F32)), taken_number,
        slot_row, slot_number - 512.0 * slot_row, rewards[...],
    ]
    cols[...] = dot(jnp.concatenate(facts, axis=0), onehot(iota((8, 128), 0) == iota((8, 128), 1), F32), TN, HIGHEST)
    totals[0] = jnp.broadcast_to(jnp.sum(weighting[...], axis=1, keepdims=True), (8, 128))

    def total_copy(stage):
        return remote(totals.at[stage], totals_in.at[stage], tot_send.at[stage], tot_recv.at[stage], across(stage))

    def total_step(stage):
        if stage > 0:
            total_copy(stage - 1).wait_recv()
            totals[stage] = totals[stage - 1] + totals_in[stage - 1]
        if stage < plan.bits:
            total_copy(stage).start()

    build_first(k1_ref[...], k1)
    build_second(k2_ref[...], k2)
    build_third(k3_ref[...], k3, k3_wide)

    kernel_copy = remote(k1_ref, k1_online, k1_send, k1_recv, other_role)

    pl.semaphore_wait(barrier, plan.bits + 1)
    total_step(0)

    @pl.when(online)
    def _():
        kernel_copy.start()

    weight_copy.wait()
    spare = raw.reshape(2, (TILES - 1) * SUB * STACK, 128)
    for pair in range(2):
        for q in range(2):
            low = 128 * (2 * pair + q)
            spare[1, 3136 * q : 3136 * q + 3136] = send[:3136, low : low + 128].astype(F32)
        for spot in range(49):
            for q in range(2):
                low = 128 * (2 * pair + q)
                w4[64 * spot : 64 * spot + 64, low : low + 128] = spare[
                    1, pl.ds(3136 * q + spot, 64, stride=49), :
                ].astype(BF16)
    total_step(1)
    build_picks(send)
    bias[...] = jnp.zeros_like(bias)
    for at, (ref, size, copies) in enumerate(((b1_ref, 32, 20), (b2_ref, 64, 9), (b3_ref, 64, 7))):
        repeat = onehot((iota((size, size * copies), 1) & (size - 1)) == iota((size, size * copies), 0), F32)
        bias[at : at + 1, : size * copies] = dot(ref[...], repeat, precision=HIGHEST)
    total_step(2)
    acc1[...] = jnp.zeros_like(acc1)
    acc2[...] = jnp.zeros_like(acc2)
    acc3[...] = jnp.zeros_like(acc3)
    bias_sums[...] = jnp.zeros_like(bias_sums)
    loss_sums[...] = jnp.zeros_like(loss_sums)
    pad3[...] = jnp.zeros_like(pad3)
    pad2[...] = jnp.zeros_like(pad2)
    a2[...] = jnp.zeros_like(a2)
    for step in range(steps):
        g1[step, 0] = jnp.zeros((SUB, 640), BF16)
        g1[step, 21] = jnp.zeros((SUB, 640), BF16)

    raw_flat = raw.reshape(2, TILES - 1, SUB * STACK, 128)

    def forward(step, slot, hooks=()):
        hooks = list(hooks)

        def hook():
            if hooks:
                hooks.pop(0)()

        rows = pl.ds(pl.multiple_of(step * SUB, SUB), SUB)
        own = cols[rows, :]
        for kind in range(8):
            bands = list(range(kind, 21, 8))
            for at, band in enumerate(bands):
                low = BAND * band // 128
                for c in range(STACK):
                    place_at = (at * STACK + c) * SUB
                    for t in range(4):
                        if low + t < TILES - 1:
                            piece = raw_flat[slot, low + t, pl.ds(c, SUB, stride=STACK), :]
                        else:
                            piece = edge[pl.ds(pl.multiple_of(step * SUB, SUB), SUB), c, :]
                            piece = jnp.concatenate([piece, jnp.zeros((SUB, 128 - piece.shape[1]), F32)], axis=1)
                        lines[place_at : place_at + SUB, 128 * t : 128 * t + 128] = piece.astype(BF16)
            count = len(bands) * STACK * SUB
            sorted_lines = dot(lines[:count], send[512 * kind : 512 * kind + 512, :WIDE]).astype(BF16)
            for at, band in enumerate(bands):
                for c in range(STACK):
                    place_at = (at * STACK + c) * SUB
                    for group in range(3):
                        x[band, :, 512 * group + 128 * c : 512 * group + 128 * c + 128] = sorted_lines[
                            place_at : place_at + SUB, 128 * group : 128 * group + 128
                        ]
        hook()
        for group, lanes in enumerate((224, 224, 192)):
            part = tall(x[:, :, 512 * group : 512 * group + 512])
            joined = jnp.concatenate([part[: 20 * SUB], part[SUB:]], axis=1)
            acc[: 20 * SUB, 224 * group : 224 * group + lanes] = dot(joined, k1[:, :lanes])
        hook()
        for y in range(20):
            act, slope = silu_and_slope(acc[y * SUB : (y + 1) * SUB, :640] + bias[0:1, :640])
            a1[y % 2, y // 2] = act
            s1[y % 2, y // 2] = slope
        hook()
        for group in range(3):
            even, odd = (tall(a1[p, :, :, 192 * group : 192 * group + 256]) for p in range(2))
            joined = jnp.concatenate([even[: 9 * SUB], odd[: 9 * SUB], even[SUB:], odd[SUB:]], axis=1)
            acc[: 9 * SUB, 192 * group : 192 * group + 192] = dot(joined, k2[...])
        for y in range(9):
            act, slope = silu_and_slope(acc[y * SUB : (y + 1) * SUB, :576] + bias[1:2, :576])
            a2[y, :, :576] = act
            s2[y] = slope
        hook()
        for pair in range(4):
            low = 128 * pair
            joined = jnp.concatenate([tall(a2[ky : ky + 7, :, low : low + 256]) for ky in range(3)], axis=1)
            acc[: 7 * SUB, low : low + 128] = dot(joined, k3[...])
        hook()
        pre4 = b4[...]
        for y in range(7):
            act, slope = silu_and_slope(acc[y * SUB : (y + 1) * SUB, :448] + bias[2:3, :448])
            a3[y, rows, :] = act
            s3[y] = slope
            pre4 = pre4 + dot(act, w4[448 * y : 448 * y + 448])
        act, slope = silu_and_slope(pre4)
        a4[rows, :] = act
        logits = dot(act, w5[...], NT) + b5[...]
        picked = jnp.where(lane_action[...] == own[:, 3:4], logits, 0.0)
        high = picked.astype(BF16)
        rest = picked - high.astype(F32)
        middle = rest.astype(BF16)
        low_part = (rest - middle.astype(F32)).astype(BF16)
        thrice = dot(jnp.concatenate([high, middle, low_part], axis=0), compact[...], NT)
        chosen = thrice[:SUB] + thrice[SUB : 2 * SUB] + thrice[2 * SUB :]
        real = iota((SUB, 128), 1) < ATOMS
        shifted = chosen - jnp.max(jnp.where(real, chosen, -jnp.inf), axis=1, keepdims=True)
        exps = jnp.where(real, jnp.exp(shifted), 0.0)
        sums = jnp.sum(exps, axis=1, keepdims=True)
        probs_all[step] = exps / sums
        logp[...] = jnp.where(real, shifted - jnp.log(sums), 0.0)
        return slope

    def probs_copy(step):
        return remote(probs_all.at[step], nexts.at[step], probs_send.at[step], probs_recv.at[step], other_role)

    def grad_copy(step, half):
        spot = g1.at[step, pl.ds(1 + 10 * half, 10)]
        return remote(spot, spot, g1_send.at[2 * step + half], g1_recv.at[2 * step + half], other_role)

    def grad_start(step):
        for half in range(2):
            grad_copy(step, half).start()

    def backward(step):
        rows = pl.ds(pl.multiple_of(step * SUB, SUB), SUB)
        own = cols[rows, :]
        nodes = iota((SUB, 128), 1).astype(F32)
        reward, discount, importance = own[:, 0:1], own[:, 1:2], own[:, 2:3]
        support = -10.0 + 20.0 / (ATOMS - 1) * nodes
        spot = (jnp.clip(reward + discount * support, -10.0, 10.0) + 10.0) * ((ATOMS - 1) / 20.0)
        next_probs = nexts[step]
        projected = jnp.zeros((SUB, 128), F32)
        for j in range(ATOMS):
            projected += next_probs[:, j : j + 1] * jnp.maximum(0.0, 1.0 - jnp.abs(spot[:, j : j + 1] - nodes))
        projected = jnp.where(nodes < ATOMS, projected, 0.0)
        mass = jnp.sum(projected, axis=1, keepdims=True)
        row_loss = -jnp.sum(projected * logp[...], axis=1, keepdims=True)
        high = (row_loss * onehot(own[:, 5:6] == iota((SUB, plan.loss_rows), 1).astype(F32), F32)).astype(BF16)
        low = onehot(own[:, 6:7] == iota((SUB, 512), 1).astype(F32), BF16)
        loss_sums[...] += dot(high, low, TN)
        scaled = importance / totals[plan.bits, 0:1, 0:1]
        delta = (scaled * (probs_all[step] * mass - projected)).astype(BF16)
        spread = dot(delta, compact[...])
        delta_full = jnp.where(lane_action[...] == own[:, 4:5], spread, 0.0).astype(BF16)
        delta_all[rows, :] = delta_full
        grad4 = (dot(delta_full, w5[...]) * slope4[...]).astype(BF16)
        g4[rows, :] = grad4
        for y in range(7):
            pad3[y + 2, :, :448] = (dot(grad4, w4[448 * y : 448 * y + 448], NT) * s3[y]).astype(BF16)
        for pair in range(4):
            low = 128 * pair
            joined = jnp.concatenate([tall(pad3[2 - ky : 11 - ky, :, low : low + 128]) for ky in range(3)], axis=1)
            total = dot(joined, k3_wide[...], NT)
            if pair == 0:
                acc[: 9 * SUB, :256] = total
            else:
                acc[: 9 * SUB, low : low + 128] += total[:, :128]
                acc[: 9 * SUB, low + 128 : low + 256] = total[:, 128:]
        for y in range(9):
            pad2[y + 1] = (acc[y * SUB : (y + 1) * SUB, :576] * s2[y]).astype(BF16)
        for parity in range(2):
            for group in range(3):
                low = 192 * group
                part = tall(pad2[:, :, low : low + 192])
                total = dot(part[SUB:], k2[256 * parity : 256 * parity + 256], NT) + dot(
                    part[: 10 * SUB], k2[256 * parity + 512 : 256 * parity + 768], NT
                )
                if group == 0:
                    acc[: 10 * SUB, :256] = total
                else:
                    acc[: 10 * SUB, low : low + 64] += total[:, :64]
                    acc[: 10 * SUB, low + 64 : low + 256] = total[:, 64:]
            for m in range(10):
                g1[step, 2 * m + parity + 1] = (acc[m * SUB : (m + 1) * SUB, :640] * s1[parity, m]).astype(BF16)

    kept = ((x, x_kept), (a1, a1_kept), (a2, a2_kept), (pad2, pad2_kept), (pad3, pad3_kept))

    def keep_copies(step, low, high):
        return [pltpu.make_async_copy(kept[i][0], kept[i][1].at[step], keep_sem.at[i]) for i in range(low, high)]

    def back_copies(step, low, high):
        return [pltpu.make_async_copy(kept[i][1].at[step], kept[i][0], back_sem.at[i]) for i in range(low, high)]

    early = max(steps - 3, 0)

    def prefetch(step, slot):
        @pl.when(step < steps)
        def _():
            for c in raw_copies(step, slot):
                c.start()

    def raw_wait(step, slot):
        for c in raw_copies(step, slot):
            c.wait()

    def after_forward(step):
        @pl.when(role == 1)
        def _():
            probs_copy(step).start()

        @pl.when(online & (step + 1 < steps))
        def _():
            for c in keep_copies(step, 0, 3):
                c.start()

    raw_wait(0, 0)
    prefetch(1, 1)
    hooks = [functools.partial(total_step, stage) for stage in range(3, plan.bits + 1)]
    slope4[...] = forward(0, 0, hooks[:6])
    for late in hooks[6:]:
        late()
    after_forward(0)

    def one_step(step, _):
        @pl.when(online)
        def _():
            @pl.when(step > 0)
            def _():
                for c in keep_copies(step - 1, 3, 5):
                    c.wait()

            probs_copy(step).wait_recv()
            backward(step)

            @pl.when(step < early)
            def _():
                grad_start(step)

            @pl.when(step + 1 < steps)
            def _():
                for c in keep_copies(step, 3, 5):
                    c.start()

        @pl.when(step + 1 < steps)
        def _():
            following_step = step + 1
            slot = following_step % 2
            raw_wait(following_step, slot)
            prefetch(following_step + 1, 1 - slot)

            @pl.when(online)
            def _():
                for c in keep_copies(step, 0, 3):
                    c.wait()

            slope4[...] = forward(following_step, slot)
            after_forward(following_step)

        return 0

    lax.fori_loop(0, steps, one_step, 0)

    for stage in range(plan.bits):
        total_copy(stage).wait_send()

    def late_layers(step):
        total = None
        for group in range(3):
            low = 192 * group
            even, odd = (tall(a1[p, :, :, low : low + 256]) for p in range(2))
            joined = jnp.concatenate([even[: 9 * SUB], odd[: 9 * SUB], even[SUB:], odd[SUB:]], axis=1)
            term = dot(tall(pad2[1:10, :, low : low + 192]), joined, TN)
            total = term if total is None else total + term
        acc2[...] += total
        total = None
        for pair in range(4):
            low = 128 * pair
            joined = jnp.concatenate([tall(a2[ky : ky + 7, :, low : low + 256]) for ky in range(3)], axis=1)
            term = dot(tall(pad3[2:9, :, low : low + 128]), joined, TN)
            total = term if total is None else total + term
        acc3[...] += total
        for at, (count, lanes) in enumerate(((20, 640), (9, 576), (7, 448))):
            part = jnp.zeros((8, lanes), F32)
            for y in range(count):
                piece = (g1[step, y + 1] if at == 0 else pad2[y + 1] if at == 1 else pad3[y + 2, :, :448]).astype(F32)
                for q in range(SUB // 8):
                    part += piece[8 * q : 8 * q + 8]
            bias_sums[at, :, :lanes] += part

    def first_layer(step):
        for group in range(3):
            lanes = 192 if group == 2 else 224
            part = tall(g1[step, 1:21, :, 224 * group : 224 * group + lanes])
            pixels = tall(x[:, :, 512 * group : 512 * group + 512])
            joined = jnp.concatenate([pixels[: 20 * SUB], pixels[SUB:]], axis=1)
            acc1[:lanes] += dot(part, joined, TN)

    def weight_step(turn, step):
        @pl.when(turn > 0)
        def _():
            for c in back_copies(step, 1, 5):
                c.wait()

        late_layers(step)

        @pl.when(turn + 1 < steps)
        def _():
            for c in back_copies(turn, 1, 5):
                c.start()

        @pl.when(turn > 0)
        def _():
            for c in back_copies(step, 0, 1):
                c.wait()

        first_layer(step)

        @pl.when(turn + 1 < steps)
        def _():
            for c in back_copies(turn, 0, 1):
                c.start()

    def dense_sums():
        flat = raw.reshape(2 * (TILES - 1) * SUB * STACK, 128)
        for y in range(7):
            block = dot(a3[y], g4[...], TN)
            for px in range(7):
                for q in range(4):
                    flat[pl.ds(3136 * q + 7 * y + px, 64, stride=49), :] = block[
                        64 * px : 64 * px + 64, 128 * q : 128 * q + 128
                    ]
        for q in range(4):
            send[:3136, 128 * q : 128 * q + 128] = flat[3136 * q : 3136 * q + 3136].astype(BF16)
        head = dot(delta_all[...], a4[...], TN)
        send[ROW_HEAD : ROW_HEAD + 912] = head[:912].astype(BF16)
        send[ROW_HEAD + 912 : ROW_HEAD + 928] = jnp.concatenate(
            [head[912:LOGITS], jnp.zeros((928 - LOGITS, 512), F32)], axis=0
        ).astype(BF16)
        send[ROW_HEAD + 928 : plan.rest] = jnp.zeros((plan.rest - ROW_HEAD - 928, 512), BF16)

    def other_sums():
        def put(low, value):
            send[plan.rest + low : plan.rest + low + value.shape[0]] = value.astype(BF16)

        folded = acc1[0:32]
        for px in range(1, 7):
            folded += pltpu.roll(acc1[32 * px : 32 * px + 32], 1024 - 4 * px, 1)
        column = iota((1024, 256), 1)
        goal = ((column >> 5) & 1) * 512 + (column >> 6) * 128 + ((column >> 3) & 3) * 32 + (column & 7)
        pick = onehot(iota((1024, 256), 0) == goal, F32)
        put(ROW_ONE, jnp.concatenate([dot(folded, pick, precision=HIGHEST), jnp.zeros((32, 256), F32)], axis=1))
        folded = acc2[0:64]
        for px in range(1, 3):
            folded += pltpu.roll(acc2[64 * px : 64 * px + 64], 1024 - 64 * px, 1)
        column = iota((1024, 512), 1)
        goal = ((column >> 2) & 3) * 256 + (column & 3) * 32 + (column >> 4)
        pick = onehot(iota((1024, 512), 0) == goal, F32)
        put(ROW_TWO, dot(folded, pick, precision=HIGHEST))
        folded = acc3[0:64] + pltpu.roll(acc3[64:128], 768 - 64, 1)
        row = iota((768, 576), 0)
        goal = (row & 63) * 9 + (row >> 8) * 3 + ((row >> 6) & 3)
        pick = onehot((iota((768, 576), 1) == goal) & (((row >> 6) & 3) < 3), F32)
        third = dot(folded, pick, precision=HIGHEST)
        put(ROW_THREE, third[:, :512])
        put(ROW_THREE_REST, jnp.concatenate([third[:, 512:], jnp.zeros((64, 448), F32)], axis=1))
        bias_rows = []
        for at, (size, copies) in enumerate(((32, 20), (64, 9), (64, 7))):
            fold = onehot((iota((size * copies, 512), 0) & (size - 1)) == iota((size * copies, 512), 1), F32)
            line = jnp.sum(bias_sums[at, :, : size * copies], axis=0, keepdims=True)
            bias_rows.append(dot(line, fold, precision=HIGHEST))
        bias_rows.append(jnp.sum(g4[...].astype(F32), axis=0, keepdims=True))
        head_bias = jnp.sum(delta_all[...].astype(F32), axis=0, keepdims=True)
        bias_rows.append(head_bias[:, :512])
        bias_rows.append(jnp.concatenate([head_bias[:, 512:], jnp.zeros((1, 1024 - LOGITS), F32)], axis=1))
        bias_rows.append(jnp.zeros((10, 512), F32))
        put(ROW_BIAS, jnp.concatenate(bias_rows, axis=0))
        put(ROW_LOSS, loss_sums[...])
        left = plan.rows - plan.rest - ROW_LOSS - plan.loss_rows
        if left:
            put(ROW_LOSS + plan.loss_rows, jnp.zeros((left, 512), F32))

    def stage_rows(stream, stage):
        base, size, order = plan.streams[stream]
        low = base
        for bit in order[:stage]:
            size //= 2
            low = low + bit_of(bit) * size
        return low, size

    def aligned(at):
        return pl.multiple_of(at, 16)

    def scatter_copy(stream, stage):
        base, size, order = plan.streams[stream]
        low, count = stage_rows(stream, stage)
        half = count // 2
        away = aligned(low + (1 - bit_of(order[stage])) * half)
        into = base + size - count
        index = stream * plan.bits + stage
        return remote(
            send.at[pl.ds(away, half)], landed.at[pl.ds(into, half)], rs_send.at[index], rs_recv.at[index],
            across(order[stage]),
        )

    def scatter_start(streams):
        for stream in streams:
            scatter_copy(stream, 0).start()

    def scatter_finish(stage, streams):
        for stream in streams:
            base, size, order = plan.streams[stream]
            scatter_copy(stream, stage).wait_recv()
            low, count = stage_rows(stream, stage)
            half = count // 2
            keep = aligned(low + bit_of(order[stage]) * half)
            into = base + size - count
            target = final if stage == plan.bits - 1 else send
            block = 64 if half % 64 == 0 else 16

            def add(i, _, keep=keep, into=into, target=target, block=block):
                at = aligned(keep + i * block)
                new = landed[pl.ds(aligned(into + i * block), block)].astype(F32)
                target[pl.ds(at, block)] = (send[pl.ds(at, block)].astype(F32) + new).astype(BF16)
                return 0

            lax.fori_loop(0, half // block, add, 0)
            if stage + 1 < plan.bits:
                scatter_copy(stream, stage + 1).start()
            else:
                over_copy(stream).start()
                gather_copy(stream, 0).start()

    def over_copy(stream):
        low, count = stage_rows(stream, plan.bits)
        spot = pl.ds(aligned(low), count)
        return remote(final.at[spot], final.at[spot], x_send.at[stream], x_recv.at[stream], other_role)

    def gather_copy(stream, stage):
        order = plan.streams[stream][2]
        low, count = stage_rows(stream, plan.bits - stage)
        spot = pl.ds(aligned(low), count)
        index = stream * plan.bits + stage
        return remote(
            final.at[spot], final.at[spot], ag_send.at[index], ag_recv.at[index], across(order[plan.bits - 1 - stage])
        )

    def over_finish(streams):
        for stream in streams:
            over_copy(stream).wait_recv()
            gather_copy(stream, 0).start()

    def gather_finish(stage, streams):
        for stream in streams:
            gather_copy(stream, stage).wait_recv()
            if stage + 1 < plan.bits:
                gather_copy(stream, stage + 1).start()

    tile_rows = raw.reshape(2 * (TILES - 1) * SUB * STACK, 128)

    tile_pairs = raw.reshape((TILES - 1) * SUB * STACK, 2, 128)

    def tile_copies(step):
        return [
            pltpu.make_async_copy(
                tile_pairs.at[pl.ds(t * SUB, SUB)],
                frame_out.at[pl.ds(step * SUB, SUB), :, pl.ds(128 * t, 128)],
                tile_sem,
            )
            for t in range(TILES)
        ]

    def frame_step(step):
        frame_products(g1.at[step], band_k, acc)

        @pl.when(step > 0)
        def _():
            for c in tile_copies(step - 1):
                c.wait()

        for c in range(2):
            for t in range(TILES):
                tile_rows[pl.ds(t * SUB * 2 + c, SUB, stride=2), :] = frame_tile(acc, c, t)
        for c in tile_copies(step):
            c.start()

    bits, first, second = plan.bits, plan.first, plan.second

    late_grads = [(step, half) for step in range(early, steps) for half in range(2)]
    issue = {"soon": late_grads[:-4], "mid": late_grads[-4:-3], "over": late_grads[-3:-2], "last": late_grads[-2:]}

    def grads_at(moment):
        for step, half in issue[moment]:
            grad_copy(step, half).start()

    def turn_at(number):
        return min(number, steps - 1)

    @pl.when(online)
    def _():
        dense_sums()
        scatter_start(first)

        def turns(turn, _):
            weight_step(turn, jnp.where(turn == 0, steps - 1, turn - 1))

            @pl.when(turn == turn_at(1))
            def _():
                scatter_finish(0, first)
                grads_at("soon")

            return 0

        lax.fori_loop(0, steps, turns, 0)
        scatter_finish(1, first)
        grads_at("mid")
        other_sums()
        scatter_start(second)
        build_frame(k1_ref[:, 0:128], band_k)

    @pl.when(role == 1)
    def _():
        kernel_copy.wait_recv()
        build_frame(k1_online[:, 128:256], band_k)

    def frame_and_more(step, _):
        @pl.when(role == 1)
        def _():
            for half in range(2):
                grad_copy(step, half).wait_recv()

        frame_step(step)

        @pl.when(online & (step == 0))
        def _():
            scatter_finish(0, second)
            scatter_finish(2, first)

        @pl.when(online & (step == turn_at(1)))
        def _():
            scatter_finish(1, second)

        @pl.when(online & (step == turn_at(2)))
        def _():
            for stage in range(3, bits):
                scatter_finish(stage, first)
            grads_at("over")
            scatter_finish(2, second)

        @pl.when(online & (step == turn_at(3)))
        def _():
            for stage in range(3, bits):
                scatter_finish(stage, second)
            grads_at("last")

        @pl.when(online & (step == turn_at(5)))
        def _():
            gather_finish(0, first)
            gather_finish(0, second)

        @pl.when((role == 1) & (step == max(steps - 3, 0)))
        def _():
            over_finish(first)
            for stage in range(bits):
                gather_finish(stage, first)
                if stage == 0:
                    over_finish(second)
                else:
                    gather_finish(stage - 1, second)
            gather_finish(bits - 1, second)

        return 0

    lax.fori_loop(0, steps, frame_and_more, 0)

    @pl.when(online)
    def _():
        for stage in range(1, bits):
            gather_finish(stage, first)
            gather_finish(stage, second)

    out_copies = [
        pltpu.make_async_copy(final.at[pl.ds(0, ROW_HEAD)], dense_out, out_sem.at[0]),
        pltpu.make_async_copy(final.at[pl.ds(ROW_HEAD, plan.rows - ROW_HEAD)], sums_out, out_sem.at[1]),
    ]
    for c in out_copies:
        c.start()

    for c in tile_copies(steps - 1):
        c.wait()
    for stream in range(len(plan.streams)):
        for stage in range(plan.bits):
            gather_copy(stream, stage).wait_send()

    @pl.when(online)
    def _():
        kernel_copy.wait_send()
        for stream in range(len(plan.streams)):
            over_copy(stream).wait_send()
            for stage in range(plan.bits):
                scatter_copy(stream, stage).wait_send()

        def sent(step, _):
            for half in range(2):
                grad_copy(step, half).wait_send()
            return 0

        lax.fori_loop(0, steps, sent, 0)

    @pl.when(role == 1)
    def _():
        def sent(step, _):
            probs_copy(step).wait_send()
            return 0

        lax.fori_loop(0, steps, sent, 0)

    for c in out_copies:
        c.wait()


def core(plan, frames, edge, weights, facts, tables):
    rows = frames.shape[1]
    steps = rows // SUB
    k1, k2, k3, w4, b1, b2, b3, b4, w5, b5 = weights
    vmem, hbm = pl.BlockSpec(memory_space=pltpu.VMEM), pl.BlockSpec(memory_space=pl.ANY)
    dma = pltpu.SemaphoreType.DMA
    streams = len(plan.streams)
    scratch = [
        pltpu.VMEM((2, TILES - 1, SUB, STACK, 128), F32),
        pltpu.VMEM((3 * STACK * SUB, 512), BF16),
        pltpu.VMEM((21, SUB, 1536), BF16),
        pltpu.VMEM((2, 10, SUB, 640), BF16),
        pltpu.VMEM((2, 10, SUB, 640), F32),
        pltpu.VMEM((9, SUB, 640), BF16),
        pltpu.VMEM((9, SUB, 576), F32),
        pltpu.VMEM((7, rows, 448), BF16),
        pltpu.VMEM((7, SUB, 448), F32),
        pltpu.VMEM((rows, 512), BF16),
        pltpu.VMEM((rows, 512), BF16),
        pltpu.VMEM((rows, LOGITS), BF16),
        pltpu.VMEM((steps, 22, SUB, 640), BF16),
        pltpu.VMEM((11, SUB, 576), BF16),
        pltpu.VMEM((11, SUB, 512), BF16),
        pltpu.VMEM((21 * SUB, 2 * WIDE), F32),
        pltpu.VMEM((2, 2 * WIDE, 640), BF16),
        pltpu.VMEM((1024, 224), BF16),
        pltpu.VMEM((1024, 192), BF16),
        pltpu.VMEM((768, 128), BF16),
        pltpu.VMEM((256, 384), BF16),
        pltpu.VMEM((3136, 512), BF16),
        pltpu.VMEM((8, 640), F32),
        pltpu.VMEM((224, 1024), F32),
        pltpu.VMEM((192, 1024), F32),
        pltpu.VMEM((128, 768), F32),
        pltpu.VMEM((3, 8, 640), F32),
        pltpu.VMEM((plan.loss_rows, 512), F32),
        pltpu.VMEM((plan.rows, 512), BF16),
        pltpu.VMEM((plan.rows, 512), BF16),
        pltpu.VMEM((plan.rows, 512), BF16),
        pltpu.VMEM((steps, SUB, 128), F32),
        pltpu.VMEM((SUB, 128), F32),
        pltpu.VMEM((steps, SUB, 128), F32),
        pltpu.VMEM((plan.bits + 1, 8, 128), F32),
        pltpu.VMEM((plan.bits, 8, 128), F32),
        pltpu.VMEM((32, 256), BF16),
        pltpu.VMEM((rows, 128), F32),
        pltpu.VMEM((SUB, 512), F32),
        dma((5,)), dma((5,)), dma((2,)), dma, dma, dma((steps,)), dma((steps,)), dma((2 * steps,)), dma((2 * steps,)),
        dma((plan.bits,)), dma((plan.bits,)), dma, dma,
        dma((streams * plan.bits,)), dma((streams * plan.bits,)), dma((streams * plan.bits,)), dma((streams * plan.bits,)),
        dma((streams,)), dma((streams,)), dma((2,)),
    ]
    return pl.pallas_call(
        functools.partial(core_kernel, plan, steps),
        in_specs=[hbm, vmem, vmem, vmem, vmem, hbm] + [vmem] * 14,
        out_specs=[hbm] * 8,
        out_shape=[
            jax.ShapeDtypeStruct((rows, 2, TILES * 128), F32),
            jax.ShapeDtypeStruct((ROW_HEAD, 512), BF16),
            jax.ShapeDtypeStruct((plan.rows - ROW_HEAD, 512), BF16),
            jax.ShapeDtypeStruct((steps - 1, 21, SUB, 1536), BF16),
            jax.ShapeDtypeStruct((steps - 1, 2, 10, SUB, 640), BF16),
            jax.ShapeDtypeStruct((steps - 1, 9, SUB, 640), BF16),
            jax.ShapeDtypeStruct((steps - 1, 11, SUB, 576), BF16),
            jax.ShapeDtypeStruct((steps - 1, 11, SUB, 512), BF16),
        ],
        scratch_shapes=scratch,
        compiler_params=pltpu.CompilerParams(vmem_limit_bytes=63 << 20, collective_id=0, has_side_effects=True),
        name="core",
    )(frames, edge, k1, k2, k3, w4, b1, b2, b3, b4, w5, b5, *facts, *tables)[:3]


def finish_kernel(plan, own, frames, dense, sums, frame_out, w4, k1, b1, k2, b2, k3, b3, b4, w5, b5, losses):
    frame_out[...] = frames[:, :, :PIX]
    w4[...] = dense[...].astype(F32)

    def part(low, high):
        return sums[plan.rest - ROW_HEAD + low : plan.rest - ROW_HEAD + high]

    @pl.when(pl.program_id(0) == 0)
    def _():
        w5[:912] = sums[:912].astype(F32)
        w5[912:] = sums[912:928].astype(F32)[: LOGITS - 912]
        k2[...] = part(ROW_TWO, ROW_THREE).astype(F32)
        k3[:, :512] = part(ROW_THREE, ROW_THREE_REST).astype(F32)
        k3[:, 512:] = part(ROW_THREE_REST, ROW_ONE)[:, :64].astype(F32)
        k1[...] = part(ROW_ONE, ROW_BIAS)[:, :256].astype(F32)
        rows = part(ROW_BIAS, ROW_LOSS).astype(F32)
        b1[...] = rows[0:1, :32]
        b2[...] = rows[1:2, :64]
        b3[...] = rows[2:3, :64]
        b4[...] = rows[3:4]
        b5[:, :512] = rows[4:5]
        b5[:, 512:] = rows[5:6, : LOGITS - 512]
        device = lax.axis_index("role") * plan.batch + lax.axis_index("batch")
        slot = device * own + iota((1, own), 1)
        chosen = dot(part(ROW_LOSS, ROW_LOSS + plan.loss_rows), onehot(iota((512, own), 0) == (slot & 511), BF16))
        mine = iota((plan.loss_rows, own), 0) == (slot >> 9)
        losses[...] = jnp.sum(jnp.where(mine, chosen, 0.0), axis=0, keepdims=True)


def finish(plan, own, frames, dense, sums):
    rows = frames.shape[0]
    small = ((32, 256), (1, 32), (64, 512), (1, 64), (64, 576), (1, 64), (1, 512), (LOGITS, 512), (1, LOGITS), (1, own))
    block, pieces = (56, 4) if rows % 56 == 0 else (16, 14)
    frame_at, dense_at = (lambda i: (i, 0, 0)), (lambda i: (jnp.minimum(i, pieces - 1), 0))
    return pl.pallas_call(
        functools.partial(finish_kernel, plan, own),
        grid=(rows // block,),
        in_specs=[
            pl.BlockSpec((block, 2, TILES * 128), frame_at),
            pl.BlockSpec((ROW_HEAD // pieces, 512), dense_at),
            pl.BlockSpec(sums.shape, lambda i: (0, 0)),
        ],
        out_specs=[
            pl.BlockSpec((block, 2, PIX), frame_at),
            pl.BlockSpec((ROW_HEAD // pieces, 512), dense_at),
            *[pl.BlockSpec(s, lambda i: (0, 0)) for s in small],
        ],
        out_shape=[jax.ShapeDtypeStruct(s, F32) for s in ((rows, 2, PIX), (ROW_HEAD, 512), *small)],
        compiler_params=pltpu.CompilerParams(vmem_limit_bytes=60 << 20),
        name="finish",
    )(frames, dense, sums)


def on_device(
    frames,
    conv1_weight,
    conv1_bias,
    conv2_weight,
    conv2_bias,
    conv3_weight,
    conv3_bias,
    dense_weight,
    dense_bias,
    head_weight,
    head_bias,
    taken_actions,
    next_actions,
    rewards,
    discounts,
    importance,
    buffer_slots,
):
    roles, batch = lax.axis_size("role"), lax.axis_size("batch")
    rows = frames.shape[1]
    slots = rows * batch
    plan = Plan(batch, slots)

    lane_action = jnp.asarray(np.arange(LOGITS)[None] // ATOMS, F32)
    compact = jnp.asarray(np.arange(128)[:, None] == np.arange(LOGITS)[None] % ATOMS, BF16)
    facts = [
        v.reshape(1, rows) for v in (taken_actions, next_actions, rewards, discounts, importance, buffer_slots)
    ]
    edge = frames[0, :, :, 128 * (TILES - 1) :]
    weights = (
        conv1_weight[0].T, conv2_weight[0].T, conv3_weight[0].T, dense_weight[0],
        conv1_bias, conv2_bias, conv3_bias, dense_bias, head_weight[0].T, head_bias,
    )
    partial = core(plan, frames, edge, weights, facts, (lane_action, compact))
    frame_part, w4, k1, b1, k2, b2, k3, b3, b4, w5, b5, priorities = finish(plan, slots // (roles * batch), *partial)
    return (frame_part, k1.T, b1[0], k2.T, b2[0], k3.T, b3[0], w4, b4[0], w5.T, b5[0], priorities[0])


def solution(mesh):
    in_specs = (
        P("role", "batch", None, None),
        P("role", None, None),
        P("role", None),
        P("role", None, None),
        P("role", None),
        P("role", None, None),
        P("role", None),
        P("role", None, None),
        P("role", None),
        P("role", None, None),
        P("role", None),
        P("batch"),
        P("batch"),
        P("batch"),
        P("batch"),
        P("batch"),
        P("batch"),
    )
    out_specs = (
        P("batch", "role", None),
        P(),
        P(),
        P(),
        P(),
        P(),
        P(),
        P(),
        P(),
        P(),
        P(),
        P(("role", "batch")),
    )
    return jax.shard_map(on_device, mesh=mesh, in_specs=in_specs, out_specs=out_specs, check_vma=False)
```

```python
import functools

import jax
import jax.numpy as jnp
import numpy as np
from jax import lax
from jax.experimental import pallas as pl
from jax.experimental.pallas import tpu as pltpu
from jax.sharding import PartitionSpec as P

STACK = 4
SIDE = 84
ACTIONS = 18
ATOMS = 51
LOGITS = ACTIONS * ATOMS
PIX = SIDE * SIDE
BAND = 4 * SIDE
WIDE = 384
TILES = 56
SUB = 32
F32 = jnp.float32
BF16 = jnp.bfloat16
HIGHEST = lax.Precision.HIGHEST
MESH = pl.DeviceIdType.MESH

NN = (((1,), (0,)), ((), ()))
NT = (((1,), (1,)), ((), ()))
TN = (((0,), (0,)), ((), ()))

ROW_HEAD = 3136
ROW_REST = 4096
ROW_TWO = 0
ROW_THREE = ROW_TWO + 64
ROW_THREE_REST = ROW_THREE + 64
ROW_ONE = ROW_THREE_REST + 64
ROW_BIAS = ROW_ONE + 32
ROW_LOSS = ROW_BIAS + 16


def dot(left, right, dims=NN, precision=None):
    return lax.dot_general(left, right, dims, precision=precision, preferred_element_type=F32)


def iota(shape, dim):
    return lax.broadcasted_iota(jnp.int32, shape, dim)


def onehot(condition, dtype):
    return jnp.where(condition, 1.0, 0.0).astype(dtype)


def silu_and_slope(pre):
    gate = 0.5 * jnp.tanh(0.5 * pre) + 0.5
    act = pre * gate
    return act.astype(BF16), gate + act * (1.0 - gate)


def tall(value):
    return value.reshape(value.shape[0] * value.shape[1], value.shape[2])


class Plan:
    def __init__(self, batch, slots):
        self.batch = batch
        self.bits = batch.bit_length() - 1
        if 1 << self.bits != batch:
            raise ValueError("batch axis")
        self.loss_rows = -(-slots // (512 * 16)) * 16
        unit = 16 * batch
        units = -(-ROW_REST // unit)
        self.rest = units * unit
        rest_units = -(-(ROW_LOSS + self.loss_rows) // unit)
        self.rows = (units + rest_units) * unit
        count = min(4, units)
        up = list(range(self.bits))
        round_way = up[:1] + up[2:] + up[1:2]
        self.streams, at = [], 0
        for s in range(count):
            size = (units // count + (1 if s < units % count else 0)) * unit
            self.streams.append((at, size, up if s % 2 == 0 else round_way))
            at += size
        self.first = list(range(count))
        self.second = [count]
        self.streams.append((at, rest_units * unit, up))


def banded_first(kernel_t, channel, line, column, real, channels, lanes):
    rows = channel.shape[0]
    spread = onehot((iota((lanes, 32), 0) & 31) == iota((lanes, 32), 1), BF16)
    tiled = dot(spread, kernel_t).astype(BF16)
    block, rest = column >> 2, column & 3
    lane_x = iota((rows, lanes), 1) >> 5
    found = []
    for half in range(2):
        parts = []
        for step in range(2):
            goal = jnp.where(real, channel * 64 + (4 * half + line) * 8 + 4 * step + rest, -1)
            pick = onehot(iota((rows, channels * 64), 1) == goal, BF16)
            parts.append(dot(pick, tiled, NT))
        found.append(jnp.where(lane_x == block, parts[0], jnp.where(lane_x == block - 1, parts[1], 0.0)).astype(BF16))
    return found


def build_first(kernel_t, out):
    row = iota((512, 1), 0)
    found = banded_first(kernel_t, row >> 7, (row >> 5) & 3, row & 31, row >= 0, STACK, 224)
    for half in range(2):
        out[512 * half : 512 * half + 512] = found[half]


def build_frame(kernel_t, out):
    row = iota((2 * WIDE, 1), 0)
    channel = (row >= WIDE).astype(jnp.int32)
    inner = row - channel * WIDE
    line = sum((inner >= SIDE * i).astype(jnp.int32) for i in range(1, 5))
    found = banded_first(kernel_t, channel, line, inner - line * SIDE, line < 4, 2, 640)
    for half in range(2):
        out[half] = found[half]


def build_second(kernel_t, out):
    goal = (iota((512, 512), 0) & 31) * 16 + (iota((512, 512), 0) >> 5)
    by_place = dot(onehot(iota((512, 512), 1) == goal, BF16), kernel_t, NT).astype(BF16)
    out[...] = jnp.zeros_like(out)
    for ky in range(4):
        for kx in range(4):
            piece = by_place[(ky * 4 + kx) * 32 : (ky * 4 + kx + 1) * 32]
            for x in range(3):
                low = 256 * ky + (2 * x + kx) * 32
                out[low : low + 32, 64 * x : 64 * x + 64] = piece


def build_third(kernel_t, tall_out, wide_out):
    goal = (iota((576, 576), 0) & 63) * 9 + (iota((576, 576), 0) >> 6)
    by_place = dot(onehot(iota((576, 576), 1) == goal, BF16), kernel_t, NT).astype(BF16)
    tall_out[...] = jnp.zeros_like(tall_out)
    wide_out[...] = jnp.zeros_like(wide_out)
    for ky in range(3):
        for kx in range(3):
            piece = by_place[(ky * 3 + kx) * 64 : (ky * 3 + kx + 1) * 64]
            for x in range(2):
                low = (x + kx) * 64
                tall_out[256 * ky + low : 256 * ky + low + 64, 64 * x : 64 * x + 64] = piece
                wide_out[low : low + 64, 128 * ky + 64 * x : 128 * ky + 64 * x + 64] = piece


def build_picks(out):
    lane = iota((1, WIDE), 1)
    group, line, column = lane >> 7, (lane >> 5) & 3, lane & 31
    goal = jnp.where(28 * group + column < SIDE, SIDE * line + 28 * group + column, -1000)
    row = iota((512, WIDE), 0)
    for kind in range(8):
        out[512 * kind : 512 * kind + 512, :WIDE] = onehot(row == goal + (BAND * kind) % 128, BF16)


def frame_products(grads, band_k, acc):
    acc[...] = dot(tall(grads[1:22]), band_k[0], NT) + dot(tall(grads[0:21]), band_k[1], NT)


def frame_tile(acc, c, t):
    pieces, at, end = [], 128 * t, min(128 * t + 128, PIX)
    while at < end:
        band, inner = divmod(at, BAND)
        size = min(end - at, BAND - inner)
        pieces.append(acc[band * SUB : (band + 1) * SUB, WIDE * c + inner : WIDE * c + inner + size])
        at += size
    if end < 128 * t + 128:
        pieces.append(jnp.zeros((SUB, 128 * t + 128 - end), F32))
    return pieces[0] if len(pieces) == 1 else jnp.concatenate(pieces, axis=1)


def core_kernel(plan, steps, *refs):
    (
        x_hbm, edge, k1_ref, k2_ref, k3_ref, w4_hbm, b1_ref, b2_ref, b3_ref, b4, w5, b5, taken, following, rewards, discounts,
        weighting, buffer_slots, lane_action, compact,
    ) = refs[:20]
    frame_out, dense_out, sums_out, x_kept, a1_kept, a2_kept, pad2_kept, pad3_kept = refs[20:28]
    (
        raw, lines, x, a1, s1, a2, s2, a3, s3, a4, g4, delta_all, g1, pad2, pad3, acc, band_k,
        k1, k2, k3, k3_wide, w4, bias, acc1, acc2, acc3, bias_sums, loss_sums, send, landed, final, probs_all, logp, nexts,
        totals, totals_in, k1_online, cols, slope4,
        keep_sem, back_sem, raw_sem, w4_sem, tile_sem, probs_send, probs_recv, g1_send, g1_recv, tot_send, tot_recv, k1_send, k1_recv,
        rs_send, rs_recv, ag_send, ag_recv, x_send, x_recv, out_sem,
    ) = refs[28:]
    role, place = lax.axis_index("role"), lax.axis_index("batch")
    online = role == 0

    def bit_of(bit):
        return (place // (1 << bit)) % 2

    def across(bit):
        return {"batch": place + (1 - 2 * bit_of(bit)) * (1 << bit)}

    other_role = {"role": 1 - role}

    def remote(src, dst, send_sem, recv_sem, device):
        return pltpu.make_async_remote_copy(
            src_ref=src, dst_ref=dst, send_sem=send_sem, recv_sem=recv_sem, device_id=device, device_id_type=MESH
        )

    def raw_copies(step, slot):
        return [
            pltpu.make_async_copy(
                x_hbm.at[0, pl.ds(step * SUB, SUB), :, pl.ds(128 * t, 128)], raw.at[slot, t], raw_sem.at[slot]
            )
            for t in range(TILES - 1)
        ]

    weight_copy = pltpu.make_async_copy(w4_hbm, send.at[pl.ds(0, 3136)], w4_sem)
    weight_copy.start()
    for c in raw_copies(0, 0):
        c.start()

    barrier = pltpu.get_barrier_semaphore()
    for bit in range(plan.bits):
        pl.semaphore_signal(barrier, inc=1, device_id=across(bit), device_id_type=MESH)
    pl.semaphore_signal(barrier, inc=1, device_id=other_role, device_id_type=MESH)

    slot_number = buffer_slots[...].astype(F32)
    slot_row = jnp.floor(slot_number * (1.0 / 512))
    taken_number = taken[...].astype(F32)
    facts = [
        rewards[...], discounts[...], weighting[...], jnp.where(online, taken_number, following[...].astype(F32)), taken_number,
        slot_row, slot_number - 512.0 * slot_row, rewards[...],
    ]
    cols[...] = dot(jnp.concatenate(facts, axis=0), onehot(iota((8, 128), 0) == iota((8, 128), 1), F32), TN, HIGHEST)
    totals[0] = jnp.broadcast_to(jnp.sum(weighting[...], axis=1, keepdims=True), (8, 128))

    def total_copy(stage):
        return remote(totals.at[stage], totals_in.at[stage], tot_send.at[stage], tot_recv.at[stage], across(stage))

    def total_step(stage):
        if stage > 0:
            total_copy(stage - 1).wait_recv()
            totals[stage] = totals[stage - 1] + totals_in[stage - 1]
        if stage < plan.bits:
            total_copy(stage).start()

    build_first(k1_ref[...], k1)
    build_second(k2_ref[...], k2)
    build_third(k3_ref[...], k3, k3_wide)

    kernel_copy = remote(k1_ref, k1_online, k1_send, k1_recv, other_role)

    pl.semaphore_wait(barrier, plan.bits + 1)
    total_step(0)

    @pl.when(online)
    def _():
        kernel_copy.start()

    weight_copy.wait()
    spare = raw.reshape(2, (TILES - 1) * SUB * STACK, 128)
    for pair in range(2):
        for q in range(2):
            low = 128 * (2 * pair + q)
            spare[1, 3136 * q : 3136 * q + 3136] = send[:3136, low : low + 128].astype(F32)
        for spot in range(49):
            for q in range(2):
                low = 128 * (2 * pair + q)
                w4[64 * spot : 64 * spot + 64, low : low + 128] = spare[
                    1, pl.ds(3136 * q + spot, 64, stride=49), :
                ].astype(BF16)
    build_picks(send)
    bias[...] = jnp.zeros_like(bias)
    for at, (ref, size, copies) in enumerate(((b1_ref, 32, 20), (b2_ref, 64, 9), (b3_ref, 64, 7))):
        repeat = onehot((iota((size, size * copies), 1) & (size - 1)) == iota((size, size * copies), 0), F32)
        bias[at : at + 1, : size * copies] = dot(ref[...], repeat, precision=HIGHEST)
    acc1[...] = jnp.zeros_like(acc1)
    acc2[...] = jnp.zeros_like(acc2)
    acc3[...] = jnp.zeros_like(acc3)
    bias_sums[...] = jnp.zeros_like(bias_sums)
    loss_sums[...] = jnp.zeros_like(loss_sums)
    pad3[...] = jnp.zeros_like(pad3)
    pad2[...] = jnp.zeros_like(pad2)
    a2[...] = jnp.zeros_like(a2)
    for step in range(steps):
        g1[step, 0] = jnp.zeros((SUB, 640), BF16)
        g1[step, 21] = jnp.zeros((SUB, 640), BF16)

    raw_flat = raw.reshape(2, TILES - 1, SUB * STACK, 128)

    def forward(step, slot, hooks=()):
        hooks = list(hooks)

        def hook():
            if hooks:
                hooks.pop(0)()

        rows = pl.ds(pl.multiple_of(step * SUB, SUB), SUB)
        own = cols[rows, :]
        for kind in range(8):
            bands = list(range(kind, 21, 8))
            for at, band in enumerate(bands):
                low = BAND * band // 128
                for c in range(STACK):
                    place_at = (at * STACK + c) * SUB
                    for t in range(4):
                        if low + t < TILES - 1:
                            piece = raw_flat[slot, low + t, pl.ds(c, SUB, stride=STACK), :]
                        else:
                            piece = edge[pl.ds(pl.multiple_of(step * SUB, SUB), SUB), c, :]
                            piece = jnp.concatenate([piece, jnp.zeros((SUB, 128 - piece.shape[1]), F32)], axis=1)
                        lines[place_at : place_at + SUB, 128 * t : 128 * t + 128] = piece.astype(BF16)
            count = len(bands) * STACK * SUB
            sorted_lines = dot(lines[:count], send[512 * kind : 512 * kind + 512, :WIDE]).astype(BF16)
            for at, band in enumerate(bands):
                for c in range(STACK):
                    place_at = (at * STACK + c) * SUB
                    for group in range(3):
                        x[band, :, 512 * group + 128 * c : 512 * group + 128 * c + 128] = sorted_lines[
                            place_at : place_at + SUB, 128 * group : 128 * group + 128
                        ]
        hook()
        for group, lanes in enumerate((224, 224, 192)):
            part = tall(x[:, :, 512 * group : 512 * group + 512])
            joined = jnp.concatenate([part[: 20 * SUB], part[SUB:]], axis=1)
            acc[: 20 * SUB, 224 * group : 224 * group + lanes] = dot(joined, k1[:, :lanes])
        hook()
        for y in range(20):
            act, slope = silu_and_slope(acc[y * SUB : (y + 1) * SUB, :640] + bias[0:1, :640])
            a1[y % 2, y // 2] = act
            s1[y % 2, y // 2] = slope
        hook()
        for group in range(3):
            even, odd = (tall(a1[p, :, :, 192 * group : 192 * group + 256]) for p in range(2))
            joined = jnp.concatenate([even[: 9 * SUB], odd[: 9 * SUB], even[SUB:], odd[SUB:]], axis=1)
            acc[: 9 * SUB, 192 * group : 192 * group + 192] = dot(joined, k2[...])
        for y in range(9):
            act, slope = silu_and_slope(acc[y * SUB : (y + 1) * SUB, :576] + bias[1:2, :576])
            a2[y, :, :576] = act
            s2[y] = slope
        hook()
        for pair in range(4):
            low = 128 * pair
            joined = jnp.concatenate([tall(a2[ky : ky + 7, :, low : low + 256]) for ky in range(3)], axis=1)
            acc[: 7 * SUB, low : low + 128] = dot(joined, k3[...])
        hook()
        pre4 = b4[...]
        for y in range(7):
            act, slope = silu_and_slope(acc[y * SUB : (y + 1) * SUB, :448] + bias[2:3, :448])
            a3[y, rows, :] = act
            s3[y] = slope
            pre4 = pre4 + dot(act, w4[448 * y : 448 * y + 448])
        act, slope = silu_and_slope(pre4)
        a4[rows, :] = act
        logits = dot(act, w5[...], NT) + b5[...]
        picked = jnp.where(lane_action[...] == own[:, 3:4], logits, 0.0)
        high = picked.astype(BF16)
        rest = picked - high.astype(F32)
        middle = rest.astype(BF16)
        low_part = (rest - middle.astype(F32)).astype(BF16)
        thrice = dot(jnp.concatenate([high, middle, low_part], axis=0), compact[...], NT)
        chosen = thrice[:SUB] + thrice[SUB : 2 * SUB] + thrice[2 * SUB :]
        real = iota((SUB, 128), 1) < ATOMS
        shifted = chosen - jnp.max(jnp.where(real, chosen, -jnp.inf), axis=1, keepdims=True)
        exps = jnp.where(real, jnp.exp(shifted), 0.0)
        sums = jnp.sum(exps, axis=1, keepdims=True)
        probs_all[step] = exps / sums
        logp[...] = jnp.where(real, shifted - jnp.log(sums), 0.0)
        return slope

    def probs_copy(step):
        return remote(probs_all.at[step], nexts.at[step], probs_send.at[step], probs_recv.at[step], other_role)

    def grad_copy(step, half):
        spot = g1.at[step, pl.ds(1 + 10 * half, 10)]
        return remote(spot, spot, g1_send.at[2 * step + half], g1_recv.at[2 * step + half], other_role)

    def grad_start(step):
        for half in range(2):
            grad_copy(step, half).start()

    def backward(step):
        rows = pl.ds(pl.multiple_of(step * SUB, SUB), SUB)
        own = cols[rows, :]
        nodes = iota((SUB, 128), 1).astype(F32)
        reward, discount, importance = own[:, 0:1], own[:, 1:2], own[:, 2:3]
        support = -10.0 + 20.0 / (ATOMS - 1) * nodes
        spot = (jnp.clip(reward + discount * support, -10.0, 10.0) + 10.0) * ((ATOMS - 1) / 20.0)
        next_probs = nexts[step]
        projected = jnp.zeros((SUB, 128), F32)
        for j in range(ATOMS):
            projected += next_probs[:, j : j + 1] * jnp.maximum(0.0, 1.0 - jnp.abs(spot[:, j : j + 1] - nodes))
        projected = jnp.where(nodes < ATOMS, projected, 0.0)
        mass = jnp.sum(projected, axis=1, keepdims=True)
        row_loss = -jnp.sum(projected * logp[...], axis=1, keepdims=True)
        high = (row_loss * onehot(own[:, 5:6] == iota((SUB, plan.loss_rows), 1).astype(F32), F32)).astype(BF16)
        low = onehot(own[:, 6:7] == iota((SUB, 512), 1).astype(F32), BF16)
        loss_sums[...] += dot(high, low, TN)
        scaled = importance / totals[plan.bits, 0:1, 0:1]
        delta = (scaled * (probs_all[step] * mass - projected)).astype(BF16)
        spread = dot(delta, compact[...])
        delta_full = jnp.where(lane_action[...] == own[:, 4:5], spread, 0.0).astype(BF16)
        delta_all[rows, :] = delta_full
        grad4 = (dot(delta_full, w5[...]) * slope4[...]).astype(BF16)
        g4[rows, :] = grad4
        for y in range(7):
            pad3[y + 2, :, :448] = (dot(grad4, w4[448 * y : 448 * y + 448], NT) * s3[y]).astype(BF16)
        for pair in range(4):
            low = 128 * pair
            joined = jnp.concatenate([tall(pad3[2 - ky : 11 - ky, :, low : low + 128]) for ky in range(3)], axis=1)
            total = dot(joined, k3_wide[...], NT)
            if pair == 0:
                acc[: 9 * SUB, :256] = total
            else:
                acc[: 9 * SUB, low : low + 128] += total[:, :128]
                acc[: 9 * SUB, low + 128 : low + 256] = total[:, 128:]
        for y in range(9):
            pad2[y + 1] = (acc[y * SUB : (y + 1) * SUB, :576] * s2[y]).astype(BF16)
        for parity in range(2):
            for group in range(3):
                low = 192 * group
                part = tall(pad2[:, :, low : low + 192])
                total = dot(part[SUB:], k2[256 * parity : 256 * parity + 256], NT) + dot(
                    part[: 10 * SUB], k2[256 * parity + 512 : 256 * parity + 768], NT
                )
                if group == 0:
                    acc[: 10 * SUB, :256] = total
                else:
                    acc[: 10 * SUB, low : low + 64] += total[:, :64]
                    acc[: 10 * SUB, low + 64 : low + 256] = total[:, 64:]
            for m in range(10):
                g1[step, 2 * m + parity + 1] = (acc[m * SUB : (m + 1) * SUB, :640] * s1[parity, m]).astype(BF16)

    kept = ((x, x_kept), (a1, a1_kept), (a2, a2_kept), (pad2, pad2_kept), (pad3, pad3_kept))

    def keep_copies(step, low, high):
        return [pltpu.make_async_copy(kept[i][0], kept[i][1].at[step], keep_sem.at[i]) for i in range(low, high)]

    def back_copies(step, low, high):
        return [pltpu.make_async_copy(kept[i][1].at[step], kept[i][0], back_sem.at[i]) for i in range(low, high)]

    early = max(steps - 3, 0)

    def prefetch(step, slot):
        @pl.when(step < steps)
        def _():
            for c in raw_copies(step, slot):
                c.start()

    def raw_wait(step, slot):
        for c in raw_copies(step, slot):
            c.wait()

    def after_forward(step):
        @pl.when(role == 1)
        def _():
            probs_copy(step).start()

        @pl.when(online & (step + 1 < steps))
        def _():
            for c in keep_copies(step, 0, 3):
                c.start()

    total_step(1)
    raw_wait(0, 0)
    prefetch(1, 1)
    slope4[...] = forward(0, 0, [functools.partial(total_step, 2), lambda: None, functools.partial(total_step, 3)])
    for stage in range(4, plan.bits + 1):
        total_step(stage)
    after_forward(0)

    def one_step(step, _):
        @pl.when(online)
        def _():
            @pl.when(step > 0)
            def _():
                for c in keep_copies(step - 1, 3, 5):
                    c.wait()

            probs_copy(step).wait_recv()
            backward(step)

            @pl.when(step < early)
            def _():
                grad_start(step)

            @pl.when(step + 1 < steps)
            def _():
                for c in keep_copies(step, 3, 5):
                    c.start()

        @pl.when(step + 1 < steps)
        def _():
            following_step = step + 1
            slot = following_step % 2
            raw_wait(following_step, slot)
            prefetch(following_step + 1, 1 - slot)

            @pl.when(online)
            def _():
                for c in keep_copies(step, 0, 3):
                    c.wait()

            slope4[...] = forward(following_step, slot)
            after_forward(following_step)

        return 0

    lax.fori_loop(0, steps, one_step, 0)

    for stage in range(plan.bits):
        total_copy(stage).wait_send()

    def late_layers(step):
        total = None
        for group in range(3):
            low = 192 * group
            even, odd = (tall(a1[p, :, :, low : low + 256]) for p in range(2))
            joined = jnp.concatenate([even[: 9 * SUB], odd[: 9 * SUB], even[SUB:], odd[SUB:]], axis=1)
            term = dot(tall(pad2[1:10, :, low : low + 192]), joined, TN)
            total = term if total is None else total + term
        acc2[...] += total
        total = None
        for pair in range(4):
            low = 128 * pair
            joined = jnp.concatenate([tall(a2[ky : ky + 7, :, low : low + 256]) for ky in range(3)], axis=1)
            term = dot(tall(pad3[2:9, :, low : low + 128]), joined, TN)
            total = term if total is None else total + term
        acc3[...] += total
        for at, (count, lanes) in enumerate(((20, 640), (9, 576), (7, 448))):
            part = jnp.zeros((8, lanes), F32)
            for y in range(count):
                piece = (g1[step, y + 1] if at == 0 else pad2[y + 1] if at == 1 else pad3[y + 2, :, :448]).astype(F32)
                for q in range(SUB // 8):
                    part += piece[8 * q : 8 * q + 8]
            bias_sums[at, :, :lanes] += part

    def first_layer(step):
        for group in range(3):
            lanes = 192 if group == 2 else 224
            part = tall(g1[step, 1:21, :, 224 * group : 224 * group + lanes])
            pixels = tall(x[:, :, 512 * group : 512 * group + 512])
            joined = jnp.concatenate([pixels[: 20 * SUB], pixels[SUB:]], axis=1)
            acc1[:lanes] += dot(part, joined, TN)

    def weight_step(turn, step):
        @pl.when(turn > 0)
        def _():
            for c in back_copies(step, 1, 5):
                c.wait()

        late_layers(step)

        @pl.when(turn + 1 < steps)
        def _():
            for c in back_copies(turn, 1, 5):
                c.start()

        @pl.when(turn > 0)
        def _():
            for c in back_copies(step, 0, 1):
                c.wait()

        first_layer(step)

        @pl.when(turn + 1 < steps)
        def _():
            for c in back_copies(turn, 0, 1):
                c.start()

    def dense_sums():
        flat = raw.reshape(2 * (TILES - 1) * SUB * STACK, 128)
        for y in range(7):
            block = dot(a3[y], g4[...], TN)
            for px in range(7):
                for q in range(4):
                    flat[pl.ds(3136 * q + 7 * y + px, 64, stride=49), :] = block[
                        64 * px : 64 * px + 64, 128 * q : 128 * q + 128
                    ]
        for q in range(4):
            send[:3136, 128 * q : 128 * q + 128] = flat[3136 * q : 3136 * q + 3136].astype(BF16)
        head = dot(delta_all[...], a4[...], TN)
        send[ROW_HEAD : ROW_HEAD + 912] = head[:912].astype(BF16)
        send[ROW_HEAD + 912 : ROW_HEAD + 928] = jnp.concatenate(
            [head[912:LOGITS], jnp.zeros((928 - LOGITS, 512), F32)], axis=0
        ).astype(BF16)
        send[ROW_HEAD + 928 : plan.rest] = jnp.zeros((plan.rest - ROW_HEAD - 928, 512), BF16)

    def other_sums():
        def put(low, value):
            send[plan.rest + low : plan.rest + low + value.shape[0]] = value.astype(BF16)

        folded = acc1[0:32]
        for px in range(1, 7):
            folded += pltpu.roll(acc1[32 * px : 32 * px + 32], 1024 - 4 * px, 1)
        column = iota((1024, 256), 1)
        goal = ((column >> 5) & 1) * 512 + (column >> 6) * 128 + ((column >> 3) & 3) * 32 + (column & 7)
        pick = onehot(iota((1024, 256), 0) == goal, F32)
        put(ROW_ONE, jnp.concatenate([dot(folded, pick, precision=HIGHEST), jnp.zeros((32, 256), F32)], axis=1))
        folded = acc2[0:64]
        for px in range(1, 3):
            folded += pltpu.roll(acc2[64 * px : 64 * px + 64], 1024 - 64 * px, 1)
        column = iota((1024, 512), 1)
        goal = ((column >> 2) & 3) * 256 + (column & 3) * 32 + (column >> 4)
        pick = onehot(iota((1024, 512), 0) == goal, F32)
        put(ROW_TWO, dot(folded, pick, precision=HIGHEST))
        folded = acc3[0:64] + pltpu.roll(acc3[64:128], 768 - 64, 1)
        row = iota((768, 576), 0)
        goal = (row & 63) * 9 + (row >> 8) * 3 + ((row >> 6) & 3)
        pick = onehot((iota((768, 576), 1) == goal) & (((row >> 6) & 3) < 3), F32)
        third = dot(folded, pick, precision=HIGHEST)
        put(ROW_THREE, third[:, :512])
        put(ROW_THREE_REST, jnp.concatenate([third[:, 512:], jnp.zeros((64, 448), F32)], axis=1))
        bias_rows = []
        for at, (size, copies) in enumerate(((32, 20), (64, 9), (64, 7))):
            fold = onehot((iota((size * copies, 512), 0) & (size - 1)) == iota((size * copies, 512), 1), F32)
            line = jnp.sum(bias_sums[at, :, : size * copies], axis=0, keepdims=True)
            bias_rows.append(dot(line, fold, precision=HIGHEST))
        bias_rows.append(jnp.sum(g4[...].astype(F32), axis=0, keepdims=True))
        head_bias = jnp.sum(delta_all[...].astype(F32), axis=0, keepdims=True)
        bias_rows.append(head_bias[:, :512])
        bias_rows.append(jnp.concatenate([head_bias[:, 512:], jnp.zeros((1, 1024 - LOGITS), F32)], axis=1))
        bias_rows.append(jnp.zeros((10, 512), F32))
        put(ROW_BIAS, jnp.concatenate(bias_rows, axis=0))
        put(ROW_LOSS, loss_sums[...])
        left = plan.rows - plan.rest - ROW_LOSS - plan.loss_rows
        if left:
            put(ROW_LOSS + plan.loss_rows, jnp.zeros((left, 512), F32))

    def stage_rows(stream, stage):
        base, size, order = plan.streams[stream]
        low = base
        for bit in order[:stage]:
            size //= 2
            low = low + bit_of(bit) * size
        return low, size

    def aligned(at):
        return pl.multiple_of(at, 16)

    def scatter_copy(stream, stage):
        base, size, order = plan.streams[stream]
        low, count = stage_rows(stream, stage)
        half = count // 2
        away = aligned(low + (1 - bit_of(order[stage])) * half)
        into = base + size - count
        index = stream * plan.bits + stage
        return remote(
            send.at[pl.ds(away, half)], landed.at[pl.ds(into, half)], rs_send.at[index], rs_recv.at[index],
            across(order[stage]),
        )

    def scatter_start(streams):
        for stream in streams:
            scatter_copy(stream, 0).start()

    def scatter_finish(stage, streams):
        for stream in streams:
            base, size, order = plan.streams[stream]
            scatter_copy(stream, stage).wait_recv()
            low, count = stage_rows(stream, stage)
            half = count // 2
            keep = aligned(low + bit_of(order[stage]) * half)
            into = base + size - count
            target = final if stage == plan.bits - 1 else send
            block = next(b for b in (128, 64, 32, 16) if half % b == 0)

            def add(i, _, keep=keep, into=into, target=target, block=block):
                at = aligned(keep + i * block)
                target[pl.ds(at, block)] = send[pl.ds(at, block)] + landed[pl.ds(aligned(into + i * block), block)]
                return 0

            lax.fori_loop(0, half // block, add, 0)
            if stage + 1 < plan.bits:
                scatter_copy(stream, stage + 1).start()
            else:
                over_copy(stream).start()
                gather_copy(stream, 0).start()

    def over_copy(stream):
        low, count = stage_rows(stream, plan.bits)
        spot = pl.ds(aligned(low), count)
        return remote(final.at[spot], final.at[spot], x_send.at[stream], x_recv.at[stream], other_role)

    def gather_copy(stream, stage):
        order = plan.streams[stream][2]
        low, count = stage_rows(stream, plan.bits - stage)
        spot = pl.ds(aligned(low), count)
        index = stream * plan.bits + stage
        return remote(
            final.at[spot], final.at[spot], ag_send.at[index], ag_recv.at[index], across(order[plan.bits - 1 - stage])
        )

    def over_finish(streams):
        for stream in streams:
            over_copy(stream).wait_recv()
            gather_copy(stream, 0).start()

    def gather_finish(stage, streams):
        for stream in streams:
            gather_copy(stream, stage).wait_recv()
            if stage + 1 < plan.bits:
                gather_copy(stream, stage + 1).start()

    tile_rows = raw.reshape(2 * (TILES - 1) * SUB * STACK, 128)

    tile_pairs = raw.reshape((TILES - 1) * SUB * STACK, 2, 128)

    def tile_copies(step):
        return [
            pltpu.make_async_copy(
                tile_pairs.at[pl.ds(t * SUB, SUB)],
                frame_out.at[pl.ds(step * SUB, SUB), :, pl.ds(128 * t, 128)],
                tile_sem,
            )
            for t in range(TILES)
        ]

    def frame_step(step):
        frame_products(g1.at[step], band_k, acc)

        @pl.when(step > 0)
        def _():
            for c in tile_copies(step - 1):
                c.wait()

        for c in range(2):
            for t in range(TILES):
                tile_rows[pl.ds(t * SUB * 2 + c, SUB, stride=2), :] = frame_tile(acc, c, t)
        for c in tile_copies(step):
            c.start()

    bits, first, second = plan.bits, plan.first, plan.second

    late_grads = [(step, half) for step in range(early, steps) for half in range(2)]
    issue = {"soon": late_grads[:-4], "mid": late_grads[-4:-2], "over": late_grads[-2:-1], "last": late_grads[-1:]}

    def grads_at(moment):
        for step, half in issue[moment]:
            grad_copy(step, half).start()

    def turn_at(number):
        return min(number, steps - 1)

    @pl.when(online)
    def _():
        dense_sums()
        scatter_start(first)

        def turns(turn, _):
            weight_step(turn, jnp.where(turn == 0, steps - 1, turn - 1))

            @pl.when(turn == 0)
            def _():
                scatter_finish(0, first)
                grads_at("soon")

            return 0

        lax.fori_loop(0, steps, turns, 0)
        scatter_finish(1, first)
        grads_at("mid")
        other_sums()
        scatter_start(second)
        build_frame(k1_ref[:, 0:128], band_k)

    @pl.when(role == 1)
    def _():
        kernel_copy.wait_recv()
        build_frame(k1_online[:, 128:256], band_k)

    def frame_and_more(step, _):
        @pl.when(role == 1)
        def _():
            for half in range(2):
                grad_copy(step, half).wait_recv()

        frame_step(step)

        @pl.when(online & (step == 0))
        def _():
            scatter_finish(0, second)

        @pl.when(online & (step == turn_at(1)))
        def _():
            scatter_finish(2, first)
            scatter_finish(1, second)

        @pl.when(online & (step == turn_at(2)))
        def _():
            for stage in range(3, bits):
                scatter_finish(stage, first)
            grads_at("over")
            scatter_finish(2, second)

        @pl.when(online & (step == turn_at(3)))
        def _():
            for stage in range(3, bits):
                scatter_finish(stage, second)
            grads_at("last")
            gather_finish(0, first)

        @pl.when(online & (step == turn_at(4)))
        def _():
            gather_finish(0, second)

        @pl.when((role == 1) & (step == max(steps - 3, 0)))
        def _():
            over_finish(first)
            gather_finish(0, first)
            over_finish(second)
            for stage in range(1, bits - 2):
                gather_finish(stage, first)
                gather_finish(stage - 1, second)

        @pl.when((role == 1) & (step == max(steps - 2, 0)))
        def _():
            gather_finish(bits - 2, first)
            gather_finish(bits - 3, second)
            gather_finish(bits - 2, second)

        @pl.when((role == 1) & (step == steps - 1))
        def _():
            gather_finish(bits - 1, first)
            gather_finish(bits - 1, second)

        return 0

    lax.fori_loop(0, steps, frame_and_more, 0)

    @pl.when(online)
    def _():
        for stage in range(1, bits):
            gather_finish(stage, first)
            gather_finish(stage, second)

    out_copies = [
        pltpu.make_async_copy(final.at[pl.ds(0, ROW_HEAD)], dense_out, out_sem.at[0]),
        pltpu.make_async_copy(final.at[pl.ds(ROW_HEAD, plan.rows - ROW_HEAD)], sums_out, out_sem.at[1]),
    ]
    for c in out_copies:
        c.start()

    for c in tile_copies(steps - 1):
        c.wait()
    for stream in range(len(plan.streams)):
        for stage in range(plan.bits):
            gather_copy(stream, stage).wait_send()

    @pl.when(online)
    def _():
        kernel_copy.wait_send()
        for stream in range(len(plan.streams)):
            over_copy(stream).wait_send()
            for stage in range(plan.bits):
                scatter_copy(stream, stage).wait_send()

        def sent(step, _):
            for half in range(2):
                grad_copy(step, half).wait_send()
            return 0

        lax.fori_loop(0, steps, sent, 0)

    @pl.when(role == 1)
    def _():
        def sent(step, _):
            probs_copy(step).wait_send()
            return 0

        lax.fori_loop(0, steps, sent, 0)

    for c in out_copies:
        c.wait()


def core(plan, frames, edge, weights, facts, tables):
    rows = frames.shape[1]
    steps = rows // SUB
    k1, k2, k3, w4, b1, b2, b3, b4, w5, b5 = weights
    vmem, hbm = pl.BlockSpec(memory_space=pltpu.VMEM), pl.BlockSpec(memory_space=pl.ANY)
    dma = pltpu.SemaphoreType.DMA
    streams = len(plan.streams)
    scratch = [
        pltpu.VMEM((2, TILES - 1, SUB, STACK, 128), F32),
        pltpu.VMEM((3 * STACK * SUB, 512), BF16),
        pltpu.VMEM((21, SUB, 1536), BF16),
        pltpu.VMEM((2, 10, SUB, 640), BF16),
        pltpu.VMEM((2, 10, SUB, 640), F32),
        pltpu.VMEM((9, SUB, 640), BF16),
        pltpu.VMEM((9, SUB, 576), F32),
        pltpu.VMEM((7, rows, 448), BF16),
        pltpu.VMEM((7, SUB, 448), F32),
        pltpu.VMEM((rows, 512), BF16),
        pltpu.VMEM((rows, 512), BF16),
        pltpu.VMEM((rows, LOGITS), BF16),
        pltpu.VMEM((steps, 22, SUB, 640), BF16),
        pltpu.VMEM((11, SUB, 576), BF16),
        pltpu.VMEM((11, SUB, 512), BF16),
        pltpu.VMEM((21 * SUB, 2 * WIDE), F32),
        pltpu.VMEM((2, 2 * WIDE, 640), BF16),
        pltpu.VMEM((1024, 224), BF16),
        pltpu.VMEM((1024, 192), BF16),
        pltpu.VMEM((768, 128), BF16),
        pltpu.VMEM((256, 384), BF16),
        pltpu.VMEM((3136, 512), BF16),
        pltpu.VMEM((8, 640), F32),
        pltpu.VMEM((224, 1024), F32),
        pltpu.VMEM((192, 1024), F32),
        pltpu.VMEM((128, 768), F32),
        pltpu.VMEM((3, 8, 640), F32),
        pltpu.VMEM((plan.loss_rows, 512), F32),
        pltpu.VMEM((plan.rows, 512), BF16),
        pltpu.VMEM((plan.rows, 512), BF16),
        pltpu.VMEM((plan.rows, 512), BF16),
        pltpu.VMEM((steps, SUB, 128), F32),
        pltpu.VMEM((SUB, 128), F32),
        pltpu.VMEM((steps, SUB, 128), F32),
        pltpu.VMEM((plan.bits + 1, 8, 128), F32),
        pltpu.VMEM((plan.bits, 8, 128), F32),
        pltpu.VMEM((32, 256), BF16),
        pltpu.VMEM((rows, 128), F32),
        pltpu.VMEM((SUB, 512), F32),
        dma((5,)), dma((5,)), dma((2,)), dma, dma, dma((steps,)), dma((steps,)), dma((2 * steps,)), dma((2 * steps,)),
        dma((plan.bits,)), dma((plan.bits,)), dma, dma,
        dma((streams * plan.bits,)), dma((streams * plan.bits,)), dma((streams * plan.bits,)), dma((streams * plan.bits,)),
        dma((streams,)), dma((streams,)), dma((2,)),
    ]
    return pl.pallas_call(
        functools.partial(core_kernel, plan, steps),
        in_specs=[hbm, vmem, vmem, vmem, vmem, hbm] + [vmem] * 14,
        out_specs=[hbm] * 8,
        out_shape=[
            jax.ShapeDtypeStruct((rows, 2, TILES * 128), F32),
            jax.ShapeDtypeStruct((ROW_HEAD, 512), BF16),
            jax.ShapeDtypeStruct((plan.rows - ROW_HEAD, 512), BF16),
            jax.ShapeDtypeStruct((steps - 1, 21, SUB, 1536), BF16),
            jax.ShapeDtypeStruct((steps - 1, 2, 10, SUB, 640), BF16),
            jax.ShapeDtypeStruct((steps - 1, 9, SUB, 640), BF16),
            jax.ShapeDtypeStruct((steps - 1, 11, SUB, 576), BF16),
            jax.ShapeDtypeStruct((steps - 1, 11, SUB, 512), BF16),
        ],
        scratch_shapes=scratch,
        compiler_params=pltpu.CompilerParams(vmem_limit_bytes=63 << 20, collective_id=0, has_side_effects=True),
        name="core",
    )(frames, edge, k1, k2, k3, w4, b1, b2, b3, b4, w5, b5, *facts, *tables)[:3]


def finish_kernel(plan, own, frames, dense, sums, frame_out, w4, k1, b1, k2, b2, k3, b3, b4, w5, b5, losses):
    frame_out[...] = frames[:, :, :PIX]
    w4[...] = dense[...].astype(F32)

    def part(low, high):
        return sums[plan.rest - ROW_HEAD + low : plan.rest - ROW_HEAD + high]

    @pl.when(pl.program_id(0) == 0)
    def _():
        w5[:912] = sums[:912].astype(F32)
        w5[912:] = sums[912:928].astype(F32)[: LOGITS - 912]
        k2[...] = part(ROW_TWO, ROW_THREE).astype(F32)
        k3[:, :512] = part(ROW_THREE, ROW_THREE_REST).astype(F32)
        k3[:, 512:] = part(ROW_THREE_REST, ROW_ONE)[:, :64].astype(F32)
        k1[...] = part(ROW_ONE, ROW_BIAS)[:, :256].astype(F32)
        rows = part(ROW_BIAS, ROW_LOSS).astype(F32)
        b1[...] = rows[0:1, :32]
        b2[...] = rows[1:2, :64]
        b3[...] = rows[2:3, :64]
        b4[...] = rows[3:4]
        b5[:, :512] = rows[4:5]
        b5[:, 512:] = rows[5:6, : LOGITS - 512]
        device = lax.axis_index("role") * plan.batch + lax.axis_index("batch")
        slot = device * own + iota((1, own), 1)
        chosen = dot(part(ROW_LOSS, ROW_LOSS + plan.loss_rows), onehot(iota((512, own), 0) == (slot & 511), BF16))
        mine = iota((plan.loss_rows, own), 0) == (slot >> 9)
        losses[...] = jnp.sum(jnp.where(mine, chosen, 0.0), axis=0, keepdims=True)


def finish(plan, own, frames, dense, sums):
    rows = frames.shape[0]
    small = ((32, 256), (1, 32), (64, 512), (1, 64), (64, 576), (1, 64), (1, 512), (LOGITS, 512), (1, LOGITS), (1, own))
    block, pieces = (56, 4) if rows % 56 == 0 else (16, 14)
    frame_at, dense_at = (lambda i: (i, 0, 0)), (lambda i: (jnp.minimum(i, pieces - 1), 0))
    return pl.pallas_call(
        functools.partial(finish_kernel, plan, own),
        grid=(rows // block,),
        in_specs=[
            pl.BlockSpec((block, 2, TILES * 128), frame_at),
            pl.BlockSpec((ROW_HEAD // pieces, 512), dense_at),
            pl.BlockSpec(sums.shape, lambda i: (0, 0)),
        ],
        out_specs=[
            pl.BlockSpec((block, 2, PIX), frame_at),
            pl.BlockSpec((ROW_HEAD // pieces, 512), dense_at),
            *[pl.BlockSpec(s, lambda i: (0, 0)) for s in small],
        ],
        out_shape=[jax.ShapeDtypeStruct(s, F32) for s in ((rows, 2, PIX), (ROW_HEAD, 512), *small)],
        compiler_params=pltpu.CompilerParams(vmem_limit_bytes=60 << 20),
        name="finish",
    )(frames, dense, sums)


def on_device(
    frames,
    conv1_weight,
    conv1_bias,
    conv2_weight,
    conv2_bias,
    conv3_weight,
    conv3_bias,
    dense_weight,
    dense_bias,
    head_weight,
    head_bias,
    taken_actions,
    next_actions,
    rewards,
    discounts,
    importance,
    buffer_slots,
):
    roles, batch = lax.axis_size("role"), lax.axis_size("batch")
    rows = frames.shape[1]
    slots = rows * batch
    plan = Plan(batch, slots)

    lane_action = jnp.asarray(np.arange(LOGITS)[None] // ATOMS, F32)
    compact = jnp.asarray(np.arange(128)[:, None] == np.arange(LOGITS)[None] % ATOMS, BF16)
    facts = [
        v.reshape(1, rows) for v in (taken_actions, next_actions, rewards, discounts, importance, buffer_slots)
    ]
    edge = frames[0, :, :, 128 * (TILES - 1) :]
    weights = (
        conv1_weight[0].T, conv2_weight[0].T, conv3_weight[0].T, dense_weight[0],
        conv1_bias, conv2_bias, conv3_bias, dense_bias, head_weight[0].T, head_bias,
    )
    partial = core(plan, frames, edge, weights, facts, (lane_action, compact))
    frame_part, w4, k1, b1, k2, b2, k3, b3, b4, w5, b5, priorities = finish(plan, slots // (roles * batch), *partial)
    return (frame_part, k1.T, b1[0], k2.T, b2[0], k3.T, b3[0], w4, b4[0], w5.T, b5[0], priorities[0])


def solution(mesh):
    in_specs = (
        P("role", "batch", None, None),
        P("role", None, None),
        P("role", None),
        P("role", None, None),
        P("role", None),
        P("role", None, None),
        P("role", None),
        P("role", None, None),
        P("role", None),
        P("role", None, None),
        P("role", None),
        P("batch"),
        P("batch"),
        P("batch"),
        P("batch"),
        P("batch"),
        P("batch"),
    )
    out_specs = (
        P("batch", "role", None),
        P(),
        P(),
        P(),
        P(),
        P(),
        P(),
        P(),
        P(),
        P(),
        P(),
        P(("role", "batch")),
    )
    return jax.shard_map(on_device, mesh=mesh, in_specs=in_specs, out_specs=out_specs, check_vma=False)
```

```python
import functools

import jax
import jax.numpy as jnp
import numpy as np
from jax import lax
from jax.experimental import pallas as pl
from jax.experimental.pallas import tpu as pltpu
from jax.sharding import PartitionSpec as P

STACK = 4
SIDE = 84
ACTIONS = 18
ATOMS = 51
LOGITS = ACTIONS * ATOMS
PIX = SIDE * SIDE
BAND = 4 * SIDE
WIDE = 384
TILES = 56
SUB = 32
F32 = jnp.float32
BF16 = jnp.bfloat16
HIGHEST = lax.Precision.HIGHEST
MESH = pl.DeviceIdType.MESH

NN = (((1,), (0,)), ((), ()))
NT = (((1,), (1,)), ((), ()))
TN = (((0,), (0,)), ((), ()))

ROW_HEAD = 3136
ROW_REST = 4096
ROW_TWO = 0
ROW_THREE = ROW_TWO + 64
ROW_THREE_REST = ROW_THREE + 64
ROW_ONE = ROW_THREE_REST + 64
ROW_BIAS = ROW_ONE + 32
ROW_LOSS = ROW_BIAS + 16


def dot(left, right, dims=NN, precision=None):
    return lax.dot_general(left, right, dims, precision=precision, preferred_element_type=F32)


def iota(shape, dim):
    return lax.broadcasted_iota(jnp.int32, shape, dim)


def onehot(condition, dtype):
    return jnp.where(condition, 1.0, 0.0).astype(dtype)


def silu_and_slope(pre):
    gate = 0.5 * jnp.tanh(0.5 * pre) + 0.5
    act = pre * gate
    return act.astype(BF16), gate + act * (1.0 - gate)


def tall(value):
    return value.reshape(value.shape[0] * value.shape[1], value.shape[2])


class Plan:
    def __init__(self, batch, slots):
        self.batch = batch
        self.bits = batch.bit_length() - 1
        if 1 << self.bits != batch:
            raise ValueError("batch axis")
        self.loss_rows = -(-slots // (512 * 16)) * 16
        unit = 16 * batch
        units = -(-ROW_REST // unit)
        self.rest = units * unit
        rest_units = -(-(ROW_LOSS + self.loss_rows) // unit)
        self.rows = (units + rest_units) * unit
        count = min(4, units)
        up = list(range(self.bits))
        round_way = up[:1] + up[2:] + up[1:2]
        self.streams, at = [], 0
        for s in range(count):
            size = (units // count + (1 if s < units % count else 0)) * unit
            self.streams.append((at, size, up if s % 2 == 0 else round_way))
            at += size
        self.first = list(range(count))
        self.second = [count]
        self.streams.append((at, rest_units * unit, up))


def banded_first(kernel_t, channel, line, column, real, channels, lanes):
    rows = channel.shape[0]
    spread = onehot((iota((lanes, 32), 0) & 31) == iota((lanes, 32), 1), BF16)
    tiled = dot(spread, kernel_t).astype(BF16)
    block, rest = column >> 2, column & 3
    lane_x = iota((rows, lanes), 1) >> 5
    found = []
    for half in range(2):
        parts = []
        for step in range(2):
            goal = jnp.where(real, channel * 64 + (4 * half + line) * 8 + 4 * step + rest, -1)
            pick = onehot(iota((rows, channels * 64), 1) == goal, BF16)
            parts.append(dot(pick, tiled, NT))
        found.append(jnp.where(lane_x == block, parts[0], jnp.where(lane_x == block - 1, parts[1], 0.0)).astype(BF16))
    return found


def build_first(kernel_t, out):
    row = iota((512, 1), 0)
    found = banded_first(kernel_t, row >> 7, (row >> 5) & 3, row & 31, row >= 0, STACK, 224)
    for half in range(2):
        out[512 * half : 512 * half + 512] = found[half]


def build_frame(kernel_t, out):
    row = iota((2 * WIDE, 1), 0)
    channel = (row >= WIDE).astype(jnp.int32)
    inner = row - channel * WIDE
    line = sum((inner >= SIDE * i).astype(jnp.int32) for i in range(1, 5))
    found = banded_first(kernel_t, channel, line, inner - line * SIDE, line < 4, 2, 640)
    for half in range(2):
        out[half] = found[half]


def build_second(kernel_t, out):
    goal = (iota((512, 512), 0) & 31) * 16 + (iota((512, 512), 0) >> 5)
    by_place = dot(onehot(iota((512, 512), 1) == goal, BF16), kernel_t, NT).astype(BF16)
    out[...] = jnp.zeros_like(out)
    for ky in range(4):
        for kx in range(4):
            piece = by_place[(ky * 4 + kx) * 32 : (ky * 4 + kx + 1) * 32]
            for x in range(3):
                low = 256 * ky + (2 * x + kx) * 32
                out[low : low + 32, 64 * x : 64 * x + 64] = piece


def build_third(kernel_t, tall_out, wide_out):
    goal = (iota((576, 576), 0) & 63) * 9 + (iota((576, 576), 0) >> 6)
    by_place = dot(onehot(iota((576, 576), 1) == goal, BF16), kernel_t, NT).astype(BF16)
    tall_out[...] = jnp.zeros_like(tall_out)
    wide_out[...] = jnp.zeros_like(wide_out)
    for ky in range(3):
        for kx in range(3):
            piece = by_place[(ky * 3 + kx) * 64 : (ky * 3 + kx + 1) * 64]
            for x in range(2):
                low = (x + kx) * 64
                tall_out[256 * ky + low : 256 * ky + low + 64, 64 * x : 64 * x + 64] = piece
                wide_out[low : low + 64, 128 * ky + 64 * x : 128 * ky + 64 * x + 64] = piece


def build_picks(out):
    lane = iota((1, WIDE), 1)
    group, line, column = lane >> 7, (lane >> 5) & 3, lane & 31
    goal = jnp.where(28 * group + column < SIDE, SIDE * line + 28 * group + column, -1000)
    row = iota((512, WIDE), 0)
    for kind in range(8):
        out[512 * kind : 512 * kind + 512, :WIDE] = onehot(row == goal + (BAND * kind) % 128, BF16)


def frame_products(grads, band_k, acc):
    acc[...] = dot(tall(grads[1:22]), band_k[0], NT) + dot(tall(grads[0:21]), band_k[1], NT)


def frame_tile(acc, c, t):
    pieces, at, end = [], 128 * t, min(128 * t + 128, PIX)
    while at < end:
        band, inner = divmod(at, BAND)
        size = min(end - at, BAND - inner)
        pieces.append(acc[band * SUB : (band + 1) * SUB, WIDE * c + inner : WIDE * c + inner + size])
        at += size
    if end < 128 * t + 128:
        pieces.append(jnp.zeros((SUB, 128 * t + 128 - end), F32))
    return pieces[0] if len(pieces) == 1 else jnp.concatenate(pieces, axis=1)


def core_kernel(plan, steps, *refs):
    (
        x_hbm, edge, k1_ref, k2_ref, k3_ref, w4_hbm, b1_ref, b2_ref, b3_ref, b4, w5, b5, taken, following, rewards, discounts,
        weighting, buffer_slots, lane_action, compact,
    ) = refs[:20]
    frame_out, dense_out, sums_out, x_kept, a1_kept, a2_kept, pad2_kept, pad3_kept = refs[20:28]
    (
        raw, lines, x, a1, s1, a2, s2, a3, s3, a4, g4, delta_all, g1, pad2, pad3, acc, band_k,
        k1, k2, k3, k3_wide, w4, bias, acc1, acc2, acc3, bias_sums, loss_sums, send, landed, final, probs_all, logp, nexts,
        totals, totals_in, k1_online, cols, slope4,
        keep_sem, back_sem, raw_sem, w4_sem, tile_sem, probs_send, probs_recv, g1_send, g1_recv, tot_send, tot_recv, k1_send, k1_recv,
        rs_send, rs_recv, ag_send, ag_recv, x_send, x_recv, out_sem,
    ) = refs[28:]
    role, place = lax.axis_index("role"), lax.axis_index("batch")
    online = role == 0

    def bit_of(bit):
        return (place // (1 << bit)) % 2

    def across(bit):
        return {"batch": place + (1 - 2 * bit_of(bit)) * (1 << bit)}

    other_role = {"role": 1 - role}

    def remote(src, dst, send_sem, recv_sem, device):
        return pltpu.make_async_remote_copy(
            src_ref=src, dst_ref=dst, send_sem=send_sem, recv_sem=recv_sem, device_id=device, device_id_type=MESH
        )

    def raw_copies(step, slot):
        return [
            pltpu.make_async_copy(
                x_hbm.at[0, pl.ds(step * SUB, SUB), :, pl.ds(128 * t, 128)], raw.at[slot, t], raw_sem.at[slot]
            )
            for t in range(TILES - 1)
        ]

    weight_copy = pltpu.make_async_copy(w4_hbm, send.at[pl.ds(0, 3136)], w4_sem)
    weight_copy.start()
    for c in raw_copies(0, 0):
        c.start()

    barrier = pltpu.get_barrier_semaphore()
    for bit in range(plan.bits):
        pl.semaphore_signal(barrier, inc=1, device_id=across(bit), device_id_type=MESH)
    pl.semaphore_signal(barrier, inc=1, device_id=other_role, device_id_type=MESH)

    slot_number = buffer_slots[...].astype(F32)
    slot_row = jnp.floor(slot_number * (1.0 / 512))
    taken_number = taken[...].astype(F32)
    facts = [
        rewards[...], discounts[...], weighting[...], jnp.where(online, taken_number, following[...].astype(F32)), taken_number,
        slot_row, slot_number - 512.0 * slot_row, rewards[...],
    ]
    cols[...] = dot(jnp.concatenate(facts, axis=0), onehot(iota((8, 128), 0) == iota((8, 128), 1), F32), TN, HIGHEST)
    totals[0] = jnp.broadcast_to(jnp.sum(weighting[...], axis=1, keepdims=True), (8, 128))

    def total_copy(stage):
        return remote(totals.at[stage], totals_in.at[stage], tot_send.at[stage], tot_recv.at[stage], across(stage))

    def total_step(stage):
        if stage > 0:
            total_copy(stage - 1).wait_recv()
            totals[stage] = totals[stage - 1] + totals_in[stage - 1]
        if stage < plan.bits:
            total_copy(stage).start()

    build_first(k1_ref[...], k1)
    build_second(k2_ref[...], k2)
    build_third(k3_ref[...], k3, k3_wide)

    kernel_copy = remote(k1_ref, k1_online, k1_send, k1_recv, other_role)

    pl.semaphore_wait(barrier, plan.bits + 1)
    total_step(0)

    @pl.when(online)
    def _():
        kernel_copy.start()

    weight_copy.wait()
    spare = raw.reshape(2, (TILES - 1) * SUB * STACK, 128)
    for pair in range(2):
        for q in range(2):
            low = 128 * (2 * pair + q)
            spare[1, 3136 * q : 3136 * q + 3136] = send[:3136, low : low + 128].astype(F32)
        for spot in range(49):
            for q in range(2):
                low = 128 * (2 * pair + q)
                w4[64 * spot : 64 * spot + 64, low : low + 128] = spare[
                    1, pl.ds(3136 * q + spot, 64, stride=49), :
                ].astype(BF16)
    build_picks(send)
    bias[...] = jnp.zeros_like(bias)
    for at, (ref, size, copies) in enumerate(((b1_ref, 32, 20), (b2_ref, 64, 9), (b3_ref, 64, 7))):
        repeat = onehot((iota((size, size * copies), 1) & (size - 1)) == iota((size, size * copies), 0), F32)
        bias[at : at + 1, : size * copies] = dot(ref[...], repeat, precision=HIGHEST)
    acc1[...] = jnp.zeros_like(acc1)
    acc2[...] = jnp.zeros_like(acc2)
    acc3[...] = jnp.zeros_like(acc3)
    bias_sums[...] = jnp.zeros_like(bias_sums)
    loss_sums[...] = jnp.zeros_like(loss_sums)
    pad3[...] = jnp.zeros_like(pad3)
    pad2[...] = jnp.zeros_like(pad2)
    a2[...] = jnp.zeros_like(a2)
    for step in range(steps):
        g1[step, 0] = jnp.zeros((SUB, 640), BF16)
        g1[step, 21] = jnp.zeros((SUB, 640), BF16)

    raw_flat = raw.reshape(2, TILES - 1, SUB * STACK, 128)

    def forward(step, slot, hooks=()):
        hooks = list(hooks)

        def hook():
            if hooks:
                hooks.pop(0)()

        rows = pl.ds(pl.multiple_of(step * SUB, SUB), SUB)
        own = cols[rows, :]
        for kind in range(8):
            bands = list(range(kind, 21, 8))
            for at, band in enumerate(bands):
                low = BAND * band // 128
                for c in range(STACK):
                    place_at = (at * STACK + c) * SUB
                    for t in range(4):
                        if low + t < TILES - 1:
                            piece = raw_flat[slot, low + t, pl.ds(c, SUB, stride=STACK), :]
                        else:
                            piece = edge[pl.ds(pl.multiple_of(step * SUB, SUB), SUB), c, :]
                            piece = jnp.concatenate([piece, jnp.zeros((SUB, 128 - piece.shape[1]), F32)], axis=1)
                        lines[place_at : place_at + SUB, 128 * t : 128 * t + 128] = piece.astype(BF16)
            count = len(bands) * STACK * SUB
            sorted_lines = dot(lines[:count], send[512 * kind : 512 * kind + 512, :WIDE]).astype(BF16)
            for at, band in enumerate(bands):
                for c in range(STACK):
                    place_at = (at * STACK + c) * SUB
                    for group in range(3):
                        x[band, :, 512 * group + 128 * c : 512 * group + 128 * c + 128] = sorted_lines[
                            place_at : place_at + SUB, 128 * group : 128 * group + 128
                        ]
        hook()
        for group, lanes in enumerate((224, 224, 192)):
            part = tall(x[:, :, 512 * group : 512 * group + 512])
            joined = jnp.concatenate([part[: 20 * SUB], part[SUB:]], axis=1)
            acc[: 20 * SUB, 224 * group : 224 * group + lanes] = dot(joined, k1[:, :lanes])
        hook()
        for y in range(20):
            act, slope = silu_and_slope(acc[y * SUB : (y + 1) * SUB, :640] + bias[0:1, :640])
            a1[y % 2, y // 2] = act
            s1[y % 2, y // 2] = slope
        hook()
        for group in range(3):
            even, odd = (tall(a1[p, :, :, 192 * group : 192 * group + 256]) for p in range(2))
            joined = jnp.concatenate([even[: 9 * SUB], odd[: 9 * SUB], even[SUB:], odd[SUB:]], axis=1)
            acc[: 9 * SUB, 192 * group : 192 * group + 192] = dot(joined, k2[...])
        for y in range(9):
            act, slope = silu_and_slope(acc[y * SUB : (y + 1) * SUB, :576] + bias[1:2, :576])
            a2[y, :, :576] = act
            s2[y] = slope
        hook()
        for pair in range(4):
            low = 128 * pair
            joined = jnp.concatenate([tall(a2[ky : ky + 7, :, low : low + 256]) for ky in range(3)], axis=1)
            acc[: 7 * SUB, low : low + 128] = dot(joined, k3[...])
        hook()
        pre4 = b4[...]
        for y in range(7):
            act, slope = silu_and_slope(acc[y * SUB : (y + 1) * SUB, :448] + bias[2:3, :448])
            a3[y, rows, :] = act
            s3[y] = slope
            pre4 = pre4 + dot(act, w4[448 * y : 448 * y + 448])
        act, slope = silu_and_slope(pre4)
        a4[rows, :] = act
        logits = dot(act, w5[...], NT) + b5[...]
        picked = jnp.where(lane_action[...] == own[:, 3:4], logits, 0.0)
        high = picked.astype(BF16)
        rest = picked - high.astype(F32)
        middle = rest.astype(BF16)
        low_part = (rest - middle.astype(F32)).astype(BF16)
        thrice = dot(jnp.concatenate([high, middle, low_part], axis=0), compact[...], NT)
        chosen = thrice[:SUB] + thrice[SUB : 2 * SUB] + thrice[2 * SUB :]
        real = iota((SUB, 128), 1) < ATOMS
        shifted = chosen - jnp.max(jnp.where(real, chosen, -jnp.inf), axis=1, keepdims=True)
        exps = jnp.where(real, jnp.exp(shifted), 0.0)
        sums = jnp.sum(exps, axis=1, keepdims=True)
        probs_all[step] = exps / sums
        logp[...] = jnp.where(real, shifted - jnp.log(sums), 0.0)
        return slope

    def probs_copy(step):
        return remote(probs_all.at[step], nexts.at[step], probs_send.at[step], probs_recv.at[step], other_role)

    def grad_copy(step, half):
        spot = g1.at[step, pl.ds(1 + 10 * half, 10)]
        return remote(spot, spot, g1_send.at[2 * step + half], g1_recv.at[2 * step + half], other_role)

    def grad_start(step):
        for half in range(2):
            grad_copy(step, half).start()

    def backward(step):
        rows = pl.ds(pl.multiple_of(step * SUB, SUB), SUB)
        own = cols[rows, :]
        nodes = iota((SUB, 128), 1).astype(F32)
        reward, discount, importance = own[:, 0:1], own[:, 1:2], own[:, 2:3]
        support = -10.0 + 20.0 / (ATOMS - 1) * nodes
        spot = (jnp.clip(reward + discount * support, -10.0, 10.0) + 10.0) * ((ATOMS - 1) / 20.0)
        next_probs = nexts[step]
        projected = jnp.zeros((SUB, 128), F32)
        for j in range(ATOMS):
            projected += next_probs[:, j : j + 1] * jnp.maximum(0.0, 1.0 - jnp.abs(spot[:, j : j + 1] - nodes))
        projected = jnp.where(nodes < ATOMS, projected, 0.0)
        mass = jnp.sum(projected, axis=1, keepdims=True)
        row_loss = -jnp.sum(projected * logp[...], axis=1, keepdims=True)
        high = (row_loss * onehot(own[:, 5:6] == iota((SUB, plan.loss_rows), 1).astype(F32), F32)).astype(BF16)
        low = onehot(own[:, 6:7] == iota((SUB, 512), 1).astype(F32), BF16)
        loss_sums[...] += dot(high, low, TN)
        scaled = importance / totals[plan.bits, 0:1, 0:1]
        delta = (scaled * (probs_all[step] * mass - projected)).astype(BF16)
        spread = dot(delta, compact[...])
        delta_full = jnp.where(lane_action[...] == own[:, 4:5], spread, 0.0).astype(BF16)
        delta_all[rows, :] = delta_full
        grad4 = (dot(delta_full, w5[...]) * slope4[...]).astype(BF16)
        g4[rows, :] = grad4
        for y in range(7):
            pad3[y + 2, :, :448] = (dot(grad4, w4[448 * y : 448 * y + 448], NT) * s3[y]).astype(BF16)
        for pair in range(4):
            low = 128 * pair
            joined = jnp.concatenate([tall(pad3[2 - ky : 11 - ky, :, low : low + 128]) for ky in range(3)], axis=1)
            total = dot(joined, k3_wide[...], NT)
            if pair == 0:
                acc[: 9 * SUB, :256] = total
            else:
                acc[: 9 * SUB, low : low + 128] += total[:, :128]
                acc[: 9 * SUB, low + 128 : low + 256] = total[:, 128:]
        for y in range(9):
            pad2[y + 1] = (acc[y * SUB : (y + 1) * SUB, :576] * s2[y]).astype(BF16)
        for parity in range(2):
            for group in range(3):
                low = 192 * group
                part = tall(pad2[:, :, low : low + 192])
                total = dot(part[SUB:], k2[256 * parity : 256 * parity + 256], NT) + dot(
                    part[: 10 * SUB], k2[256 * parity + 512 : 256 * parity + 768], NT
                )
                if group == 0:
                    acc[: 10 * SUB, :256] = total
                else:
                    acc[: 10 * SUB, low : low + 64] += total[:, :64]
                    acc[: 10 * SUB, low + 64 : low + 256] = total[:, 64:]
            for m in range(10):
                g1[step, 2 * m + parity + 1] = (acc[m * SUB : (m + 1) * SUB, :640] * s1[parity, m]).astype(BF16)

    kept = ((x, x_kept), (a1, a1_kept), (a2, a2_kept), (pad2, pad2_kept), (pad3, pad3_kept))

    def keep_copies(step, low, high):
        return [pltpu.make_async_copy(kept[i][0], kept[i][1].at[step], keep_sem.at[i]) for i in range(low, high)]

    def back_copies(step, low, high):
        return [pltpu.make_async_copy(kept[i][1].at[step], kept[i][0], back_sem.at[i]) for i in range(low, high)]

    early = max(steps - 3, 0)

    def prefetch(step, slot):
        @pl.when(step < steps)
        def _():
            for c in raw_copies(step, slot):
                c.start()

    def raw_wait(step, slot):
        for c in raw_copies(step, slot):
            c.wait()

    def after_forward(step):
        @pl.when(role == 1)
        def _():
            probs_copy(step).start()

        @pl.when(online & (step + 1 < steps))
        def _():
            for c in keep_copies(step, 0, 3):
                c.start()

    total_step(1)
    raw_wait(0, 0)
    prefetch(1, 1)
    slope4[...] = forward(0, 0, [functools.partial(total_step, 2), lambda: None, functools.partial(total_step, 3)])
    for stage in range(4, plan.bits + 1):
        total_step(stage)
    after_forward(0)

    def one_step(step, _):
        @pl.when(online)
        def _():
            @pl.when(step > 0)
            def _():
                for c in keep_copies(step - 1, 3, 5):
                    c.wait()

            probs_copy(step).wait_recv()
            backward(step)

            @pl.when(step < early)
            def _():
                grad_start(step)

            @pl.when(step + 1 < steps)
            def _():
                for c in keep_copies(step, 3, 5):
                    c.start()

        @pl.when(step + 1 < steps)
        def _():
            following_step = step + 1
            slot = following_step % 2
            raw_wait(following_step, slot)
            prefetch(following_step + 1, 1 - slot)

            @pl.when(online)
            def _():
                for c in keep_copies(step, 0, 3):
                    c.wait()

            slope4[...] = forward(following_step, slot)
            after_forward(following_step)

        return 0

    lax.fori_loop(0, steps, one_step, 0)

    for stage in range(plan.bits):
        total_copy(stage).wait_send()

    def late_layers(step):
        total = None
        for group in range(3):
            low = 192 * group
            even, odd = (tall(a1[p, :, :, low : low + 256]) for p in range(2))
            joined = jnp.concatenate([even[: 9 * SUB], odd[: 9 * SUB], even[SUB:], odd[SUB:]], axis=1)
            term = dot(tall(pad2[1:10, :, low : low + 192]), joined, TN)
            total = term if total is None else total + term
        acc2[...] += total
        total = None
        for pair in range(4):
            low = 128 * pair
            joined = jnp.concatenate([tall(a2[ky : ky + 7, :, low : low + 256]) for ky in range(3)], axis=1)
            term = dot(tall(pad3[2:9, :, low : low + 128]), joined, TN)
            total = term if total is None else total + term
        acc3[...] += total
        for at, (count, lanes) in enumerate(((20, 640), (9, 576), (7, 448))):
            part = jnp.zeros((8, lanes), F32)
            for y in range(count):
                piece = (g1[step, y + 1] if at == 0 else pad2[y + 1] if at == 1 else pad3[y + 2, :, :448]).astype(F32)
                for q in range(SUB // 8):
                    part += piece[8 * q : 8 * q + 8]
            bias_sums[at, :, :lanes] += part

    def first_layer(step):
        for group in range(3):
            lanes = 192 if group == 2 else 224
            part = tall(g1[step, 1:21, :, 224 * group : 224 * group + lanes])
            pixels = tall(x[:, :, 512 * group : 512 * group + 512])
            joined = jnp.concatenate([pixels[: 20 * SUB], pixels[SUB:]], axis=1)
            acc1[:lanes] += dot(part, joined, TN)

    def weight_step(turn, step):
        @pl.when(turn > 0)
        def _():
            for c in back_copies(step, 1, 5):
                c.wait()

        late_layers(step)

        @pl.when(turn + 1 < steps)
        def _():
            for c in back_copies(turn, 1, 5):
                c.start()

        @pl.when(turn > 0)
        def _():
            for c in back_copies(step, 0, 1):
                c.wait()

        first_layer(step)

        @pl.when(turn + 1 < steps)
        def _():
            for c in back_copies(turn, 0, 1):
                c.start()

    def dense_sums():
        flat = raw.reshape(2 * (TILES - 1) * SUB * STACK, 128)
        for y in range(7):
            block = dot(a3[y], g4[...], TN)
            for px in range(7):
                for q in range(4):
                    flat[pl.ds(3136 * q + 7 * y + px, 64, stride=49), :] = block[
                        64 * px : 64 * px + 64, 128 * q : 128 * q + 128
                    ]
        for q in range(4):
            send[:3136, 128 * q : 128 * q + 128] = flat[3136 * q : 3136 * q + 3136].astype(BF16)
        head = dot(delta_all[...], a4[...], TN)
        send[ROW_HEAD : ROW_HEAD + 912] = head[:912].astype(BF16)
        send[ROW_HEAD + 912 : ROW_HEAD + 928] = jnp.concatenate(
            [head[912:LOGITS], jnp.zeros((928 - LOGITS, 512), F32)], axis=0
        ).astype(BF16)
        send[ROW_HEAD + 928 : plan.rest] = jnp.zeros((plan.rest - ROW_HEAD - 928, 512), BF16)

    def other_sums():
        def put(low, value):
            send[plan.rest + low : plan.rest + low + value.shape[0]] = value.astype(BF16)

        folded = acc1[0:32]
        for px in range(1, 7):
            folded += pltpu.roll(acc1[32 * px : 32 * px + 32], 1024 - 4 * px, 1)
        column = iota((1024, 256), 1)
        goal = ((column >> 5) & 1) * 512 + (column >> 6) * 128 + ((column >> 3) & 3) * 32 + (column & 7)
        pick = onehot(iota((1024, 256), 0) == goal, F32)
        put(ROW_ONE, jnp.concatenate([dot(folded, pick, precision=HIGHEST), jnp.zeros((32, 256), F32)], axis=1))
        folded = acc2[0:64]
        for px in range(1, 3):
            folded += pltpu.roll(acc2[64 * px : 64 * px + 64], 1024 - 64 * px, 1)
        column = iota((1024, 512), 1)
        goal = ((column >> 2) & 3) * 256 + (column & 3) * 32 + (column >> 4)
        pick = onehot(iota((1024, 512), 0) == goal, F32)
        put(ROW_TWO, dot(folded, pick, precision=HIGHEST))
        folded = acc3[0:64] + pltpu.roll(acc3[64:128], 768 - 64, 1)
        row = iota((768, 576), 0)
        goal = (row & 63) * 9 + (row >> 8) * 3 + ((row >> 6) & 3)
        pick = onehot((iota((768, 576), 1) == goal) & (((row >> 6) & 3) < 3), F32)
        third = dot(folded, pick, precision=HIGHEST)
        put(ROW_THREE, third[:, :512])
        put(ROW_THREE_REST, jnp.concatenate([third[:, 512:], jnp.zeros((64, 448), F32)], axis=1))
        bias_rows = []
        for at, (size, copies) in enumerate(((32, 20), (64, 9), (64, 7))):
            fold = onehot((iota((size * copies, 512), 0) & (size - 1)) == iota((size * copies, 512), 1), F32)
            line = jnp.sum(bias_sums[at, :, : size * copies], axis=0, keepdims=True)
            bias_rows.append(dot(line, fold, precision=HIGHEST))
        bias_rows.append(jnp.sum(g4[...].astype(F32), axis=0, keepdims=True))
        head_bias = jnp.sum(delta_all[...].astype(F32), axis=0, keepdims=True)
        bias_rows.append(head_bias[:, :512])
        bias_rows.append(jnp.concatenate([head_bias[:, 512:], jnp.zeros((1, 1024 - LOGITS), F32)], axis=1))
        bias_rows.append(jnp.zeros((10, 512), F32))
        put(ROW_BIAS, jnp.concatenate(bias_rows, axis=0))
        put(ROW_LOSS, loss_sums[...])
        left = plan.rows - plan.rest - ROW_LOSS - plan.loss_rows
        if left:
            put(ROW_LOSS + plan.loss_rows, jnp.zeros((left, 512), F32))

    def stage_rows(stream, stage):
        base, size, order = plan.streams[stream]
        low = base
        for bit in order[:stage]:
            size //= 2
            low = low + bit_of(bit) * size
        return low, size

    def aligned(at):
        return pl.multiple_of(at, 16)

    def scatter_copy(stream, stage):
        base, size, order = plan.streams[stream]
        low, count = stage_rows(stream, stage)
        half = count // 2
        away = aligned(low + (1 - bit_of(order[stage])) * half)
        into = base + size - count
        index = stream * plan.bits + stage
        return remote(
            send.at[pl.ds(away, half)], landed.at[pl.ds(into, half)], rs_send.at[index], rs_recv.at[index],
            across(order[stage]),
        )

    def scatter_start(streams):
        for stream in streams:
            scatter_copy(stream, 0).start()

    def scatter_finish(stage, streams):
        for stream in streams:
            base, size, order = plan.streams[stream]
            scatter_copy(stream, stage).wait_recv()
            low, count = stage_rows(stream, stage)
            half = count // 2
            keep = aligned(low + bit_of(order[stage]) * half)
            into = base + size - count
            target = final if stage == plan.bits - 1 else send
            block = next(b for b in (128, 64, 32, 16) if half % b == 0)

            def add(i, _, keep=keep, into=into, target=target, block=block):
                at = aligned(keep + i * block)
                target[pl.ds(at, block)] = send[pl.ds(at, block)] + landed[pl.ds(aligned(into + i * block), block)]
                return 0

            lax.fori_loop(0, half // block, add, 0)
            if stage + 1 < plan.bits:
                scatter_copy(stream, stage + 1).start()
            else:
                over_copy(stream).start()
                gather_copy(stream, 0).start()

    def over_copy(stream):
        low, count = stage_rows(stream, plan.bits)
        spot = pl.ds(aligned(low), count)
        return remote(final.at[spot], final.at[spot], x_send.at[stream], x_recv.at[stream], other_role)

    def gather_copy(stream, stage):
        order = plan.streams[stream][2]
        low, count = stage_rows(stream, plan.bits - stage)
        spot = pl.ds(aligned(low), count)
        index = stream * plan.bits + stage
        return remote(
            final.at[spot], final.at[spot], ag_send.at[index], ag_recv.at[index], across(order[plan.bits - 1 - stage])
        )

    def over_finish(streams):
        for stream in streams:
            over_copy(stream).wait_recv()
            gather_copy(stream, 0).start()

    def gather_finish(stage, streams):
        for stream in streams:
            gather_copy(stream, stage).wait_recv()
            if stage + 1 < plan.bits:
                gather_copy(stream, stage + 1).start()

    tile_rows = raw.reshape(2 * (TILES - 1) * SUB * STACK, 128)

    tile_pairs = raw.reshape((TILES - 1) * SUB * STACK, 2, 128)

    def tile_copies(step):
        return [
            pltpu.make_async_copy(
                tile_pairs.at[pl.ds(t * SUB, SUB)],
                frame_out.at[pl.ds(step * SUB, SUB), :, pl.ds(128 * t, 128)],
                tile_sem,
            )
            for t in range(TILES)
        ]

    def frame_step(step):
        frame_products(g1.at[step], band_k, acc)

        @pl.when(step > 0)
        def _():
            for c in tile_copies(step - 1):
                c.wait()

        for c in range(2):
            for t in range(TILES):
                tile_rows[pl.ds(t * SUB * 2 + c, SUB, stride=2), :] = frame_tile(acc, c, t)
        for c in tile_copies(step):
            c.start()

    bits, first, second = plan.bits, plan.first, plan.second

    late_grads = [(step, half) for step in range(early, steps) for half in range(2)]
    issue = {"soon": late_grads[:-4], "mid": late_grads[-4:-3], "over": late_grads[-3:-2], "last": late_grads[-2:]}

    def grads_at(moment):
        for step, half in issue[moment]:
            grad_copy(step, half).start()

    def turn_at(number):
        return min(number, steps - 1)

    @pl.when(online)
    def _():
        dense_sums()
        scatter_start(first)

        def turns(turn, _):
            weight_step(turn, jnp.where(turn == 0, steps - 1, turn - 1))

            @pl.when(turn == turn_at(1))
            def _():
                scatter_finish(0, first)
                grads_at("soon")

            return 0

        lax.fori_loop(0, steps, turns, 0)
        scatter_finish(1, first)
        grads_at("mid")
        other_sums()
        scatter_start(second)
        build_frame(k1_ref[:, 0:128], band_k)

    @pl.when(role == 1)
    def _():
        kernel_copy.wait_recv()
        build_frame(k1_online[:, 128:256], band_k)

    def frame_and_more(step, _):
        @pl.when(role == 1)
        def _():
            for half in range(2):
                grad_copy(step, half).wait_recv()

        frame_step(step)

        @pl.when(online & (step == 0))
        def _():
            scatter_finish(0, second)
            scatter_finish(2, first)

        @pl.when(online & (step == turn_at(1)))
        def _():
            scatter_finish(1, second)

        @pl.when(online & (step == turn_at(2)))
        def _():
            for stage in range(3, bits):
                scatter_finish(stage, first)
            grads_at("over")
            scatter_finish(2, second)

        @pl.when(online & (step == turn_at(3)))
        def _():
            for stage in range(3, bits):
                scatter_finish(stage, second)
            grads_at("last")

        @pl.when(online & (step == turn_at(5)))
        def _():
            gather_finish(0, first)
            gather_finish(0, second)

        @pl.when((role == 1) & (step == max(steps - 3, 0)))
        def _():
            over_finish(first)
            gather_finish(0, first)
            over_finish(second)
            for stage in range(1, bits - 2):
                gather_finish(stage, first)
                gather_finish(stage - 1, second)

        @pl.when((role == 1) & (step == max(steps - 2, 0)))
        def _():
            gather_finish(bits - 2, first)
            gather_finish(bits - 3, second)
            gather_finish(bits - 2, second)

        @pl.when((role == 1) & (step == steps - 1))
        def _():
            gather_finish(bits - 1, first)
            gather_finish(bits - 1, second)

        return 0

    lax.fori_loop(0, steps, frame_and_more, 0)

    @pl.when(online)
    def _():
        for stage in range(1, bits):
            gather_finish(stage, first)
            gather_finish(stage, second)

    out_copies = [
        pltpu.make_async_copy(final.at[pl.ds(0, ROW_HEAD)], dense_out, out_sem.at[0]),
        pltpu.make_async_copy(final.at[pl.ds(ROW_HEAD, plan.rows - ROW_HEAD)], sums_out, out_sem.at[1]),
    ]
    for c in out_copies:
        c.start()

    for c in tile_copies(steps - 1):
        c.wait()
    for stream in range(len(plan.streams)):
        for stage in range(plan.bits):
            gather_copy(stream, stage).wait_send()

    @pl.when(online)
    def _():
        kernel_copy.wait_send()
        for stream in range(len(plan.streams)):
            over_copy(stream).wait_send()
            for stage in range(plan.bits):
                scatter_copy(stream, stage).wait_send()

        def sent(step, _):
            for half in range(2):
                grad_copy(step, half).wait_send()
            return 0

        lax.fori_loop(0, steps, sent, 0)

    @pl.when(role == 1)
    def _():
        def sent(step, _):
            probs_copy(step).wait_send()
            return 0

        lax.fori_loop(0, steps, sent, 0)

    for c in out_copies:
        c.wait()


def core(plan, frames, edge, weights, facts, tables):
    rows = frames.shape[1]
    steps = rows // SUB
    k1, k2, k3, w4, b1, b2, b3, b4, w5, b5 = weights
    vmem, hbm = pl.BlockSpec(memory_space=pltpu.VMEM), pl.BlockSpec(memory_space=pl.ANY)
    dma = pltpu.SemaphoreType.DMA
    streams = len(plan.streams)
    scratch = [
        pltpu.VMEM((2, TILES - 1, SUB, STACK, 128), F32),
        pltpu.VMEM((3 * STACK * SUB, 512), BF16),
        pltpu.VMEM((21, SUB, 1536), BF16),
        pltpu.VMEM((2, 10, SUB, 640), BF16),
        pltpu.VMEM((2, 10, SUB, 640), F32),
        pltpu.VMEM((9, SUB, 640), BF16),
        pltpu.VMEM((9, SUB, 576), F32),
        pltpu.VMEM((7, rows, 448), BF16),
        pltpu.VMEM((7, SUB, 448), F32),
        pltpu.VMEM((rows, 512), BF16),
        pltpu.VMEM((rows, 512), BF16),
        pltpu.VMEM((rows, LOGITS), BF16),
        pltpu.VMEM((steps, 22, SUB, 640), BF16),
        pltpu.VMEM((11, SUB, 576), BF16),
        pltpu.VMEM((11, SUB, 512), BF16),
        pltpu.VMEM((21 * SUB, 2 * WIDE), F32),
        pltpu.VMEM((2, 2 * WIDE, 640), BF16),
        pltpu.VMEM((1024, 224), BF16),
        pltpu.VMEM((1024, 192), BF16),
        pltpu.VMEM((768, 128), BF16),
        pltpu.VMEM((256, 384), BF16),
        pltpu.VMEM((3136, 512), BF16),
        pltpu.VMEM((8, 640), F32),
        pltpu.VMEM((224, 1024), F32),
        pltpu.VMEM((192, 1024), F32),
        pltpu.VMEM((128, 768), F32),
        pltpu.VMEM((3, 8, 640), F32),
        pltpu.VMEM((plan.loss_rows, 512), F32),
        pltpu.VMEM((plan.rows, 512), BF16),
        pltpu.VMEM((plan.rows, 512), BF16),
        pltpu.VMEM((plan.rows, 512), BF16),
        pltpu.VMEM((steps, SUB, 128), F32),
        pltpu.VMEM((SUB, 128), F32),
        pltpu.VMEM((steps, SUB, 128), F32),
        pltpu.VMEM((plan.bits + 1, 8, 128), F32),
        pltpu.VMEM((plan.bits, 8, 128), F32),
        pltpu.VMEM((32, 256), BF16),
        pltpu.VMEM((rows, 128), F32),
        pltpu.VMEM((SUB, 512), F32),
        dma((5,)), dma((5,)), dma((2,)), dma, dma, dma((steps,)), dma((steps,)), dma((2 * steps,)), dma((2 * steps,)),
        dma((plan.bits,)), dma((plan.bits,)), dma, dma,
        dma((streams * plan.bits,)), dma((streams * plan.bits,)), dma((streams * plan.bits,)), dma((streams * plan.bits,)),
        dma((streams,)), dma((streams,)), dma((2,)),
    ]
    return pl.pallas_call(
        functools.partial(core_kernel, plan, steps),
        in_specs=[hbm, vmem, vmem, vmem, vmem, hbm] + [vmem] * 14,
        out_specs=[hbm] * 8,
        out_shape=[
            jax.ShapeDtypeStruct((rows, 2, TILES * 128), F32),
            jax.ShapeDtypeStruct((ROW_HEAD, 512), BF16),
            jax.ShapeDtypeStruct((plan.rows - ROW_HEAD, 512), BF16),
            jax.ShapeDtypeStruct((steps - 1, 21, SUB, 1536), BF16),
            jax.ShapeDtypeStruct((steps - 1, 2, 10, SUB, 640), BF16),
            jax.ShapeDtypeStruct((steps - 1, 9, SUB, 640), BF16),
            jax.ShapeDtypeStruct((steps - 1, 11, SUB, 576), BF16),
            jax.ShapeDtypeStruct((steps - 1, 11, SUB, 512), BF16),
        ],
        scratch_shapes=scratch,
        compiler_params=pltpu.CompilerParams(vmem_limit_bytes=63 << 20, collective_id=0, has_side_effects=True),
        name="core",
    )(frames, edge, k1, k2, k3, w4, b1, b2, b3, b4, w5, b5, *facts, *tables)[:3]


def finish_kernel(plan, own, frames, dense, sums, frame_out, w4, k1, b1, k2, b2, k3, b3, b4, w5, b5, losses):
    frame_out[...] = frames[:, :, :PIX]
    w4[...] = dense[...].astype(F32)

    def part(low, high):
        return sums[plan.rest - ROW_HEAD + low : plan.rest - ROW_HEAD + high]

    @pl.when(pl.program_id(0) == 0)
    def _():
        w5[:912] = sums[:912].astype(F32)
        w5[912:] = sums[912:928].astype(F32)[: LOGITS - 912]
        k2[...] = part(ROW_TWO, ROW_THREE).astype(F32)
        k3[:, :512] = part(ROW_THREE, ROW_THREE_REST).astype(F32)
        k3[:, 512:] = part(ROW_THREE_REST, ROW_ONE)[:, :64].astype(F32)
        k1[...] = part(ROW_ONE, ROW_BIAS)[:, :256].astype(F32)
        rows = part(ROW_BIAS, ROW_LOSS).astype(F32)
        b1[...] = rows[0:1, :32]
        b2[...] = rows[1:2, :64]
        b3[...] = rows[2:3, :64]
        b4[...] = rows[3:4]
        b5[:, :512] = rows[4:5]
        b5[:, 512:] = rows[5:6, : LOGITS - 512]
        device = lax.axis_index("role") * plan.batch + lax.axis_index("batch")
        slot = device * own + iota((1, own), 1)
        chosen = dot(part(ROW_LOSS, ROW_LOSS + plan.loss_rows), onehot(iota((512, own), 0) == (slot & 511), BF16))
        mine = iota((plan.loss_rows, own), 0) == (slot >> 9)
        losses[...] = jnp.sum(jnp.where(mine, chosen, 0.0), axis=0, keepdims=True)


def finish(plan, own, frames, dense, sums):
    rows = frames.shape[0]
    small = ((32, 256), (1, 32), (64, 512), (1, 64), (64, 576), (1, 64), (1, 512), (LOGITS, 512), (1, LOGITS), (1, own))
    block, pieces = (56, 4) if rows % 56 == 0 else (16, 14)
    frame_at, dense_at = (lambda i: (i, 0, 0)), (lambda i: (jnp.minimum(i, pieces - 1), 0))
    return pl.pallas_call(
        functools.partial(finish_kernel, plan, own),
        grid=(rows // block,),
        in_specs=[
            pl.BlockSpec((block, 2, TILES * 128), frame_at),
            pl.BlockSpec((ROW_HEAD // pieces, 512), dense_at),
            pl.BlockSpec(sums.shape, lambda i: (0, 0)),
        ],
        out_specs=[
            pl.BlockSpec((block, 2, PIX), frame_at),
            pl.BlockSpec((ROW_HEAD // pieces, 512), dense_at),
            *[pl.BlockSpec(s, lambda i: (0, 0)) for s in small],
        ],
        out_shape=[jax.ShapeDtypeStruct(s, F32) for s in ((rows, 2, PIX), (ROW_HEAD, 512), *small)],
        compiler_params=pltpu.CompilerParams(vmem_limit_bytes=60 << 20),
        name="finish",
    )(frames, dense, sums)


def on_device(
    frames,
    conv1_weight,
    conv1_bias,
    conv2_weight,
    conv2_bias,
    conv3_weight,
    conv3_bias,
    dense_weight,
    dense_bias,
    head_weight,
    head_bias,
    taken_actions,
    next_actions,
    rewards,
    discounts,
    importance,
    buffer_slots,
):
    roles, batch = lax.axis_size("role"), lax.axis_size("batch")
    rows = frames.shape[1]
    slots = rows * batch
    plan = Plan(batch, slots)

    lane_action = jnp.asarray(np.arange(LOGITS)[None] // ATOMS, F32)
    compact = jnp.asarray(np.arange(128)[:, None] == np.arange(LOGITS)[None] % ATOMS, BF16)
    facts = [
        v.reshape(1, rows) for v in (taken_actions, next_actions, rewards, discounts, importance, buffer_slots)
    ]
    edge = frames[0, :, :, 128 * (TILES - 1) :]
    weights = (
        conv1_weight[0].T, conv2_weight[0].T, conv3_weight[0].T, dense_weight[0],
        conv1_bias, conv2_bias, conv3_bias, dense_bias, head_weight[0].T, head_bias,
    )
    partial = core(plan, frames, edge, weights, facts, (lane_action, compact))
    frame_part, w4, k1, b1, k2, b2, k3, b3, b4, w5, b5, priorities = finish(plan, slots // (roles * batch), *partial)
    return (frame_part, k1.T, b1[0], k2.T, b2[0], k3.T, b3[0], w4, b4[0], w5.T, b5[0], priorities[0])


def solution(mesh):
    in_specs = (
        P("role", "batch", None, None),
        P("role", None, None),
        P("role", None),
        P("role", None, None),
        P("role", None),
        P("role", None, None),
        P("role", None),
        P("role", None, None),
        P("role", None),
        P("role", None, None),
        P("role", None),
        P("batch"),
        P("batch"),
        P("batch"),
        P("batch"),
        P("batch"),
        P("batch"),
    )
    out_specs = (
        P("batch", "role", None),
        P(),
        P(),
        P(),
        P(),
        P(),
        P(),
        P(),
        P(),
        P(),
        P(),
        P(("role", "batch")),
    )
    return jax.shard_map(on_device, mesh=mesh, in_specs=in_specs, out_specs=out_specs, check_vma=False)
```

```python
import functools

import jax
import jax.numpy as jnp
import numpy as np
from jax import lax
from jax.experimental import pallas as pl
from jax.experimental.pallas import tpu as pltpu
from jax.sharding import PartitionSpec as P

STACK = 4
SIDE = 84
ACTIONS = 18
ATOMS = 51
LOGITS = ACTIONS * ATOMS
PIX = SIDE * SIDE
BAND = 4 * SIDE
WIDE = 384
TILES = 56
SUB = 32
F32 = jnp.float32
BF16 = jnp.bfloat16
HIGHEST = lax.Precision.HIGHEST
MESH = pl.DeviceIdType.MESH

NN = (((1,), (0,)), ((), ()))
NT = (((1,), (1,)), ((), ()))
TN = (((0,), (0,)), ((), ()))

ROW_HEAD = 3136
ROW_REST = 4096
ROW_TWO = 0
ROW_THREE = ROW_TWO + 64
ROW_THREE_REST = ROW_THREE + 64
ROW_ONE = ROW_THREE_REST + 64
ROW_BIAS = ROW_ONE + 32
ROW_LOSS = ROW_BIAS + 16


def dot(left, right, dims=NN, precision=None):
    return lax.dot_general(left, right, dims, precision=precision, preferred_element_type=F32)


def iota(shape, dim):
    return lax.broadcasted_iota(jnp.int32, shape, dim)


def onehot(condition, dtype):
    return jnp.where(condition, 1.0, 0.0).astype(dtype)


def silu_and_slope(pre):
    gate = 0.5 * jnp.tanh(0.5 * pre) + 0.5
    act = pre * gate
    return act.astype(BF16), gate + act * (1.0 - gate)


def tall(value):
    return value.reshape(value.shape[0] * value.shape[1], value.shape[2])


class Plan:
    def __init__(self, batch, slots):
        self.batch = batch
        self.bits = batch.bit_length() - 1
        if 1 << self.bits != batch:
            raise ValueError("batch axis")
        self.loss_rows = -(-slots // (512 * 16)) * 16
        unit = 16 * batch
        units = -(-ROW_REST // unit)
        self.rest = units * unit
        rest_units = -(-(ROW_LOSS + self.loss_rows) // unit)
        self.rows = (units + rest_units) * unit
        count = min(4, units)
        up = list(range(self.bits))
        round_way = up[:1] + up[2:] + up[1:2]
        self.streams, at = [], 0
        for s in range(count):
            size = (units // count + (1 if s < units % count else 0)) * unit
            self.streams.append((at, size, up if s % 2 == 0 else round_way))
            at += size
        self.first = list(range(count))
        self.second = [count]
        self.streams.append((at, rest_units * unit, up))


def banded_first(kernel_t, channel, line, column, real, channels, lanes):
    rows = channel.shape[0]
    spread = onehot((iota((lanes, 32), 0) & 31) == iota((lanes, 32), 1), BF16)
    tiled = dot(spread, kernel_t).astype(BF16)
    block, rest = column >> 2, column & 3
    lane_x = iota((rows, lanes), 1) >> 5
    found = []
    for half in range(2):
        parts = []
        for step in range(2):
            goal = jnp.where(real, channel * 64 + (4 * half + line) * 8 + 4 * step + rest, -1)
            pick = onehot(iota((rows, channels * 64), 1) == goal, BF16)
            parts.append(dot(pick, tiled, NT))
        found.append(jnp.where(lane_x == block, parts[0], jnp.where(lane_x == block - 1, parts[1], 0.0)).astype(BF16))
    return found


def build_first(kernel_t, out):
    row = iota((512, 1), 0)
    found = banded_first(kernel_t, row >> 7, (row >> 5) & 3, row & 31, row >= 0, STACK, 224)
    for half in range(2):
        out[512 * half : 512 * half + 512] = found[half]


def build_frame(kernel_t, out):
    row = iota((2 * WIDE, 1), 0)
    channel = (row >= WIDE).astype(jnp.int32)
    inner = row - channel * WIDE
    line = sum((inner >= SIDE * i).astype(jnp.int32) for i in range(1, 5))
    found = banded_first(kernel_t, channel, line, inner - line * SIDE, line < 4, 2, 640)
    for half in range(2):
        out[half] = found[half]


def build_second(kernel_t, out):
    goal = (iota((512, 512), 0) & 31) * 16 + (iota((512, 512), 0) >> 5)
    by_place = dot(onehot(iota((512, 512), 1) == goal, BF16), kernel_t, NT).astype(BF16)
    out[...] = jnp.zeros_like(out)
    for ky in range(4):
        for kx in range(4):
            piece = by_place[(ky * 4 + kx) * 32 : (ky * 4 + kx + 1) * 32]
            for x in range(3):
                low = 256 * ky + (2 * x + kx) * 32
                out[low : low + 32, 64 * x : 64 * x + 64] = piece


def build_third(kernel_t, tall_out, wide_out):
    goal = (iota((576, 576), 0) & 63) * 9 + (iota((576, 576), 0) >> 6)
    by_place = dot(onehot(iota((576, 576), 1) == goal, BF16), kernel_t, NT).astype(BF16)
    tall_out[...] = jnp.zeros_like(tall_out)
    wide_out[...] = jnp.zeros_like(wide_out)
    for ky in range(3):
        for kx in range(3):
            piece = by_place[(ky * 3 + kx) * 64 : (ky * 3 + kx + 1) * 64]
            for x in range(2):
                low = (x + kx) * 64
                tall_out[256 * ky + low : 256 * ky + low + 64, 64 * x : 64 * x + 64] = piece
                wide_out[low : low + 64, 128 * ky + 64 * x : 128 * ky + 64 * x + 64] = piece


def build_picks(out):
    lane = iota((1, WIDE), 1)
    group, line, column = lane >> 7, (lane >> 5) & 3, lane & 31
    goal = jnp.where(28 * group + column < SIDE, SIDE * line + 28 * group + column, -1000)
    row = iota((512, WIDE), 0)
    for kind in range(8):
        out[512 * kind : 512 * kind + 512, :WIDE] = onehot(row == goal + (BAND * kind) % 128, BF16)


def frame_products(grads, band_k, acc):
    acc[...] = dot(tall(grads[1:22]), band_k[0], NT) + dot(tall(grads[0:21]), band_k[1], NT)


def frame_tile(acc, c, t):
    pieces, at, end = [], 128 * t, min(128 * t + 128, PIX)
    while at < end:
        band, inner = divmod(at, BAND)
        size = min(end - at, BAND - inner)
        pieces.append(acc[band * SUB : (band + 1) * SUB, WIDE * c + inner : WIDE * c + inner + size])
        at += size
    if end < 128 * t + 128:
        pieces.append(jnp.zeros((SUB, 128 * t + 128 - end), F32))
    return pieces[0] if len(pieces) == 1 else jnp.concatenate(pieces, axis=1)


def core_kernel(plan, steps, *refs):
    (
        x_hbm, edge, k1_ref, k2_ref, k3_ref, w4_hbm, b1_ref, b2_ref, b3_ref, b4, w5, b5, taken, following, rewards, discounts,
        weighting, buffer_slots, lane_action, compact,
    ) = refs[:20]
    frame_out, dense_out, sums_out, x_kept, a1_kept, a2_kept, pad2_kept, pad3_kept = refs[20:28]
    (
        raw, lines, x, a1, s1, a2, s2, a3, s3, a4, g4, delta_all, g1, pad2, pad3, acc, band_k,
        k1, k2, k3, k3_wide, w4, bias, acc1, acc2, acc3, bias_sums, loss_sums, send, landed, final, probs_all, logp, nexts,
        totals, totals_in, k1_online, cols, slope4,
        keep_sem, back_sem, raw_sem, w4_sem, tile_sem, probs_send, probs_recv, g1_send, g1_recv, tot_send, tot_recv, k1_send, k1_recv,
        rs_send, rs_recv, ag_send, ag_recv, x_send, x_recv, out_sem,
    ) = refs[28:]
    role, place = lax.axis_index("role"), lax.axis_index("batch")
    online = role == 0

    def bit_of(bit):
        return (place // (1 << bit)) % 2

    def across(bit):
        return {"batch": place + (1 - 2 * bit_of(bit)) * (1 << bit)}

    other_role = {"role": 1 - role}

    def remote(src, dst, send_sem, recv_sem, device):
        return pltpu.make_async_remote_copy(
            src_ref=src, dst_ref=dst, send_sem=send_sem, recv_sem=recv_sem, device_id=device, device_id_type=MESH
        )

    def raw_copies(step, slot):
        return [
            pltpu.make_async_copy(
                x_hbm.at[0, pl.ds(step * SUB, SUB), :, pl.ds(128 * t, 128)], raw.at[slot, t], raw_sem.at[slot]
            )
            for t in range(TILES - 1)
        ]

    weight_copy = pltpu.make_async_copy(w4_hbm, send.at[pl.ds(0, 3136)], w4_sem)
    weight_copy.start()
    for c in raw_copies(0, 0):
        c.start()

    barrier = pltpu.get_barrier_semaphore()
    for bit in range(plan.bits):
        pl.semaphore_signal(barrier, inc=1, device_id=across(bit), device_id_type=MESH)
    pl.semaphore_signal(barrier, inc=1, device_id=other_role, device_id_type=MESH)

    slot_number = buffer_slots[...].astype(F32)
    slot_row = jnp.floor(slot_number * (1.0 / 512))
    taken_number = taken[...].astype(F32)
    facts = [
        rewards[...], discounts[...], weighting[...], jnp.where(online, taken_number, following[...].astype(F32)), taken_number,
        slot_row, slot_number - 512.0 * slot_row, rewards[...],
    ]
    cols[...] = dot(jnp.concatenate(facts, axis=0), onehot(iota((8, 128), 0) == iota((8, 128), 1), F32), TN, HIGHEST)
    totals[0] = jnp.broadcast_to(jnp.sum(weighting[...], axis=1, keepdims=True), (8, 128))

    def total_copy(stage):
        return remote(totals.at[stage], totals_in.at[stage], tot_send.at[stage], tot_recv.at[stage], across(stage))

    def total_step(stage):
        if stage > 0:
            total_copy(stage - 1).wait_recv()
            totals[stage] = totals[stage - 1] + totals_in[stage - 1]
        if stage < plan.bits:
            total_copy(stage).start()

    build_first(k1_ref[...], k1)
    build_second(k2_ref[...], k2)
    build_third(k3_ref[...], k3, k3_wide)

    kernel_copy = remote(k1_ref, k1_online, k1_send, k1_recv, other_role)

    pl.semaphore_wait(barrier, plan.bits + 1)
    total_step(0)

    @pl.when(online)
    def _():
        kernel_copy.start()

    weight_copy.wait()
    spare = raw.reshape(2, (TILES - 1) * SUB * STACK, 128)
    for pair in range(2):
        for q in range(2):
            low = 128 * (2 * pair + q)
            spare[1, 3136 * q : 3136 * q + 3136] = send[:3136, low : low + 128].astype(F32)
        for spot in range(49):
            for q in range(2):
                low = 128 * (2 * pair + q)
                w4[64 * spot : 64 * spot + 64, low : low + 128] = spare[
                    1, pl.ds(3136 * q + spot, 64, stride=49), :
                ].astype(BF16)
    build_picks(send)
    bias[...] = jnp.zeros_like(bias)
    for at, (ref, size, copies) in enumerate(((b1_ref, 32, 20), (b2_ref, 64, 9), (b3_ref, 64, 7))):
        repeat = onehot((iota((size, size * copies), 1) & (size - 1)) == iota((size, size * copies), 0), F32)
        bias[at : at + 1, : size * copies] = dot(ref[...], repeat, precision=HIGHEST)
    acc1[...] = jnp.zeros_like(acc1)
    acc2[...] = jnp.zeros_like(acc2)
    acc3[...] = jnp.zeros_like(acc3)
    bias_sums[...] = jnp.zeros_like(bias_sums)
    loss_sums[...] = jnp.zeros_like(loss_sums)
    pad3[...] = jnp.zeros_like(pad3)
    pad2[...] = jnp.zeros_like(pad2)
    a2[...] = jnp.zeros_like(a2)
    for step in range(steps):
        g1[step, 0] = jnp.zeros((SUB, 640), BF16)
        g1[step, 21] = jnp.zeros((SUB, 640), BF16)

    raw_flat = raw.reshape(2, TILES - 1, SUB * STACK, 128)

    def forward(step, slot, hooks=()):
        hooks = list(hooks)

        def hook():
            if hooks:
                hooks.pop(0)()

        rows = pl.ds(pl.multiple_of(step * SUB, SUB), SUB)
        own = cols[rows, :]
        for kind in range(8):
            bands = list(range(kind, 21, 8))
            width = 384 if (BAND * kind) % 128 + BAND <= 384 else 512
            for at, band in enumerate(bands):
                low = BAND * band // 128
                for c in range(STACK):
                    place_at = (at * STACK + c) * SUB
                    for t in range(width // 128):
                        if low + t < TILES - 1:
                            piece = raw_flat[slot, low + t, pl.ds(c, SUB, stride=STACK), :]
                        else:
                            piece = edge[pl.ds(pl.multiple_of(step * SUB, SUB), SUB), c, :]
                            piece = jnp.concatenate([piece, jnp.zeros((SUB, 128 - piece.shape[1]), F32)], axis=1)
                        lines[place_at : place_at + SUB, 128 * t : 128 * t + 128] = piece.astype(BF16)
            count = len(bands) * STACK * SUB
            sorted_lines = dot(lines[:count, :width], send[512 * kind : 512 * kind + width, :WIDE]).astype(BF16)
            for at, band in enumerate(bands):
                for c in range(STACK):
                    place_at = (at * STACK + c) * SUB
                    for group in range(3):
                        x[band, :, 512 * group + 128 * c : 512 * group + 128 * c + 128] = sorted_lines[
                            place_at : place_at + SUB, 128 * group : 128 * group + 128
                        ]
        hook()
        for group, lanes in enumerate((224, 224, 192)):
            part = tall(x[:, :, 512 * group : 512 * group + 512])
            joined = jnp.concatenate([part[: 20 * SUB], part[SUB:]], axis=1)
            acc[: 20 * SUB, 224 * group : 224 * group + lanes] = dot(joined, k1[:, :lanes])
        hook()
        for y in range(20):
            act, slope = silu_and_slope(acc[y * SUB : (y + 1) * SUB, :640] + bias[0:1, :640])
            a1[y % 2, y // 2] = act
            s1[y % 2, y // 2] = slope
        hook()
        for group in range(3):
            even, odd = (tall(a1[p, :, :, 192 * group : 192 * group + 256]) for p in range(2))
            joined = jnp.concatenate([even[: 9 * SUB], odd[: 9 * SUB], even[SUB:], odd[SUB:]], axis=1)
            acc[: 9 * SUB, 192 * group : 192 * group + 192] = dot(joined, k2[...])
        for y in range(9):
            act, slope = silu_and_slope(acc[y * SUB : (y + 1) * SUB, :576] + bias[1:2, :576])
            a2[y, :, :576] = act
            s2[y] = slope
        hook()
        for pair in range(4):
            low = 128 * pair
            joined = jnp.concatenate([tall(a2[ky : ky + 7, :, low : low + 256]) for ky in range(3)], axis=1)
            acc[: 7 * SUB, low : low + 128] = dot(joined, k3[...])
        hook()
        pre4 = b4[...]
        for y in range(7):
            act, slope = silu_and_slope(acc[y * SUB : (y + 1) * SUB, :448] + bias[2:3, :448])
            a3[y, rows, :] = act
            s3[y] = slope
            pre4 = pre4 + dot(act, w4[448 * y : 448 * y + 448])
        act, slope = silu_and_slope(pre4)
        a4[rows, :] = act
        logits = dot(act, w5[...], NT) + b5[...]
        picked = jnp.where(lane_action[...] == own[:, 3:4], logits, 0.0)
        high = picked.astype(BF16)
        rest = picked - high.astype(F32)
        middle = rest.astype(BF16)
        low_part = (rest - middle.astype(F32)).astype(BF16)
        thrice = dot(jnp.concatenate([high, middle, low_part], axis=0), compact[...], NT)
        chosen = thrice[:SUB] + thrice[SUB : 2 * SUB] + thrice[2 * SUB :]
        real = iota((SUB, 128), 1) < ATOMS
        shifted = chosen - jnp.max(jnp.where(real, chosen, -jnp.inf), axis=1, keepdims=True)
        exps = jnp.where(real, jnp.exp(shifted), 0.0)
        sums = jnp.sum(exps, axis=1, keepdims=True)
        probs_all[step] = exps / sums
        logp[...] = jnp.where(real, shifted - jnp.log(sums), 0.0)
        return slope

    def probs_copy(step):
        return remote(probs_all.at[step], nexts.at[step], probs_send.at[step], probs_recv.at[step], other_role)

    def grad_copy(step, half):
        spot = g1.at[step, pl.ds(1 + 10 * half, 10)]
        return remote(spot, spot, g1_send.at[2 * step + half], g1_recv.at[2 * step + half], other_role)

    def grad_start(step):
        for half in range(2):
            grad_copy(step, half).start()

    def backward(step):
        rows = pl.ds(pl.multiple_of(step * SUB, SUB), SUB)
        own = cols[rows, :]
        nodes = iota((SUB, 128), 1).astype(F32)
        reward, discount, importance = own[:, 0:1], own[:, 1:2], own[:, 2:3]
        support = -10.0 + 20.0 / (ATOMS - 1) * nodes
        spot = (jnp.clip(reward + discount * support, -10.0, 10.0) + 10.0) * ((ATOMS - 1) / 20.0)
        next_probs = nexts[step]
        projected = jnp.zeros((SUB, 128), F32)
        for j in range(ATOMS):
            projected += next_probs[:, j : j + 1] * jnp.maximum(0.0, 1.0 - jnp.abs(spot[:, j : j + 1] - nodes))
        projected = jnp.where(nodes < ATOMS, projected, 0.0)
        mass = jnp.sum(projected, axis=1, keepdims=True)
        row_loss = -jnp.sum(projected * logp[...], axis=1, keepdims=True)
        high = (row_loss * onehot(own[:, 5:6] == iota((SUB, plan.loss_rows), 1).astype(F32), F32)).astype(BF16)
        low = onehot(own[:, 6:7] == iota((SUB, 512), 1).astype(F32), BF16)
        loss_sums[...] += dot(high, low, TN)
        scaled = importance / totals[plan.bits, 0:1, 0:1]
        delta = (scaled * (probs_all[step] * mass - projected)).astype(BF16)
        spread = dot(delta, compact[...])
        delta_full = jnp.where(lane_action[...] == own[:, 4:5], spread, 0.0).astype(BF16)
        delta_all[rows, :] = delta_full
        grad4 = (dot(delta_full, w5[...]) * slope4[...]).astype(BF16)
        g4[rows, :] = grad4
        for y in range(7):
            pad3[y + 2, :, :448] = (dot(grad4, w4[448 * y : 448 * y + 448], NT) * s3[y]).astype(BF16)
        for pair in range(4):
            low = 128 * pair
            joined = jnp.concatenate([tall(pad3[2 - ky : 11 - ky, :, low : low + 128]) for ky in range(3)], axis=1)
            total = dot(joined, k3_wide[...], NT)
            if pair == 0:
                acc[: 9 * SUB, :256] = total
            else:
                acc[: 9 * SUB, low : low + 128] += total[:, :128]
                acc[: 9 * SUB, low + 128 : low + 256] = total[:, 128:]
        for y in range(9):
            pad2[y + 1] = (acc[y * SUB : (y + 1) * SUB, :576] * s2[y]).astype(BF16)
        for parity in range(2):
            for group in range(3):
                low = 192 * group
                part = tall(pad2[:, :, low : low + 192])
                total = dot(part[SUB:], k2[256 * parity : 256 * parity + 256], NT) + dot(
                    part[: 10 * SUB], k2[256 * parity + 512 : 256 * parity + 768], NT
                )
                if group == 0:
                    acc[: 10 * SUB, :256] = total
                else:
                    acc[: 10 * SUB, low : low + 64] += total[:, :64]
                    acc[: 10 * SUB, low + 64 : low + 256] = total[:, 64:]
            for m in range(10):
                g1[step, 2 * m + parity + 1] = (acc[m * SUB : (m + 1) * SUB, :640] * s1[parity, m]).astype(BF16)

    kept = ((x, x_kept), (a1, a1_kept), (a2, a2_kept), (pad2, pad2_kept), (pad3, pad3_kept))

    def keep_copies(step, low, high):
        return [pltpu.make_async_copy(kept[i][0], kept[i][1].at[step], keep_sem.at[i]) for i in range(low, high)]

    def back_copies(step, low, high):
        return [pltpu.make_async_copy(kept[i][1].at[step], kept[i][0], back_sem.at[i]) for i in range(low, high)]

    early = max(steps - 3, 0)

    def prefetch(step, slot):
        @pl.when(step < steps)
        def _():
            for c in raw_copies(step, slot):
                c.start()

    def raw_wait(step, slot):
        for c in raw_copies(step, slot):
            c.wait()

    def after_forward(step):
        @pl.when(role == 1)
        def _():
            probs_copy(step).start()

        @pl.when(online & (step + 1 < steps))
        def _():
            for c in keep_copies(step, 0, 3):
                c.start()

    total_step(1)
    raw_wait(0, 0)
    prefetch(1, 1)
    slope4[...] = forward(0, 0, [functools.partial(total_step, 2), lambda: None, functools.partial(total_step, 3)])
    for stage in range(4, plan.bits + 1):
        total_step(stage)
    after_forward(0)

    def one_step(step, _):
        @pl.when(online)
        def _():
            @pl.when(step > 0)
            def _():
                for c in keep_copies(step - 1, 3, 5):
                    c.wait()

            probs_copy(step).wait_recv()
            backward(step)

            @pl.when(step < early)
            def _():
                grad_start(step)

            @pl.when(step + 1 < steps)
            def _():
                for c in keep_copies(step, 3, 5):
                    c.start()

        @pl.when(step + 1 < steps)
        def _():
            following_step = step + 1
            slot = following_step % 2
            raw_wait(following_step, slot)
            prefetch(following_step + 1, 1 - slot)

            @pl.when(online)
            def _():
                for c in keep_copies(step, 0, 3):
                    c.wait()

            slope4[...] = forward(following_step, slot)
            after_forward(following_step)

        return 0

    lax.fori_loop(0, steps, one_step, 0)

    for stage in range(plan.bits):
        total_copy(stage).wait_send()

    def late_layers(step):
        total = None
        for group in range(3):
            low = 192 * group
            even, odd = (tall(a1[p, :, :, low : low + 256]) for p in range(2))
            joined = jnp.concatenate([even[: 9 * SUB], odd[: 9 * SUB], even[SUB:], odd[SUB:]], axis=1)
            term = dot(tall(pad2[1:10, :, low : low + 192]), joined, TN)
            total = term if total is None else total + term
        acc2[...] += total
        total = None
        for pair in range(4):
            low = 128 * pair
            joined = jnp.concatenate([tall(a2[ky : ky + 7, :, low : low + 256]) for ky in range(3)], axis=1)
            term = dot(tall(pad3[2:9, :, low : low + 128]), joined, TN)
            total = term if total is None else total + term
        acc3[...] += total
        for at, (count, lanes) in enumerate(((20, 640), (9, 576), (7, 448))):
            part = jnp.zeros((8, lanes), F32)
            for y in range(count):
                piece = (g1[step, y + 1] if at == 0 else pad2[y + 1] if at == 1 else pad3[y + 2, :, :448]).astype(F32)
                for q in range(SUB // 8):
                    part += piece[8 * q : 8 * q + 8]
            bias_sums[at, :, :lanes] += part

    def first_layer(step):
        for group in range(3):
            lanes = 192 if group == 2 else 224
            part = tall(g1[step, 1:21, :, 224 * group : 224 * group + lanes])
            pixels = tall(x[:, :, 512 * group : 512 * group + 512])
            joined = jnp.concatenate([pixels[: 20 * SUB], pixels[SUB:]], axis=1)
            acc1[:lanes] += dot(part, joined, TN)

    def weight_step(turn, step):
        @pl.when(turn > 0)
        def _():
            for c in back_copies(step, 1, 5):
                c.wait()

        late_layers(step)

        @pl.when(turn + 1 < steps)
        def _():
            for c in back_copies(turn, 1, 5):
                c.start()

        @pl.when(turn > 0)
        def _():
            for c in back_copies(step, 0, 1):
                c.wait()

        first_layer(step)

        @pl.when(turn + 1 < steps)
        def _():
            for c in back_copies(turn, 0, 1):
                c.start()

    def dense_sums():
        flat = raw.reshape(2 * (TILES - 1) * SUB * STACK, 128)
        for y in range(7):
            block = dot(a3[y], g4[...], TN)
            for px in range(7):
                for q in range(4):
                    flat[pl.ds(3136 * q + 7 * y + px, 64, stride=49), :] = block[
                        64 * px : 64 * px + 64, 128 * q : 128 * q + 128
                    ]
        for q in range(4):
            send[:3136, 128 * q : 128 * q + 128] = flat[3136 * q : 3136 * q + 3136].astype(BF16)
        head = dot(delta_all[...], a4[...], TN)
        send[ROW_HEAD : ROW_HEAD + 912] = head[:912].astype(BF16)
        send[ROW_HEAD + 912 : ROW_HEAD + 928] = jnp.concatenate(
            [head[912:LOGITS], jnp.zeros((928 - LOGITS, 512), F32)], axis=0
        ).astype(BF16)
        send[ROW_HEAD + 928 : plan.rest] = jnp.zeros((plan.rest - ROW_HEAD - 928, 512), BF16)

    def other_sums():
        def put(low, value):
            send[plan.rest + low : plan.rest + low + value.shape[0]] = value.astype(BF16)

        folded = acc1[0:32]
        for px in range(1, 7):
            folded += pltpu.roll(acc1[32 * px : 32 * px + 32], 1024 - 4 * px, 1)
        column = iota((1024, 256), 1)
        goal = ((column >> 5) & 1) * 512 + (column >> 6) * 128 + ((column >> 3) & 3) * 32 + (column & 7)
        pick = onehot(iota((1024, 256), 0) == goal, F32)
        put(ROW_ONE, jnp.concatenate([dot(folded, pick, precision=HIGHEST), jnp.zeros((32, 256), F32)], axis=1))
        folded = acc2[0:64]
        for px in range(1, 3):
            folded += pltpu.roll(acc2[64 * px : 64 * px + 64], 1024 - 64 * px, 1)
        column = iota((1024, 512), 1)
        goal = ((column >> 2) & 3) * 256 + (column & 3) * 32 + (column >> 4)
        pick = onehot(iota((1024, 512), 0) == goal, F32)
        put(ROW_TWO, dot(folded, pick, precision=HIGHEST))
        folded = acc3[0:64] + pltpu.roll(acc3[64:128], 768 - 64, 1)
        row = iota((768, 576), 0)
        goal = (row & 63) * 9 + (row >> 8) * 3 + ((row >> 6) & 3)
        pick = onehot((iota((768, 576), 1) == goal) & (((row >> 6) & 3) < 3), F32)
        third = dot(folded, pick, precision=HIGHEST)
        put(ROW_THREE, third[:, :512])
        put(ROW_THREE_REST, jnp.concatenate([third[:, 512:], jnp.zeros((64, 448), F32)], axis=1))
        bias_rows = []
        for at, (size, copies) in enumerate(((32, 20), (64, 9), (64, 7))):
            fold = onehot((iota((size * copies, 512), 0) & (size - 1)) == iota((size * copies, 512), 1), F32)
            line = jnp.sum(bias_sums[at, :, : size * copies], axis=0, keepdims=True)
            bias_rows.append(dot(line, fold, precision=HIGHEST))
        bias_rows.append(jnp.sum(g4[...].astype(F32), axis=0, keepdims=True))
        head_bias = jnp.sum(delta_all[...].astype(F32), axis=0, keepdims=True)
        bias_rows.append(head_bias[:, :512])
        bias_rows.append(jnp.concatenate([head_bias[:, 512:], jnp.zeros((1, 1024 - LOGITS), F32)], axis=1))
        bias_rows.append(jnp.zeros((10, 512), F32))
        put(ROW_BIAS, jnp.concatenate(bias_rows, axis=0))
        put(ROW_LOSS, loss_sums[...])
        left = plan.rows - plan.rest - ROW_LOSS - plan.loss_rows
        if left:
            put(ROW_LOSS + plan.loss_rows, jnp.zeros((left, 512), F32))

    def stage_rows(stream, stage):
        base, size, order = plan.streams[stream]
        low = base
        for bit in order[:stage]:
            size //= 2
            low = low + bit_of(bit) * size
        return low, size

    def aligned(at):
        return pl.multiple_of(at, 16)

    def scatter_copy(stream, stage):
        base, size, order = plan.streams[stream]
        low, count = stage_rows(stream, stage)
        half = count // 2
        away = aligned(low + (1 - bit_of(order[stage])) * half)
        into = base + size - count
        index = stream * plan.bits + stage
        return remote(
            send.at[pl.ds(away, half)], landed.at[pl.ds(into, half)], rs_send.at[index], rs_recv.at[index],
            across(order[stage]),
        )

    def scatter_start(streams):
        for stream in streams:
            scatter_copy(stream, 0).start()

    def scatter_finish(stage, streams):
        for stream in streams:
            base, size, order = plan.streams[stream]
            scatter_copy(stream, stage).wait_recv()
            low, count = stage_rows(stream, stage)
            half = count // 2
            keep = aligned(low + bit_of(order[stage]) * half)
            into = base + size - count
            target = final if stage == plan.bits - 1 else send
            block = next(b for b in (128, 64, 32, 16) if half % b == 0)

            def add(i, _, keep=keep, into=into, target=target, block=block):
                at = aligned(keep + i * block)
                target[pl.ds(at, block)] = send[pl.ds(at, block)] + landed[pl.ds(aligned(into + i * block), block)]
                return 0

            lax.fori_loop(0, half // block, add, 0)
            if stage + 1 < plan.bits:
                scatter_copy(stream, stage + 1).start()
            else:
                over_copy(stream).start()
                gather_copy(stream, 0).start()

    def over_copy(stream):
        low, count = stage_rows(stream, plan.bits)
        spot = pl.ds(aligned(low), count)
        return remote(final.at[spot], final.at[spot], x_send.at[stream], x_recv.at[stream], other_role)

    def gather_copy(stream, stage):
        order = plan.streams[stream][2]
        low, count = stage_rows(stream, plan.bits - stage)
        spot = pl.ds(aligned(low), count)
        index = stream * plan.bits + stage
        return remote(
            final.at[spot], final.at[spot], ag_send.at[index], ag_recv.at[index], across(order[plan.bits - 1 - stage])
        )

    def result_copies(stream):
        low, size, _ = plan.streams[stream]
        cut = min(max(low, ROW_HEAD), low + size)
        found = []
        if low < cut:
            spot = pl.ds(low, cut - low)
            found.append(pltpu.make_async_copy(final.at[spot], dense_out.at[spot], out_sem.at[2 * stream]))
        if cut < low + size:
            here, there = pl.ds(cut, low + size - cut), pl.ds(cut - ROW_HEAD, low + size - cut)
            found.append(pltpu.make_async_copy(final.at[here], sums_out.at[there], out_sem.at[2 * stream + 1]))
        return found

    def over_finish(streams):
        for stream in streams:
            over_copy(stream).wait_recv()
            gather_copy(stream, 0).start()

    def gather_finish(stage, streams):
        for stream in streams:
            gather_copy(stream, stage).wait_recv()
            if stage + 1 < plan.bits:
                gather_copy(stream, stage + 1).start()
            else:
                for c in result_copies(stream):
                    c.start()

    tile_rows = raw.reshape(2 * (TILES - 1) * SUB * STACK, 128)

    tile_pairs = raw.reshape((TILES - 1) * SUB * STACK, 2, 128)

    def tile_copies(step):
        return [
            pltpu.make_async_copy(
                tile_pairs.at[pl.ds(t * SUB, SUB)],
                frame_out.at[pl.ds(step * SUB, SUB), :, pl.ds(128 * t, 128)],
                tile_sem,
            )
            for t in range(TILES)
        ]

    def frame_step(step):
        frame_products(g1.at[step], band_k, acc)

        @pl.when(step > 0)
        def _():
            for c in tile_copies(step - 1):
                c.wait()

        for c in range(2):
            for t in range(TILES):
                tile_rows[pl.ds(t * SUB * 2 + c, SUB, stride=2), :] = frame_tile(acc, c, t)
        for c in tile_copies(step):
            c.start()

    bits, first, second = plan.bits, plan.first, plan.second

    late_grads = [(step, half) for step in range(early, steps) for half in range(2)]
    issue = {"soon": late_grads[:-4], "mid": late_grads[-4:-3], "over": late_grads[-3:-2], "last": late_grads[-2:]}

    def grads_at(moment):
        for step, half in issue[moment]:
            grad_copy(step, half).start()

    def turn_at(number):
        return min(number, steps - 1)

    @pl.when(online)
    def _():
        dense_sums()
        scatter_start(first)

        def turns(turn, _):
            weight_step(turn, jnp.where(turn == 0, steps - 1, turn - 1))

            @pl.when(turn == turn_at(1))
            def _():
                scatter_finish(0, first)
                grads_at("soon")

            return 0

        lax.fori_loop(0, steps, turns, 0)
        scatter_finish(1, first)
        grads_at("mid")
        other_sums()
        scatter_start(second)
        build_frame(k1_ref[:, 0:128], band_k)

    @pl.when(role == 1)
    def _():
        kernel_copy.wait_recv()
        build_frame(k1_online[:, 128:256], band_k)

    def frame_and_more(step, _):
        @pl.when(role == 1)
        def _():
            for half in range(2):
                grad_copy(step, half).wait_recv()

        frame_step(step)

        @pl.when(online & (step == 0))
        def _():
            scatter_finish(0, second)
            scatter_finish(2, first)

        @pl.when(online & (step == turn_at(1)))
        def _():
            scatter_finish(1, second)

        @pl.when(online & (step == turn_at(2)))
        def _():
            for stage in range(3, bits):
                scatter_finish(stage, first)
            grads_at("over")
            scatter_finish(2, second)

        @pl.when(online & (step == turn_at(3)))
        def _():
            for stage in range(3, bits):
                scatter_finish(stage, second)
            grads_at("last")

        @pl.when(online & (step == turn_at(5)))
        def _():
            gather_finish(0, first)
            gather_finish(0, second)

        @pl.when((role == 1) & (step == max(steps - 3, 0)))
        def _():
            over_finish(first)
            gather_finish(0, first)
            over_finish(second)
            for stage in range(1, bits - 2):
                gather_finish(stage, first)
                gather_finish(stage - 1, second)

        @pl.when((role == 1) & (step == max(steps - 2, 0)))
        def _():
            gather_finish(bits - 2, first)
            gather_finish(bits - 3, second)
            gather_finish(bits - 2, second)

        @pl.when((role == 1) & (step == steps - 1))
        def _():
            gather_finish(bits - 1, first)
            gather_finish(bits - 1, second)

        return 0

    lax.fori_loop(0, steps, frame_and_more, 0)

    @pl.when(online)
    def _():
        for stage in range(1, bits):
            gather_finish(stage, first)
            gather_finish(stage, second)

    for c in tile_copies(steps - 1):
        c.wait()
    for stream in range(len(plan.streams)):
        for stage in range(plan.bits):
            gather_copy(stream, stage).wait_send()

    @pl.when(online)
    def _():
        kernel_copy.wait_send()
        for stream in range(len(plan.streams)):
            over_copy(stream).wait_send()
            for stage in range(plan.bits):
                scatter_copy(stream, stage).wait_send()

        def sent(step, _):
            for half in range(2):
                grad_copy(step, half).wait_send()
            return 0

        lax.fori_loop(0, steps, sent, 0)

    @pl.when(role == 1)
    def _():
        def sent(step, _):
            probs_copy(step).wait_send()
            return 0

        lax.fori_loop(0, steps, sent, 0)

    for stream in range(len(plan.streams)):
        for c in result_copies(stream):
            c.wait()


def core(plan, frames, edge, weights, facts, tables):
    rows = frames.shape[1]
    steps = rows // SUB
    k1, k2, k3, w4, b1, b2, b3, b4, w5, b5 = weights
    vmem, hbm = pl.BlockSpec(memory_space=pltpu.VMEM), pl.BlockSpec(memory_space=pl.ANY)
    dma = pltpu.SemaphoreType.DMA
    streams = len(plan.streams)
    scratch = [
        pltpu.VMEM((2, TILES - 1, SUB, STACK, 128), F32),
        pltpu.VMEM((3 * STACK * SUB, 512), BF16),
        pltpu.VMEM((21, SUB, 1536), BF16),
        pltpu.VMEM((2, 10, SUB, 640), BF16),
        pltpu.VMEM((2, 10, SUB, 640), F32),
        pltpu.VMEM((9, SUB, 640), BF16),
        pltpu.VMEM((9, SUB, 576), F32),
        pltpu.VMEM((7, rows, 448), BF16),
        pltpu.VMEM((7, SUB, 448), F32),
        pltpu.VMEM((rows, 512), BF16),
        pltpu.VMEM((rows, 512), BF16),
        pltpu.VMEM((rows, LOGITS), BF16),
        pltpu.VMEM((steps, 22, SUB, 640), BF16),
        pltpu.VMEM((11, SUB, 576), BF16),
        pltpu.VMEM((11, SUB, 512), BF16),
        pltpu.VMEM((21 * SUB, 2 * WIDE), F32),
        pltpu.VMEM((2, 2 * WIDE, 640), BF16),
        pltpu.VMEM((1024, 224), BF16),
        pltpu.VMEM((1024, 192), BF16),
        pltpu.VMEM((768, 128), BF16),
        pltpu.VMEM((256, 384), BF16),
        pltpu.VMEM((3136, 512), BF16),
        pltpu.VMEM((8, 640), F32),
        pltpu.VMEM((224, 1024), F32),
        pltpu.VMEM((192, 1024), F32),
        pltpu.VMEM((128, 768), F32),
        pltpu.VMEM((3, 8, 640), F32),
        pltpu.VMEM((plan.loss_rows, 512), F32),
        pltpu.VMEM((plan.rows, 512), BF16),
        pltpu.VMEM((plan.rows, 512), BF16),
        pltpu.VMEM((plan.rows, 512), BF16),
        pltpu.VMEM((steps, SUB, 128), F32),
        pltpu.VMEM((SUB, 128), F32),
        pltpu.VMEM((steps, SUB, 128), F32),
        pltpu.VMEM((plan.bits + 1, 8, 128), F32),
        pltpu.VMEM((plan.bits, 8, 128), F32),
        pltpu.VMEM((32, 256), BF16),
        pltpu.VMEM((rows, 128), F32),
        pltpu.VMEM((SUB, 512), F32),
        dma((5,)), dma((5,)), dma((2,)), dma, dma, dma((steps,)), dma((steps,)), dma((2 * steps,)), dma((2 * steps,)),
        dma((plan.bits,)), dma((plan.bits,)), dma, dma,
        dma((streams * plan.bits,)), dma((streams * plan.bits,)), dma((streams * plan.bits,)), dma((streams * plan.bits,)),
        dma((streams,)), dma((streams,)), dma((2 * streams,)),
    ]
    return pl.pallas_call(
        functools.partial(core_kernel, plan, steps),
        in_specs=[hbm, vmem, vmem, vmem, vmem, hbm] + [vmem] * 14,
        out_specs=[hbm] * 8,
        out_shape=[
            jax.ShapeDtypeStruct((rows, 2, TILES * 128), F32),
            jax.ShapeDtypeStruct((ROW_HEAD, 512), BF16),
            jax.ShapeDtypeStruct((plan.rows - ROW_HEAD, 512), BF16),
            jax.ShapeDtypeStruct((steps - 1, 21, SUB, 1536), BF16),
            jax.ShapeDtypeStruct((steps - 1, 2, 10, SUB, 640), BF16),
            jax.ShapeDtypeStruct((steps - 1, 9, SUB, 640), BF16),
            jax.ShapeDtypeStruct((steps - 1, 11, SUB, 576), BF16),
            jax.ShapeDtypeStruct((steps - 1, 11, SUB, 512), BF16),
        ],
        scratch_shapes=scratch,
        compiler_params=pltpu.CompilerParams(vmem_limit_bytes=63 << 20, collective_id=0, has_side_effects=True),
        name="core",
    )(frames, edge, k1, k2, k3, w4, b1, b2, b3, b4, w5, b5, *facts, *tables)[:3]


def finish_kernel(plan, own, frames, dense, sums, frame_out, w4, k1, b1, k2, b2, k3, b3, b4, w5, b5, losses):
    frame_out[...] = frames[:, :, :PIX]
    w4[...] = dense[...].astype(F32)

    def part(low, high):
        return sums[plan.rest - ROW_HEAD + low : plan.rest - ROW_HEAD + high]

    @pl.when(pl.program_id(0) == 0)
    def _():
        w5[:912] = sums[:912].astype(F32)
        w5[912:] = sums[912:928].astype(F32)[: LOGITS - 912]
        k2[...] = part(ROW_TWO, ROW_THREE).astype(F32)
        k3[:, :512] = part(ROW_THREE, ROW_THREE_REST).astype(F32)
        k3[:, 512:] = part(ROW_THREE_REST, ROW_ONE)[:, :64].astype(F32)
        k1[...] = part(ROW_ONE, ROW_BIAS)[:, :256].astype(F32)
        rows = part(ROW_BIAS, ROW_LOSS).astype(F32)
        b1[...] = rows[0:1, :32]
        b2[...] = rows[1:2, :64]
        b3[...] = rows[2:3, :64]
        b4[...] = rows[3:4]
        b5[:, :512] = rows[4:5]
        b5[:, 512:] = rows[5:6, : LOGITS - 512]
        device = lax.axis_index("role") * plan.batch + lax.axis_index("batch")
        slot = device * own + iota((1, own), 1)
        chosen = dot(part(ROW_LOSS, ROW_LOSS + plan.loss_rows), onehot(iota((512, own), 0) == (slot & 511), BF16))
        mine = iota((plan.loss_rows, own), 0) == (slot >> 9)
        losses[...] = jnp.sum(jnp.where(mine, chosen, 0.0), axis=0, keepdims=True)


def finish(plan, own, frames, dense, sums):
    rows = frames.shape[0]
    small = ((32, 256), (1, 32), (64, 512), (1, 64), (64, 576), (1, 64), (1, 512), (LOGITS, 512), (1, LOGITS), (1, own))
    block, pieces = (56, 4) if rows % 56 == 0 else (16, 14)
    frame_at, dense_at = (lambda i: (i, 0, 0)), (lambda i: (jnp.minimum(i, pieces - 1), 0))
    return pl.pallas_call(
        functools.partial(finish_kernel, plan, own),
        grid=(rows // block,),
        in_specs=[
            pl.BlockSpec((block, 2, TILES * 128), frame_at),
            pl.BlockSpec((ROW_HEAD // pieces, 512), dense_at),
            pl.BlockSpec(sums.shape, lambda i: (0, 0)),
        ],
        out_specs=[
            pl.BlockSpec((block, 2, PIX), frame_at),
            pl.BlockSpec((ROW_HEAD // pieces, 512), dense_at),
            *[pl.BlockSpec(s, lambda i: (0, 0)) for s in small],
        ],
        out_shape=[jax.ShapeDtypeStruct(s, F32) for s in ((rows, 2, PIX), (ROW_HEAD, 512), *small)],
        compiler_params=pltpu.CompilerParams(vmem_limit_bytes=60 << 20),
        name="finish",
    )(frames, dense, sums)


def on_device(
    frames,
    conv1_weight,
    conv1_bias,
    conv2_weight,
    conv2_bias,
    conv3_weight,
    conv3_bias,
    dense_weight,
    dense_bias,
    head_weight,
    head_bias,
    taken_actions,
    next_actions,
    rewards,
    discounts,
    importance,
    buffer_slots,
):
    roles, batch = lax.axis_size("role"), lax.axis_size("batch")
    rows = frames.shape[1]
    slots = rows * batch
    plan = Plan(batch, slots)

    lane_action = jnp.asarray(np.arange(LOGITS)[None] // ATOMS, F32)
    compact = jnp.asarray(np.arange(128)[:, None] == np.arange(LOGITS)[None] % ATOMS, BF16)
    facts = [
        v.reshape(1, rows) for v in (taken_actions, next_actions, rewards, discounts, importance, buffer_slots)
    ]
    edge = frames[0, :, :, 128 * (TILES - 1) :]
    weights = (
        conv1_weight[0].T, conv2_weight[0].T, conv3_weight[0].T, dense_weight[0],
        conv1_bias, conv2_bias, conv3_bias, dense_bias, head_weight[0].T, head_bias,
    )
    partial = core(plan, frames, edge, weights, facts, (lane_action, compact))
    frame_part, w4, k1, b1, k2, b2, k3, b3, b4, w5, b5, priorities = finish(plan, slots // (roles * batch), *partial)
    return (frame_part, k1.T, b1[0], k2.T, b2[0], k3.T, b3[0], w4, b4[0], w5.T, b5[0], priorities[0])


def solution(mesh):
    in_specs = (
        P("role", "batch", None, None),
        P("role", None, None),
        P("role", None),
        P("role", None, None),
        P("role", None),
        P("role", None, None),
        P("role", None),
        P("role", None, None),
        P("role", None),
        P("role", None, None),
        P("role", None),
        P("batch"),
        P("batch"),
        P("batch"),
        P("batch"),
        P("batch"),
        P("batch"),
    )
    out_specs = (
        P("batch", "role", None),
        P(),
        P(),
        P(),
        P(),
        P(),
        P(),
        P(),
        P(),
        P(),
        P(),
        P(("role", "batch")),
    )
    return jax.shard_map(on_device, mesh=mesh, in_specs=in_specs, out_specs=out_specs, check_vma=False)
```

```python
import functools

import jax
import jax.numpy as jnp
import numpy as np
from jax import lax
from jax.experimental import pallas as pl
from jax.experimental.pallas import tpu as pltpu
from jax.sharding import PartitionSpec as P

STACK = 4
SIDE = 84
ACTIONS = 18
ATOMS = 51
LOGITS = ACTIONS * ATOMS
PIX = SIDE * SIDE
BAND = 4 * SIDE
WIDE = 384
TILES = 56
SUB = 32
F32 = jnp.float32
BF16 = jnp.bfloat16
HIGHEST = lax.Precision.HIGHEST
MESH = pl.DeviceIdType.MESH

NN = (((1,), (0,)), ((), ()))
NT = (((1,), (1,)), ((), ()))
TN = (((0,), (0,)), ((), ()))

ROW_HEAD = 3136
ROW_REST = 4096
ROW_TWO = 0
ROW_THREE = ROW_TWO + 64
ROW_THREE_REST = ROW_THREE + 64
ROW_ONE = ROW_THREE_REST + 64
ROW_BIAS = ROW_ONE + 32
ROW_LOSS = ROW_BIAS + 16


def dot(left, right, dims=NN, precision=None):
    return lax.dot_general(left, right, dims, precision=precision, preferred_element_type=F32)


def iota(shape, dim):
    return lax.broadcasted_iota(jnp.int32, shape, dim)


def onehot(condition, dtype):
    return jnp.where(condition, 1.0, 0.0).astype(dtype)


def silu_and_slope(pre):
    gate = 0.5 * jnp.tanh(0.5 * pre) + 0.5
    act = pre * gate
    return act.astype(BF16), gate + act * (1.0 - gate)


def tall(value):
    return value.reshape(value.shape[0] * value.shape[1], value.shape[2])


class Plan:
    def __init__(self, batch, slots):
        self.batch = batch
        self.bits = batch.bit_length() - 1
        if 1 << self.bits != batch:
            raise ValueError("batch axis")
        self.loss_rows = -(-slots // (512 * 16)) * 16
        unit = 16 * batch
        units = -(-ROW_REST // unit)
        self.rest = units * unit
        rest_units = -(-(ROW_LOSS + self.loss_rows) // unit)
        self.rows = (units + rest_units) * unit
        count = min(4, units)
        up = list(range(self.bits))
        round_way = up[:1] + up[2:] + up[1:2]
        self.streams, at = [], 0
        for s in range(count):
            size = (units // count + (1 if s < units % count else 0)) * unit
            self.streams.append((at, size, up if s % 2 == 0 else round_way))
            at += size
        self.first = list(range(count))
        self.second = [count]
        self.streams.append((at, rest_units * unit, up))


def banded_first(kernel_t, channel, line, column, real, channels, lanes):
    rows = channel.shape[0]
    spread = onehot((iota((lanes, 32), 0) & 31) == iota((lanes, 32), 1), BF16)
    tiled = dot(spread, kernel_t).astype(BF16)
    block, rest = column >> 2, column & 3
    lane_x = iota((rows, lanes), 1) >> 5
    found = []
    for half in range(2):
        parts = []
        for step in range(2):
            goal = jnp.where(real, channel * 64 + (4 * half + line) * 8 + 4 * step + rest, -1)
            pick = onehot(iota((rows, channels * 64), 1) == goal, BF16)
            parts.append(dot(pick, tiled, NT))
        found.append(jnp.where(lane_x == block, parts[0], jnp.where(lane_x == block - 1, parts[1], 0.0)).astype(BF16))
    return found


def build_first(kernel_t, out):
    row = iota((512, 1), 0)
    found = banded_first(kernel_t, row >> 7, (row >> 5) & 3, row & 31, row >= 0, STACK, 224)
    for half in range(2):
        out[512 * half : 512 * half + 512] = found[half]


def build_frame(kernel_t, out):
    row = iota((2 * WIDE, 1), 0)
    channel = (row >= WIDE).astype(jnp.int32)
    inner = row - channel * WIDE
    line = sum((inner >= SIDE * i).astype(jnp.int32) for i in range(1, 5))
    found = banded_first(kernel_t, channel, line, inner - line * SIDE, line < 4, 2, 640)
    for half in range(2):
        out[half] = found[half]


def build_second(kernel_t, out):
    goal = (iota((512, 512), 0) & 31) * 16 + (iota((512, 512), 0) >> 5)
    by_place = dot(onehot(iota((512, 512), 1) == goal, BF16), kernel_t, NT).astype(BF16)
    out[...] = jnp.zeros_like(out)
    for ky in range(4):
        for kx in range(4):
            piece = by_place[(ky * 4 + kx) * 32 : (ky * 4 + kx + 1) * 32]
            for x in range(3):
                low = 256 * ky + (2 * x + kx) * 32
                out[low : low + 32, 64 * x : 64 * x + 64] = piece


def build_third(kernel_t, tall_out, wide_out):
    goal = (iota((576, 576), 0) & 63) * 9 + (iota((576, 576), 0) >> 6)
    by_place = dot(onehot(iota((576, 576), 1) == goal, BF16), kernel_t, NT).astype(BF16)
    tall_out[...] = jnp.zeros_like(tall_out)
    wide_out[...] = jnp.zeros_like(wide_out)
    for ky in range(3):
        for kx in range(3):
            piece = by_place[(ky * 3 + kx) * 64 : (ky * 3 + kx + 1) * 64]
            for x in range(2):
                low = (x + kx) * 64
                tall_out[256 * ky + low : 256 * ky + low + 64, 64 * x : 64 * x + 64] = piece
                wide_out[low : low + 64, 128 * ky + 64 * x : 128 * ky + 64 * x + 64] = piece


def build_picks(out):
    lane = iota((1, WIDE), 1)
    group, line, column = lane >> 7, (lane >> 5) & 3, lane & 31
    goal = jnp.where(28 * group + column < SIDE, SIDE * line + 28 * group + column, -1000)
    row = iota((512, WIDE), 0)
    for kind in range(8):
        out[512 * kind : 512 * kind + 512, :WIDE] = onehot(row == goal + (BAND * kind) % 128, BF16)


def frame_products(grads, band_k, acc):
    acc[...] = dot(tall(grads[1:22]), band_k[0], NT) + dot(tall(grads[0:21]), band_k[1], NT)


def frame_tile(acc, c, t):
    pieces, at, end = [], 128 * t, min(128 * t + 128, PIX)
    while at < end:
        band, inner = divmod(at, BAND)
        size = min(end - at, BAND - inner)
        pieces.append(acc[band * SUB : (band + 1) * SUB, WIDE * c + inner : WIDE * c + inner + size])
        at += size
    if end < 128 * t + 128:
        pieces.append(jnp.zeros((SUB, 128 * t + 128 - end), F32))
    return pieces[0] if len(pieces) == 1 else jnp.concatenate(pieces, axis=1)


def core_kernel(plan, steps, *refs):
    (
        x_hbm, edge, k1_ref, k2_ref, k3_ref, w4_hbm, b1_ref, b2_ref, b3_ref, b4, w5, b5, taken, following, rewards, discounts,
        weighting, buffer_slots, lane_action, compact,
    ) = refs[:20]
    frame_out, dense_out, sums_out, x_kept, a1_kept, a2_kept, pad2_kept, pad3_kept = refs[20:28]
    (
        raw, lines, x, a1, s1, a2, s2, a3, s3, a4, g4, delta_all, g1, pad2, pad3, acc, band_k,
        k1, k2, k3, k3_wide, w4, bias, acc1, acc2, acc3, bias_sums, loss_sums, send, landed, final, probs_all, logp, nexts,
        totals, totals_in, k1_online, cols, slope4,
        keep_sem, back_sem, raw_sem, w4_sem, tile_sem, probs_send, probs_recv, g1_send, g1_recv, tot_send, tot_recv, k1_send, k1_recv,
        rs_send, rs_recv, ag_send, ag_recv, x_send, x_recv, out_sem,
    ) = refs[28:]
    role, place = lax.axis_index("role"), lax.axis_index("batch")
    online = role == 0

    def bit_of(bit):
        return (place // (1 << bit)) % 2

    def across(bit):
        return {"batch": place + (1 - 2 * bit_of(bit)) * (1 << bit)}

    other_role = {"role": 1 - role}

    def remote(src, dst, send_sem, recv_sem, device):
        return pltpu.make_async_remote_copy(
            src_ref=src, dst_ref=dst, send_sem=send_sem, recv_sem=recv_sem, device_id=device, device_id_type=MESH
        )

    def raw_copies(step, slot):
        return [
            pltpu.make_async_copy(
                x_hbm.at[0, pl.ds(step * SUB, SUB), :, pl.ds(128 * t, 128)], raw.at[slot, t], raw_sem.at[slot]
            )
            for t in range(TILES - 1)
        ]

    weight_copy = pltpu.make_async_copy(w4_hbm, send.at[pl.ds(0, 3136)], w4_sem)
    weight_copy.start()
    for c in raw_copies(0, 0):
        c.start()

    barrier = pltpu.get_barrier_semaphore()
    for bit in range(plan.bits):
        pl.semaphore_signal(barrier, inc=1, device_id=across(bit), device_id_type=MESH)
    pl.semaphore_signal(barrier, inc=1, device_id=other_role, device_id_type=MESH)

    slot_number = buffer_slots[...].astype(F32)
    slot_row = jnp.floor(slot_number * (1.0 / 512))
    taken_number = taken[...].astype(F32)
    facts = [
        rewards[...], discounts[...], weighting[...], jnp.where(online, taken_number, following[...].astype(F32)), taken_number,
        slot_row, slot_number - 512.0 * slot_row, rewards[...],
    ]
    cols[...] = dot(jnp.concatenate(facts, axis=0), onehot(iota((8, 128), 0) == iota((8, 128), 1), F32), TN, HIGHEST)
    totals[0] = jnp.broadcast_to(jnp.sum(weighting[...], axis=1, keepdims=True), (8, 128))

    def total_copy(stage):
        return remote(totals.at[stage], totals_in.at[stage], tot_send.at[stage], tot_recv.at[stage], across(stage))

    def total_step(stage):
        if stage > 0:
            total_copy(stage - 1).wait_recv()
            totals[stage] = totals[stage - 1] + totals_in[stage - 1]
        if stage < plan.bits:
            total_copy(stage).start()

    build_first(k1_ref[...], k1)
    build_second(k2_ref[...], k2)
    build_third(k3_ref[...], k3, k3_wide)

    kernel_copy = remote(k1_ref, k1_online, k1_send, k1_recv, other_role)

    pl.semaphore_wait(barrier, plan.bits + 1)
    total_step(0)

    @pl.when(online)
    def _():
        kernel_copy.start()

    weight_copy.wait()
    spare = raw.reshape(2, (TILES - 1) * SUB * STACK, 128)
    for pair in range(2):
        for q in range(2):
            low = 128 * (2 * pair + q)
            spare[1, 3136 * q : 3136 * q + 3136] = send[:3136, low : low + 128].astype(F32)
        for spot in range(49):
            for q in range(2):
                low = 128 * (2 * pair + q)
                w4[64 * spot : 64 * spot + 64, low : low + 128] = spare[
                    1, pl.ds(3136 * q + spot, 64, stride=49), :
                ].astype(BF16)
    build_picks(send)
    bias[...] = jnp.zeros_like(bias)
    for at, (ref, size, copies) in enumerate(((b1_ref, 32, 20), (b2_ref, 64, 9), (b3_ref, 64, 7))):
        repeat = onehot((iota((size, size * copies), 1) & (size - 1)) == iota((size, size * copies), 0), F32)
        bias[at : at + 1, : size * copies] = dot(ref[...], repeat, precision=HIGHEST)
    acc1[...] = jnp.zeros_like(acc1)
    acc2[...] = jnp.zeros_like(acc2)
    acc3[...] = jnp.zeros_like(acc3)
    bias_sums[...] = jnp.zeros_like(bias_sums)
    loss_sums[...] = jnp.zeros_like(loss_sums)
    pad3[...] = jnp.zeros_like(pad3)
    pad2[...] = jnp.zeros_like(pad2)
    a2[...] = jnp.zeros_like(a2)
    for step in range(steps):
        g1[step, 0] = jnp.zeros((SUB, 640), BF16)
        g1[step, 21] = jnp.zeros((SUB, 640), BF16)

    raw_flat = raw.reshape(2, TILES - 1, SUB * STACK, 128)

    def forward(step, slot, hooks=()):
        hooks = list(hooks)

        def hook():
            if hooks:
                hooks.pop(0)()

        rows = pl.ds(pl.multiple_of(step * SUB, SUB), SUB)
        own = cols[rows, :]
        for kind in range(8):
            bands = list(range(kind, 21, 8))
            for at, band in enumerate(bands):
                low = BAND * band // 128
                for c in range(STACK):
                    place_at = (at * STACK + c) * SUB
                    for t in range(4):
                        if low + t < TILES - 1:
                            piece = raw_flat[slot, low + t, pl.ds(c, SUB, stride=STACK), :]
                        else:
                            piece = edge[pl.ds(pl.multiple_of(step * SUB, SUB), SUB), c, :]
                            piece = jnp.concatenate([piece, jnp.zeros((SUB, 128 - piece.shape[1]), F32)], axis=1)
                        lines[place_at : place_at + SUB, 128 * t : 128 * t + 128] = piece.astype(BF16)
            count = len(bands) * STACK * SUB
            sorted_lines = dot(lines[:count], send[512 * kind : 512 * kind + 512, :WIDE]).astype(BF16)
            for at, band in enumerate(bands):
                for c in range(STACK):
                    place_at = (at * STACK + c) * SUB
                    for group in range(3):
                        x[band, :, 512 * group + 128 * c : 512 * group + 128 * c + 128] = sorted_lines[
                            place_at : place_at + SUB, 128 * group : 128 * group + 128
                        ]
        hook()
        for group, lanes in enumerate((224, 224, 192)):
            part = tall(x[:, :, 512 * group : 512 * group + 512])
            joined = jnp.concatenate([part[: 20 * SUB], part[SUB:]], axis=1)
            acc[: 20 * SUB, 224 * group : 224 * group + lanes] = dot(joined, k1[:, :lanes])
        hook()
        for y in range(20):
            act, slope = silu_and_slope(acc[y * SUB : (y + 1) * SUB, :640] + bias[0:1, :640])
            a1[y % 2, y // 2] = act
            s1[y % 2, y // 2] = slope
        hook()
        for group in range(3):
            even, odd = (tall(a1[p, :, :, 192 * group : 192 * group + 256]) for p in range(2))
            joined = jnp.concatenate([even[: 9 * SUB], odd[: 9 * SUB], even[SUB:], odd[SUB:]], axis=1)
            acc[: 9 * SUB, 192 * group : 192 * group + 192] = dot(joined, k2[...])
        for y in range(9):
            act, slope = silu_and_slope(acc[y * SUB : (y + 1) * SUB, :576] + bias[1:2, :576])
            a2[y, :, :576] = act
            s2[y] = slope
        hook()
        for pair in range(4):
            low = 128 * pair
            joined = jnp.concatenate([tall(a2[ky : ky + 7, :, low : low + 256]) for ky in range(3)], axis=1)
            acc[: 7 * SUB, low : low + 128] = dot(joined, k3[...])
        hook()
        pre4 = b4[...]
        for y in range(7):
            act, slope = silu_and_slope(acc[y * SUB : (y + 1) * SUB, :448] + bias[2:3, :448])
            a3[y, rows, :] = act
            s3[y] = slope
            pre4 = pre4 + dot(act, w4[448 * y : 448 * y + 448])
        act, slope = silu_and_slope(pre4)
        a4[rows, :] = act
        logits = dot(act, w5[...], NT) + b5[...]
        picked = jnp.where(lane_action[...] == own[:, 3:4], logits, 0.0)
        high = picked.astype(BF16)
        rest = picked - high.astype(F32)
        middle = rest.astype(BF16)
        low_part = (rest - middle.astype(F32)).astype(BF16)
        thrice = dot(jnp.concatenate([high, middle, low_part], axis=0), compact[...], NT)
        chosen = thrice[:SUB] + thrice[SUB : 2 * SUB] + thrice[2 * SUB :]
        real = iota((SUB, 128), 1) < ATOMS
        shifted = chosen - jnp.max(jnp.where(real, chosen, -jnp.inf), axis=1, keepdims=True)
        exps = jnp.where(real, jnp.exp(shifted), 0.0)
        sums = jnp.sum(exps, axis=1, keepdims=True)
        probs_all[step] = exps / sums
        logp[...] = jnp.where(real, shifted - jnp.log(sums), 0.0)
        return slope

    def probs_copy(step):
        return remote(probs_all.at[step], nexts.at[step], probs_send.at[step], probs_recv.at[step], other_role)

    def grad_copy(step, half):
        spot = g1.at[step, pl.ds(1 + 10 * half, 10)]
        return remote(spot, spot, g1_send.at[2 * step + half], g1_recv.at[2 * step + half], other_role)

    def grad_start(step):
        for half in range(2):
            grad_copy(step, half).start()

    def backward(step):
        rows = pl.ds(pl.multiple_of(step * SUB, SUB), SUB)
        own = cols[rows, :]
        nodes = iota((SUB, 128), 1).astype(F32)
        reward, discount, importance = own[:, 0:1], own[:, 1:2], own[:, 2:3]
        support = -10.0 + 20.0 / (ATOMS - 1) * nodes
        spot = (jnp.clip(reward + discount * support, -10.0, 10.0) + 10.0) * ((ATOMS - 1) / 20.0)
        next_probs = nexts[step]
        projected = jnp.zeros((SUB, 128), F32)
        for j in range(ATOMS):
            projected += next_probs[:, j : j + 1] * jnp.maximum(0.0, 1.0 - jnp.abs(spot[:, j : j + 1] - nodes))
        projected = jnp.where(nodes < ATOMS, projected, 0.0)
        mass = jnp.sum(projected, axis=1, keepdims=True)
        row_loss = -jnp.sum(projected * logp[...], axis=1, keepdims=True)
        high = (row_loss * onehot(own[:, 5:6] == iota((SUB, plan.loss_rows), 1).astype(F32), F32)).astype(BF16)
        low = onehot(own[:, 6:7] == iota((SUB, 512), 1).astype(F32), BF16)
        loss_sums[...] += dot(high, low, TN)
        scaled = importance / totals[plan.bits, 0:1, 0:1]
        delta = (scaled * (probs_all[step] * mass - projected)).astype(BF16)
        spread = dot(delta, compact[...])
        delta_full = jnp.where(lane_action[...] == own[:, 4:5], spread, 0.0).astype(BF16)
        delta_all[rows, :] = delta_full
        grad4 = (dot(delta_full, w5[...]) * slope4[...]).astype(BF16)
        g4[rows, :] = grad4
        for y in range(7):
            pad3[y + 2, :, :448] = (dot(grad4, w4[448 * y : 448 * y + 448], NT) * s3[y]).astype(BF16)
        for pair in range(4):
            low = 128 * pair
            joined = jnp.concatenate([tall(pad3[2 - ky : 11 - ky, :, low : low + 128]) for ky in range(3)], axis=1)
            total = dot(joined, k3_wide[...], NT)
            if pair == 0:
                acc[: 9 * SUB, :256] = total
            else:
                acc[: 9 * SUB, low : low + 128] += total[:, :128]
                acc[: 9 * SUB, low + 128 : low + 256] = total[:, 128:]
        for y in range(9):
            pad2[y + 1] = (acc[y * SUB : (y + 1) * SUB, :576] * s2[y]).astype(BF16)
        for parity in range(2):
            for group in range(3):
                low = 192 * group
                part = tall(pad2[:, :, low : low + 192])
                total = dot(part[SUB:], k2[256 * parity : 256 * parity + 256], NT) + dot(
                    part[: 10 * SUB], k2[256 * parity + 512 : 256 * parity + 768], NT
                )
                if group == 0:
                    acc[: 10 * SUB, :256] = total
                else:
                    acc[: 10 * SUB, low : low + 64] += total[:, :64]
                    acc[: 10 * SUB, low + 64 : low + 256] = total[:, 64:]
            for m in range(10):
                g1[step, 2 * m + parity + 1] = (acc[m * SUB : (m + 1) * SUB, :640] * s1[parity, m]).astype(BF16)

    kept = ((x, x_kept), (a1, a1_kept), (a2, a2_kept), (pad2, pad2_kept), (pad3, pad3_kept))

    def keep_copies(step, low, high):
        return [pltpu.make_async_copy(kept[i][0], kept[i][1].at[step], keep_sem.at[i]) for i in range(low, high)]

    def back_copies(step, low, high):
        return [pltpu.make_async_copy(kept[i][1].at[step], kept[i][0], back_sem.at[i]) for i in range(low, high)]

    early = max(steps - 3, 0)

    def prefetch(step, slot):
        @pl.when(step < steps)
        def _():
            for c in raw_copies(step, slot):
                c.start()

    def raw_wait(step, slot):
        for c in raw_copies(step, slot):
            c.wait()

    def after_forward(step):
        @pl.when(role == 1)
        def _():
            probs_copy(step).start()

        @pl.when(online & (step + 1 < steps))
        def _():
            for c in keep_copies(step, 0, 3):
                c.start()

    total_step(1)
    raw_wait(0, 0)
    prefetch(1, 1)
    slope4[...] = forward(0, 0, [functools.partial(total_step, 2), lambda: None, functools.partial(total_step, 3)])
    for stage in range(4, plan.bits + 1):
        total_step(stage)
    after_forward(0)

    def one_step(step, _):
        @pl.when(online)
        def _():
            @pl.when(step > 0)
            def _():
                for c in keep_copies(step - 1, 3, 5):
                    c.wait()

            probs_copy(step).wait_recv()
            backward(step)

            @pl.when(step < early)
            def _():
                grad_start(step)

            @pl.when(step + 1 < steps)
            def _():
                for c in keep_copies(step, 3, 5):
                    c.start()

        @pl.when(step + 1 < steps)
        def _():
            following_step = step + 1
            slot = following_step % 2
            raw_wait(following_step, slot)
            prefetch(following_step + 1, 1 - slot)

            @pl.when(online)
            def _():
                for c in keep_copies(step, 0, 3):
                    c.wait()

            slope4[...] = forward(following_step, slot)
            after_forward(following_step)

        return 0

    lax.fori_loop(0, steps, one_step, 0)

    for stage in range(plan.bits):
        total_copy(stage).wait_send()

    def late_layers(step):
        total = None
        for group in range(3):
            low = 192 * group
            even, odd = (tall(a1[p, :, :, low : low + 256]) for p in range(2))
            joined = jnp.concatenate([even[: 9 * SUB], odd[: 9 * SUB], even[SUB:], odd[SUB:]], axis=1)
            term = dot(tall(pad2[1:10, :, low : low + 192]), joined, TN)
            total = term if total is None else total + term
        acc2[...] += total
        total = None
        for pair in range(4):
            low = 128 * pair
            joined = jnp.concatenate([tall(a2[ky : ky + 7, :, low : low + 256]) for ky in range(3)], axis=1)
            term = dot(tall(pad3[2:9, :, low : low + 128]), joined, TN)
            total = term if total is None else total + term
        acc3[...] += total
        for at, (count, lanes) in enumerate(((20, 640), (9, 576), (7, 448))):
            part = jnp.zeros((8, lanes), F32)
            for y in range(count):
                piece = (g1[step, y + 1] if at == 0 else pad2[y + 1] if at == 1 else pad3[y + 2, :, :448]).astype(F32)
                for q in range(SUB // 8):
                    part += piece[8 * q : 8 * q + 8]
            bias_sums[at, :, :lanes] += part

    def first_layer(step):
        for group in range(3):
            lanes = 192 if group == 2 else 224
            part = tall(g1[step, 1:21, :, 224 * group : 224 * group + lanes])
            pixels = tall(x[:, :, 512 * group : 512 * group + 512])
            joined = jnp.concatenate([pixels[: 20 * SUB], pixels[SUB:]], axis=1)
            acc1[:lanes] += dot(part, joined, TN)

    def weight_step(turn, step):
        @pl.when(turn > 0)
        def _():
            for c in back_copies(step, 1, 5):
                c.wait()

        late_layers(step)

        @pl.when(turn + 1 < steps)
        def _():
            for c in back_copies(turn, 1, 5):
                c.start()

        @pl.when(turn > 0)
        def _():
            for c in back_copies(step, 0, 1):
                c.wait()

        first_layer(step)

        @pl.when(turn + 1 < steps)
        def _():
            for c in back_copies(turn, 0, 1):
                c.start()

    def dense_sums():
        flat = raw.reshape(2 * (TILES - 1) * SUB * STACK, 128)
        for y in range(7):
            block = dot(a3[y], g4[...], TN)
            for px in range(7):
                for q in range(4):
                    flat[pl.ds(3136 * q + 7 * y + px, 64, stride=49), :] = block[
                        64 * px : 64 * px + 64, 128 * q : 128 * q + 128
                    ]
        for q in range(4):
            send[:3136, 128 * q : 128 * q + 128] = flat[3136 * q : 3136 * q + 3136].astype(BF16)
        head = dot(delta_all[...], a4[...], TN)
        send[ROW_HEAD : ROW_HEAD + 912] = head[:912].astype(BF16)
        send[ROW_HEAD + 912 : ROW_HEAD + 928] = jnp.concatenate(
            [head[912:LOGITS], jnp.zeros((928 - LOGITS, 512), F32)], axis=0
        ).astype(BF16)
        send[ROW_HEAD + 928 : plan.rest] = jnp.zeros((plan.rest - ROW_HEAD - 928, 512), BF16)

    def other_sums():
        def put(low, value):
            send[plan.rest + low : plan.rest + low + value.shape[0]] = value.astype(BF16)

        folded = acc1[0:32]
        for px in range(1, 7):
            folded += pltpu.roll(acc1[32 * px : 32 * px + 32], 1024 - 4 * px, 1)
        column = iota((1024, 256), 1)
        goal = ((column >> 5) & 1) * 512 + (column >> 6) * 128 + ((column >> 3) & 3) * 32 + (column & 7)
        pick = onehot(iota((1024, 256), 0) == goal, F32)
        put(ROW_ONE, jnp.concatenate([dot(folded, pick, precision=HIGHEST), jnp.zeros((32, 256), F32)], axis=1))
        folded = acc2[0:64]
        for px in range(1, 3):
            folded += pltpu.roll(acc2[64 * px : 64 * px + 64], 1024 - 64 * px, 1)
        column = iota((1024, 512), 1)
        goal = ((column >> 2) & 3) * 256 + (column & 3) * 32 + (column >> 4)
        pick = onehot(iota((1024, 512), 0) == goal, F32)
        put(ROW_TWO, dot(folded, pick, precision=HIGHEST))
        folded = acc3[0:64] + pltpu.roll(acc3[64:128], 768 - 64, 1)
        row = iota((768, 576), 0)
        goal = (row & 63) * 9 + (row >> 8) * 3 + ((row >> 6) & 3)
        pick = onehot((iota((768, 576), 1) == goal) & (((row >> 6) & 3) < 3), F32)
        third = dot(folded, pick, precision=HIGHEST)
        put(ROW_THREE, third[:, :512])
        put(ROW_THREE_REST, jnp.concatenate([third[:, 512:], jnp.zeros((64, 448), F32)], axis=1))
        bias_rows = []
        for at, (size, copies) in enumerate(((32, 20), (64, 9), (64, 7))):
            fold = onehot((iota((size * copies, 512), 0) & (size - 1)) == iota((size * copies, 512), 1), F32)
            line = jnp.sum(bias_sums[at, :, : size * copies], axis=0, keepdims=True)
            bias_rows.append(dot(line, fold, precision=HIGHEST))
        bias_rows.append(jnp.sum(g4[...].astype(F32), axis=0, keepdims=True))
        head_bias = jnp.sum(delta_all[...].astype(F32), axis=0, keepdims=True)
        bias_rows.append(head_bias[:, :512])
        bias_rows.append(jnp.concatenate([head_bias[:, 512:], jnp.zeros((1, 1024 - LOGITS), F32)], axis=1))
        bias_rows.append(jnp.zeros((10, 512), F32))
        put(ROW_BIAS, jnp.concatenate(bias_rows, axis=0))
        put(ROW_LOSS, loss_sums[...])
        left = plan.rows - plan.rest - ROW_LOSS - plan.loss_rows
        if left:
            put(ROW_LOSS + plan.loss_rows, jnp.zeros((left, 512), F32))

    def stage_rows(stream, stage):
        base, size, order = plan.streams[stream]
        low = base
        for bit in order[:stage]:
            size //= 2
            low = low + bit_of(bit) * size
        return low, size

    def aligned(at):
        return pl.multiple_of(at, 16)

    def scatter_copy(stream, stage):
        base, size, order = plan.streams[stream]
        low, count = stage_rows(stream, stage)
        half = count // 2
        away = aligned(low + (1 - bit_of(order[stage])) * half)
        into = base + size - count
        index = stream * plan.bits + stage
        return remote(
            send.at[pl.ds(away, half)], landed.at[pl.ds(into, half)], rs_send.at[index], rs_recv.at[index],
            across(order[stage]),
        )

    def scatter_start(streams):
        for stream in streams:
            scatter_copy(stream, 0).start()

    def scatter_finish(stage, streams):
        for stream in streams:
            base, size, order = plan.streams[stream]
            scatter_copy(stream, stage).wait_recv()
            low, count = stage_rows(stream, stage)
            half = count // 2
            keep = aligned(low + bit_of(order[stage]) * half)
            into = base + size - count
            target = final if stage == plan.bits - 1 else send
            block = next(b for b in (128, 64, 32, 16) if half % b == 0)

            def add(i, _, keep=keep, into=into, target=target, block=block):
                at = aligned(keep + i * block)
                target[pl.ds(at, block)] = send[pl.ds(at, block)] + landed[pl.ds(aligned(into + i * block), block)]
                return 0

            lax.fori_loop(0, half // block, add, 0)
            if stage + 1 < plan.bits:
                scatter_copy(stream, stage + 1).start()
            else:
                over_copy(stream).start()
                gather_copy(stream, 0).start()

    def over_copy(stream):
        low, count = stage_rows(stream, plan.bits)
        spot = pl.ds(aligned(low), count)
        return remote(final.at[spot], final.at[spot], x_send.at[stream], x_recv.at[stream], other_role)

    def gather_copy(stream, stage):
        order = plan.streams[stream][2]
        low, count = stage_rows(stream, plan.bits - stage)
        spot = pl.ds(aligned(low), count)
        index = stream * plan.bits + stage
        return remote(
            final.at[spot], final.at[spot], ag_send.at[index], ag_recv.at[index], across(order[plan.bits - 1 - stage])
        )

    def over_finish(streams):
        for stream in streams:
            over_copy(stream).wait_recv()
            gather_copy(stream, 0).start()

    def gather_finish(stage, streams):
        for stream in streams:
            gather_copy(stream, stage).wait_recv()
            if stage + 1 < plan.bits:
                gather_copy(stream, stage + 1).start()

    tile_rows = raw.reshape(2 * (TILES - 1) * SUB * STACK, 128)

    tile_pairs = raw.reshape((TILES - 1) * SUB * STACK, 2, 128)

    def tile_copies(step):
        return [
            pltpu.make_async_copy(
                tile_pairs.at[pl.ds(t * SUB, SUB)],
                frame_out.at[pl.ds(step * SUB, SUB), :, pl.ds(128 * t, 128)],
                tile_sem,
            )
            for t in range(TILES)
        ]

    def frame_step(step):
        frame_products(g1.at[step], band_k, acc)

        @pl.when(step > 0)
        def _():
            for c in tile_copies(step - 1):
                c.wait()

        for c in range(2):
            for t in range(TILES):
                tile_rows[pl.ds(t * SUB * 2 + c, SUB, stride=2), :] = frame_tile(acc, c, t)
        for c in tile_copies(step):
            c.start()

    bits, first, second = plan.bits, plan.first, plan.second

    late_grads = [(step, half) for step in range(early, steps) for half in range(2)]
    issue = {"soon": late_grads[:-4], "mid": late_grads[-4:-3], "over": late_grads[-3:-2], "last": late_grads[-2:]}

    def grads_at(moment):
        for step, half in issue[moment]:
            grad_copy(step, half).start()

    def turn_at(number):
        return min(number, steps - 1)

    @pl.when(online)
    def _():
        dense_sums()
        scatter_start(first)

        def turns(turn, _):
            weight_step(turn, jnp.where(turn == 0, steps - 1, turn - 1))

            @pl.when(turn == 0)
            def _():
                scatter_finish(0, first)
                grads_at("soon")

            return 0

        lax.fori_loop(0, steps, turns, 0)
        scatter_finish(1, first)
        grads_at("mid")
        other_sums()
        scatter_start(second)
        build_frame(k1_ref[:, 0:128], band_k)

    @pl.when(role == 1)
    def _():
        kernel_copy.wait_recv()
        build_frame(k1_online[:, 128:256], band_k)

    def frame_and_more(step, _):
        @pl.when(role == 1)
        def _():
            for half in range(2):
                grad_copy(step, half).wait_recv()

        frame_step(step)

        @pl.when(online & (step == 0))
        def _():
            scatter_finish(0, second)
            scatter_finish(2, first)

        @pl.when(online & (step == turn_at(1)))
        def _():
            scatter_finish(1, second)

        @pl.when(online & (step == turn_at(2)))
        def _():
            for stage in range(3, bits):
                scatter_finish(stage, first)
            grads_at("over")
            scatter_finish(2, second)

        @pl.when(online & (step == turn_at(3)))
        def _():
            for stage in range(3, bits):
                scatter_finish(stage, second)
            grads_at("last")
            gather_finish(0, first)

        @pl.when(online & (step == turn_at(5)))
        def _():
            gather_finish(0, second)

        @pl.when((role == 1) & (step == max(steps - 3, 0)))
        def _():
            over_finish(first)
            gather_finish(0, first)
            over_finish(second)
            for stage in range(1, bits - 2):
                gather_finish(stage, first)
                gather_finish(stage - 1, second)

        @pl.when((role == 1) & (step == max(steps - 2, 0)))
        def _():
            gather_finish(bits - 2, first)
            gather_finish(bits - 3, second)
            gather_finish(bits - 2, second)

        @pl.when((role == 1) & (step == steps - 1))
        def _():
            gather_finish(bits - 1, first)
            gather_finish(bits - 1, second)

        return 0

    lax.fori_loop(0, steps, frame_and_more, 0)

    @pl.when(online)
    def _():
        for stage in range(1, bits):
            gather_finish(stage, first)
            gather_finish(stage, second)

    out_copies = [
        pltpu.make_async_copy(final.at[pl.ds(0, ROW_HEAD)], dense_out, out_sem.at[0]),
        pltpu.make_async_copy(final.at[pl.ds(ROW_HEAD, plan.rows - ROW_HEAD)], sums_out, out_sem.at[1]),
    ]
    for c in out_copies:
        c.start()

    for c in tile_copies(steps - 1):
        c.wait()
    for stream in range(len(plan.streams)):
        for stage in range(plan.bits):
            gather_copy(stream, stage).wait_send()

    @pl.when(online)
    def _():
        kernel_copy.wait_send()
        for stream in range(len(plan.streams)):
            over_copy(stream).wait_send()
            for stage in range(plan.bits):
                scatter_copy(stream, stage).wait_send()

        def sent(step, _):
            for half in range(2):
                grad_copy(step, half).wait_send()
            return 0

        lax.fori_loop(0, steps, sent, 0)

    @pl.when(role == 1)
    def _():
        def sent(step, _):
            probs_copy(step).wait_send()
            return 0

        lax.fori_loop(0, steps, sent, 0)

    for c in out_copies:
        c.wait()


def core(plan, frames, edge, weights, facts, tables):
    rows = frames.shape[1]
    steps = rows // SUB
    k1, k2, k3, w4, b1, b2, b3, b4, w5, b5 = weights
    vmem, hbm = pl.BlockSpec(memory_space=pltpu.VMEM), pl.BlockSpec(memory_space=pl.ANY)
    dma = pltpu.SemaphoreType.DMA
    streams = len(plan.streams)
    scratch = [
        pltpu.VMEM((2, TILES - 1, SUB, STACK, 128), F32),
        pltpu.VMEM((3 * STACK * SUB, 512), BF16),
        pltpu.VMEM((21, SUB, 1536), BF16),
        pltpu.VMEM((2, 10, SUB, 640), BF16),
        pltpu.VMEM((2, 10, SUB, 640), F32),
        pltpu.VMEM((9, SUB, 640), BF16),
        pltpu.VMEM((9, SUB, 576), F32),
        pltpu.VMEM((7, rows, 448), BF16),
        pltpu.VMEM((7, SUB, 448), F32),
        pltpu.VMEM((rows, 512), BF16),
        pltpu.VMEM((rows, 512), BF16),
        pltpu.VMEM((rows, LOGITS), BF16),
        pltpu.VMEM((steps, 22, SUB, 640), BF16),
        pltpu.VMEM((11, SUB, 576), BF16),
        pltpu.VMEM((11, SUB, 512), BF16),
        pltpu.VMEM((21 * SUB, 2 * WIDE), F32),
        pltpu.VMEM((2, 2 * WIDE, 640), BF16),
        pltpu.VMEM((1024, 224), BF16),
        pltpu.VMEM((1024, 192), BF16),
        pltpu.VMEM((768, 128), BF16),
        pltpu.VMEM((256, 384), BF16),
        pltpu.VMEM((3136, 512), BF16),
        pltpu.VMEM((8, 640), F32),
        pltpu.VMEM((224, 1024), F32),
        pltpu.VMEM((192, 1024), F32),
        pltpu.VMEM((128, 768), F32),
        pltpu.VMEM((3, 8, 640), F32),
        pltpu.VMEM((plan.loss_rows, 512), F32),
        pltpu.VMEM((plan.rows, 512), BF16),
        pltpu.VMEM((plan.rows, 512), BF16),
        pltpu.VMEM((plan.rows, 512), BF16),
        pltpu.VMEM((steps, SUB, 128), F32),
        pltpu.VMEM((SUB, 128), F32),
        pltpu.VMEM((steps, SUB, 128), F32),
        pltpu.VMEM((plan.bits + 1, 8, 128), F32),
        pltpu.VMEM((plan.bits, 8, 128), F32),
        pltpu.VMEM((32, 256), BF16),
        pltpu.VMEM((rows, 128), F32),
        pltpu.VMEM((SUB, 512), F32),
        dma((5,)), dma((5,)), dma((2,)), dma, dma, dma((steps,)), dma((steps,)), dma((2 * steps,)), dma((2 * steps,)),
        dma((plan.bits,)), dma((plan.bits,)), dma, dma,
        dma((streams * plan.bits,)), dma((streams * plan.bits,)), dma((streams * plan.bits,)), dma((streams * plan.bits,)),
        dma((streams,)), dma((streams,)), dma((2,)),
    ]
    return pl.pallas_call(
        functools.partial(core_kernel, plan, steps),
        in_specs=[hbm, vmem, vmem, vmem, vmem, hbm] + [vmem] * 14,
        out_specs=[hbm] * 8,
        out_shape=[
            jax.ShapeDtypeStruct((rows, 2, TILES * 128), F32),
            jax.ShapeDtypeStruct((ROW_HEAD, 512), BF16),
            jax.ShapeDtypeStruct((plan.rows - ROW_HEAD, 512), BF16),
            jax.ShapeDtypeStruct((steps - 1, 21, SUB, 1536), BF16),
            jax.ShapeDtypeStruct((steps - 1, 2, 10, SUB, 640), BF16),
            jax.ShapeDtypeStruct((steps - 1, 9, SUB, 640), BF16),
            jax.ShapeDtypeStruct((steps - 1, 11, SUB, 576), BF16),
            jax.ShapeDtypeStruct((steps - 1, 11, SUB, 512), BF16),
        ],
        scratch_shapes=scratch,
        compiler_params=pltpu.CompilerParams(vmem_limit_bytes=63 << 20, collective_id=0, has_side_effects=True),
        name="core",
    )(frames, edge, k1, k2, k3, w4, b1, b2, b3, b4, w5, b5, *facts, *tables)[:3]


def finish_kernel(plan, own, frames, dense, sums, frame_out, w4, k1, b1, k2, b2, k3, b3, b4, w5, b5, losses):
    frame_out[...] = frames[:, :, :PIX]
    w4[...] = dense[...].astype(F32)

    def part(low, high):
        return sums[plan.rest - ROW_HEAD + low : plan.rest - ROW_HEAD + high]

    @pl.when(pl.program_id(0) == 0)
    def _():
        w5[:912] = sums[:912].astype(F32)
        w5[912:] = sums[912:928].astype(F32)[: LOGITS - 912]
        k2[...] = part(ROW_TWO, ROW_THREE).astype(F32)
        k3[:, :512] = part(ROW_THREE, ROW_THREE_REST).astype(F32)
        k3[:, 512:] = part(ROW_THREE_REST, ROW_ONE)[:, :64].astype(F32)
        k1[...] = part(ROW_ONE, ROW_BIAS)[:, :256].astype(F32)
        rows = part(ROW_BIAS, ROW_LOSS).astype(F32)
        b1[...] = rows[0:1, :32]
        b2[...] = rows[1:2, :64]
        b3[...] = rows[2:3, :64]
        b4[...] = rows[3:4]
        b5[:, :512] = rows[4:5]
        b5[:, 512:] = rows[5:6, : LOGITS - 512]
        device = lax.axis_index("role") * plan.batch + lax.axis_index("batch")
        slot = device * own + iota((1, own), 1)
        chosen = dot(part(ROW_LOSS, ROW_LOSS + plan.loss_rows), onehot(iota((512, own), 0) == (slot & 511), BF16))
        mine = iota((plan.loss_rows, own), 0) == (slot >> 9)
        losses[...] = jnp.sum(jnp.where(mine, chosen, 0.0), axis=0, keepdims=True)


def finish(plan, own, frames, dense, sums):
    rows = frames.shape[0]
    small = ((32, 256), (1, 32), (64, 512), (1, 64), (64, 576), (1, 64), (1, 512), (LOGITS, 512), (1, LOGITS), (1, own))
    block, pieces = (56, 4) if rows % 56 == 0 else (16, 14)
    frame_at, dense_at = (lambda i: (i, 0, 0)), (lambda i: (jnp.minimum(i, pieces - 1), 0))
    return pl.pallas_call(
        functools.partial(finish_kernel, plan, own),
        grid=(rows // block,),
        in_specs=[
            pl.BlockSpec((block, 2, TILES * 128), frame_at),
            pl.BlockSpec((ROW_HEAD // pieces, 512), dense_at),
            pl.BlockSpec(sums.shape, lambda i: (0, 0)),
        ],
        out_specs=[
            pl.BlockSpec((block, 2, PIX), frame_at),
            pl.BlockSpec((ROW_HEAD // pieces, 512), dense_at),
            *[pl.BlockSpec(s, lambda i: (0, 0)) for s in small],
        ],
        out_shape=[jax.ShapeDtypeStruct(s, F32) for s in ((rows, 2, PIX), (ROW_HEAD, 512), *small)],
        compiler_params=pltpu.CompilerParams(vmem_limit_bytes=60 << 20),
        name="finish",
    )(frames, dense, sums)


def on_device(
    frames,
    conv1_weight,
    conv1_bias,
    conv2_weight,
    conv2_bias,
    conv3_weight,
    conv3_bias,
    dense_weight,
    dense_bias,
    head_weight,
    head_bias,
    taken_actions,
    next_actions,
    rewards,
    discounts,
    importance,
    buffer_slots,
):
    roles, batch = lax.axis_size("role"), lax.axis_size("batch")
    rows = frames.shape[1]
    slots = rows * batch
    plan = Plan(batch, slots)

    lane_action = jnp.asarray(np.arange(LOGITS)[None] // ATOMS, F32)
    compact = jnp.asarray(np.arange(128)[:, None] == np.arange(LOGITS)[None] % ATOMS, BF16)
    facts = [
        v.reshape(1, rows) for v in (taken_actions, next_actions, rewards, discounts, importance, buffer_slots)
    ]
    edge = frames[0, :, :, 128 * (TILES - 1) :]
    weights = (
        conv1_weight[0].T, conv2_weight[0].T, conv3_weight[0].T, dense_weight[0],
        conv1_bias, conv2_bias, conv3_bias, dense_bias, head_weight[0].T, head_bias,
    )
    partial = core(plan, frames, edge, weights, facts, (lane_action, compact))
    frame_part, w4, k1, b1, k2, b2, k3, b3, b4, w5, b5, priorities = finish(plan, slots // (roles * batch), *partial)
    return (frame_part, k1.T, b1[0], k2.T, b2[0], k3.T, b3[0], w4, b4[0], w5.T, b5[0], priorities[0])


def solution(mesh):
    in_specs = (
        P("role", "batch", None, None),
        P("role", None, None),
        P("role", None),
        P("role", None, None),
        P("role", None),
        P("role", None, None),
        P("role", None),
        P("role", None, None),
        P("role", None),
        P("role", None, None),
        P("role", None),
        P("batch"),
        P("batch"),
        P("batch"),
        P("batch"),
        P("batch"),
        P("batch"),
    )
    out_specs = (
        P("batch", "role", None),
        P(),
        P(),
        P(),
        P(),
        P(),
        P(),
        P(),
        P(),
        P(),
        P(),
        P(("role", "batch")),
    )
    return jax.shard_map(on_device, mesh=mesh, in_specs=in_specs, out_specs=out_specs, check_vma=False)
```
